32 devices in a mesh: dp: 4 (over y, x), seq: 8 (over z, core).
Axes of the slice: x: 2, y: 2, z: 4, core: 2. Of those that a mesh axis runs over, the one named last changes fastest.
Arguments:
- tokens: bfloat16 [64, 64, 1152], P(('dp', 'seq')), may hold values from -6 to 6
- spatial_qkv: bfloat16 [64, 64, 1728], P(('dp', 'seq')), may hold values from -6 to 6
- wo_spatial: bfloat16 [576, 1152], replicated, may hold values from -0.25 to 0.25
- w_temporal: bfloat16 [1152, 1728], P(None, 'dp'), may hold values from -0.1875 to 0.1875
- wo_temporal: bfloat16 [576, 1152], replicated, may hold values from -0.25 to 0.25
- cotangent: bfloat16 [64, 64, 1152], P(('dp', 'seq')), may hold values from -6 to 6
Outputs:
- block_out: bfloat16 [64, 64, 1152], P(('dp', 'seq'))
- tokens_grad: bfloat16 [64, 64, 1152], P(('dp', 'seq'))
- spatial_qkv_grad: bfloat16 [64, 64, 1728], P(('dp', 'seq'))
- wo_spatial_grad: float32 [576, 1152], P('seq', 'dp')
- wo_temporal_grad: float32 [576, 1152], P('seq', 'dp')
The draws below stay inside these ranges and needn't reach their ends.
All inputs are finite; a program needn't handle non-finite values.
Results may differ from the reference program's by a relative error of at most 0.038.
Values may be sent and summed in bfloat16 or wider, within the bound.
No kernel may reach another device: no remote copies, remote signals or barrier semaphores. Data moves between devices by JAX's collectives and lax.ppermute only.
A program may use at most 64 MiB of HBM per device.

```python
import math
import jax
import jax.numpy as jnp
from jax import lax

D = 1152
HEADS = 8
DH = 72
FRAMES = 16
FR_DEV = 2
PATCH = 64
HD = 576
NFR = 64


def draw_spatial_qkv(key, part):
    keys = jax.random.split(jax.random.fold_in(key, 17), 7)
    base_shape = (NFR, PATCH, 3, HEADS, DH)
    base = jnp.clip(jax.random.normal(keys[0], base_shape, jnp.float32), -6.0, 6.0)
    signs = jnp.where(jax.random.bernoulli(keys[1], 0.5, (NFR, HEADS, DH)), 1.0, -1.0).astype(jnp.float32)
    strength = jax.random.uniform(keys[2], (NFR, HEADS), jnp.float32, 2.5, 6.0)
    margin = jax.random.uniform(keys[3], (NFR, HEADS), jnp.float32, 1.0, 3.0)
    query_pos = jax.random.randint(keys[4], (NFR, HEADS), 0, PATCH)
    first_pos = jax.random.randint(keys[5], (NFR, HEADS), 0, PATCH)
    second_pos = (first_pos + jax.random.randint(keys[6], (NFR, HEADS), 1, PATCH)) % PATCH
    patch_index = jnp.arange(PATCH).reshape(1, PATCH, 1)
    query_sel = (patch_index == query_pos[:, None, :])[..., None]
    first_sel = (patch_index == first_pos[:, None, :])[..., None]
    second_sel = (patch_index == second_pos[:, None, :])[..., None]
    column = jnp.arange(DH).reshape(1, 1, DH)
    reduction = margin * DH ** 0.5 / (4.0 * strength)
    lowered = jnp.where(column < 4, reduction[..., None], 0.0)
    query_plant = (strength[..., None] * signs)[:, None]
    first_plant = (6.0 * signs)[:, None]
    second_plant = ((6.0 - lowered) * signs)[:, None]
    query_part = jnp.where(query_sel, query_plant, base[:, :, 0])
    key_part = jnp.where(first_sel, first_plant, jnp.where(second_sel, second_plant, base[:, :, 1]))
    stacked = jnp.stack([query_part, key_part, base[:, :, 2]], axis=2)
    return stacked.reshape(NFR, PATCH, 3 * HEADS * DH).astype(jnp.bfloat16)


def strengthened(drawn, rng, source, target, shards_of, factor):
    def block_of(axis_at):
        return (jnp.arange(drawn.shape[axis_at]) // (drawn.shape[axis_at] // shards_of)).reshape((-1,) + (1,) * (drawn.ndim - 1 - axis_at))

    near = jax.random.permutation(rng, shards_of)[block_of(target)]
    far = (block_of(target) + shards_of // 2) % shards_of
    return jnp.where((block_of(source) == near) | (block_of(source) == far), factor * drawn, drawn)


def block_scale(own_key, dims, cuts, least, top_value):
    def one(dim, shards_of):
        steps = jax.random.uniform(jax.random.fold_in(jax.random.fold_in(own_key, 6), dim), (shards_of,), jnp.float32, least / len(cuts), top_value / len(cuts))
        return jnp.repeat(jnp.exp(steps), dims[dim] // shards_of).reshape((-1,) + (1,) * (len(dims) - dim - 1))

    factor_of = one(*cuts[0])
    for cut in cuts[1:]:
        factor_of = factor_of * one(*cut)
    return factor_of


def normal_values(key, extent, scale, reach, pieces=(), held_as=jnp.bfloat16):
    entries = jax.random.normal(key, extent, jnp.float32) * scale
    if len(pieces) > 0:
        entries = block_scale(key, extent, pieces, -0.22, 0.18) * entries
    return jnp.clip(entries, min=-reach, max=reach).astype(held_as)


def gaussian_with(stream_key, shape, scale, reach, cuts, heavy, kind=jnp.bfloat16):
    entries = scale * jax.random.normal(stream_key, shape, jnp.float32)
    if cuts:
        entries = entries * block_scale(stream_key, shape, cuts, -0.22, 0.18)
    return jnp.clip(strengthened(entries, jax.random.fold_in(stream_key, 3), *heavy), -reach, reach).astype(kind)


def setup_inputs(seed: int = 0) -> dict:
    seeds = jax.random.split(jax.random.key(seed), 7)
    tokens = normal_values(seeds[0], (NFR, PATCH, D), 1.0, 6.0, ((0, 32),))
    spatial_qkv = draw_spatial_qkv(jax.random.fold_in(seeds[6], 71), 0)
    wo_spatial = normal_values(seeds[2], (HD, D), HD ** -0.5, 0.25)
    w_temporal = normal_values(seeds[3], (D, 3 * HD), D ** -0.5, 0.1875, ((1, 4),))
    wo_temporal = normal_values(seeds[4], (HD, D), HD ** -0.5, 0.25)
    cotangent = gaussian_with(seeds[5], (NFR, PATCH, D), 1.0, 6.0, ((0, 32),), (0, 2, 32, 2.75))
    return dict(tokens=tokens, spatial_qkv=spatial_qkv, wo_spatial=wo_spatial, w_temporal=w_temporal, wo_temporal=wo_temporal, cotangent=cotangent)


def split_three(packed):
    inner_width = packed.shape[-1] // 3
    return (packed[..., :inner_width], packed[..., inner_width:2 * inner_width], packed[..., 2 * inner_width:])

def head_view(matrix):
    batch_size, length, inner_width = matrix.shape
    return matrix.astype(jnp.float32).reshape(batch_size, length, inner_width // DH, DH)

def attention_weights_of(query_heads, key_heads):
    scores = jnp.einsum('blhd,bmhd->bhlm', query_heads, key_heads) * (1.0 / math.sqrt(DH))
    return jax.nn.softmax(scores, axis=-1)

def attention(queries, key_rows, values):
    batch_size, length, inner_width = queries.shape
    weights_full = attention_weights_of(head_view(queries), head_view(key_rows))
    rounded = lax.optimization_barrier(weights_full.astype(jnp.bfloat16)).astype(jnp.float32)
    output = jnp.einsum('bhlm,bmhd->blhd', rounded, head_view(values))
    return output.reshape(batch_size, length, inner_width).astype(jnp.bfloat16)

def attention_grad(queries, key_rows, values, output_grad):
    batch_size, length, inner_width = queries.shape
    query_heads = head_view(queries)
    key_heads = head_view(key_rows)
    value_heads = head_view(values)
    grad_heads = head_view(output_grad)
    weights_full = attention_weights_of(query_heads, key_heads)
    rounded = lax.optimization_barrier(weights_full.astype(jnp.bfloat16)).astype(jnp.float32)
    value_grad = jnp.einsum('bhlm,blhd->bmhd', rounded, grad_heads)
    weight_grad = jnp.einsum('blhd,bmhd->bhlm', grad_heads, value_heads)
    centered = weight_grad - lax.optimization_barrier(jnp.sum(weights_full * weight_grad, axis=-1, keepdims=True))
    score_grad = (weights_full * centered * (1.0 / math.sqrt(DH))).astype(jnp.bfloat16)
    score_grad = lax.optimization_barrier(score_grad).astype(jnp.float32)
    query_grad = jnp.einsum('bhlm,bmhd->blhd', score_grad, key_heads)
    key_grad = jnp.einsum('bhlm,blhd->bmhd', score_grad, query_heads)
    joined = [part_grad.reshape(batch_size, length, inner_width) for part_grad in (query_grad, key_grad, value_grad)]
    return jnp.concatenate(joined, axis=-1).astype(jnp.bfloat16)

def to_clips(matrix, clip_count):
    frame_total, patch_share, channels = matrix.shape
    grouped = matrix.reshape(clip_count, FRAMES, patch_share, channels).transpose(0, 2, 1, 3)
    return grouped.reshape(clip_count * patch_share, FRAMES, channels)

def from_clips(matrix, clip_count):
    batch_rows, frame_count, channels = matrix.shape
    patch_share = batch_rows // clip_count
    grouped = matrix.reshape(clip_count, patch_share, frame_count, channels).transpose(0, 2, 1, 3)
    return grouped.reshape(clip_count * frame_count, patch_share, channels)

def group_sum(left, right):
    group_count = NFR // FR_DEV
    left_groups = left.reshape(group_count, FR_DEV * PATCH, left.shape[-1])
    right_groups = right.reshape(group_count, FR_DEV * PATCH, right.shape[-1])

    def add_group(running, pair):
        left_part, right_part = pair
        partial_value = jnp.dot(left_part.T, right_part, preferred_element_type=jnp.float32).astype(jnp.bfloat16)
        return (running + lax.optimization_barrier(partial_value).astype(jnp.float32), None)
    initial = jnp.zeros((left.shape[-1], right.shape[-1]), jnp.float32)
    total_sum, unused = lax.scan(add_group, initial, (left_groups, right_groups))
    return total_sum

def reference(tokens, spatial_qkv, wo_spatial, w_temporal, wo_temporal, cotangent):
    row_total = NFR * PATCH
    clip_count = NFR // FRAMES
    spatial_query, spatial_keys, spatial_values = split_three(spatial_qkv)
    spatial_out = attention(spatial_query, spatial_keys, spatial_values)
    spatial_rows = spatial_out.reshape(row_total, -1)
    hidden_rows = (tokens.reshape(row_total, D).astype(jnp.float32) + jnp.dot(spatial_rows, wo_spatial, preferred_element_type=jnp.float32)).astype(jnp.bfloat16)
    temporal_qkv = jnp.dot(hidden_rows, w_temporal, preferred_element_type=jnp.float32).astype(jnp.bfloat16)
    clip_qkv = to_clips(temporal_qkv.reshape(NFR, PATCH, -1), clip_count)
    temporal_query, temporal_keys, temporal_values = split_three(clip_qkv)
    temporal_out = from_clips(attention(temporal_query, temporal_keys, temporal_values), clip_count)
    temporal_rows = temporal_out.reshape(row_total, -1)
    block_out = (hidden_rows.astype(jnp.float32) + jnp.dot(temporal_rows, wo_temporal, preferred_element_type=jnp.float32)).astype(jnp.bfloat16)
    grad_rows = cotangent.reshape(row_total, D)
    out_grad = jnp.dot(grad_rows, wo_temporal.T, preferred_element_type=jnp.float32).astype(jnp.bfloat16)
    clip_grad = to_clips(out_grad.reshape(NFR, PATCH, -1), clip_count)
    temporal_qkv_grad = from_clips(attention_grad(temporal_query, temporal_keys, temporal_values, clip_grad), clip_count)
    projection_grad = jnp.dot(temporal_qkv_grad.reshape(row_total, -1), w_temporal.T, preferred_element_type=jnp.float32).astype(jnp.bfloat16)
    projection_grad = lax.optimization_barrier(projection_grad)
    tokens_grad = (grad_rows.astype(jnp.float32) + projection_grad.astype(jnp.float32)).astype(jnp.bfloat16)
    spatial_out_grad = jnp.dot(tokens_grad, wo_spatial.T, preferred_element_type=jnp.float32).astype(jnp.bfloat16)
    spatial_qkv_grad = attention_grad(spatial_query, spatial_keys, spatial_values, spatial_out_grad.reshape(NFR, PATCH, -1))
    wo_spatial_grad = group_sum(spatial_rows, tokens_grad)
    wo_temporal_grad = group_sum(temporal_rows, grad_rows)
    return (block_out.reshape(NFR, PATCH, D), tokens_grad.reshape(NFR, PATCH, D), spatial_qkv_grad, wo_spatial_grad, wo_temporal_grad)
```

```python
import functools
import math

import jax
import jax.numpy as jnp
from jax import lax
from jax.experimental import pallas as pl
from jax.experimental.pallas import tpu as pltpu
from jax.sharding import PartitionSpec as P

DH = 72
FRAMES = 16
LANES = 128
BF16 = jnp.bfloat16
F32 = jnp.float32
VMEM = pl.BlockSpec(memory_space=pltpu.VMEM)
SMEM = pl.BlockSpec(memory_space=pltpu.SMEM)
LIMIT = 40 * 1024 * 1024


def dot(left, right):
    return jnp.dot(left, right, preferred_element_type=F32)


def dot_bt(left, right):
    return lax.dot_general(left, right, (((1,), (1,)), ((), ())), preferred_element_type=F32)


def dot_at(left, right):
    return lax.dot_general(left, right, (((0,), (0,)), ((), ())), preferred_element_type=F32)


def call(body, outs, args, scratch=(), flops=0):
    moved = sum(math.prod(a.shape) * a.dtype.itemsize for a in (*args, *outs))
    return pl.pallas_call(
        body,
        out_shape=outs,
        in_specs=[SMEM if a.dtype == jnp.int32 else VMEM for a in args],
        out_specs=[VMEM] * len(outs),
        scratch_shapes=list(scratch),
        compiler_params=pltpu.CompilerParams(vmem_limit_bytes=LIMIT),
        cost_estimate=pl.CostEstimate(flops=flops, bytes_accessed=moved, transcendentals=0),
    )(*args)


def shape(dims, dtype=BF16):
    return jax.ShapeDtypeStruct(dims, dtype)


def window(head):
    low = head * DH // LANES * LANES
    high = -(-(head + 1) * DH // LANES) * LANES
    return low, high


def head_only(block, head):
    low, high = window(head)
    lane = lax.broadcasted_iota(jnp.int32, (1, high - low), 1) + low
    keep = (lane >= head * DH) & (lane < (head + 1) * DH)
    return jnp.where(keep, block, jnp.zeros_like(block))


def add_tiles(tiles, head, value):
    low, high = window(head)
    for at in range(low // LANES, high // LANES):
        part = value[:, at * LANES - low : (at + 1) * LANES - low]
        tiles[at] = part if tiles[at] is None else tiles[at] + part


def joined(tiles):
    return jnp.concatenate([tile.astype(BF16) for tile in tiles], axis=1)


def same_group(rows, kind):
    row = lax.broadcasted_iota(jnp.int32, (rows, rows), 0)
    col = lax.broadcasted_iota(jnp.int32, (rows, rows), 1)
    how, size = kind
    return row // size == col // size if how == "block" else row % size == col % size


def softmax_forward(q_ref, k_ref, v_ref, p_ref, heads, kind):
    rows = q_ref.shape[0]
    mask = same_group(rows, kind)
    tiles = [None] * (q_ref.shape[1] // LANES)
    for head in range(heads):
        low, high = window(head)
        s = dot_bt(q_ref[:, low:high], head_only(k_ref[:, low:high], head)) * (1.0 / math.sqrt(DH))
        s = jnp.where(mask, s, -jnp.inf)
        e = jnp.exp(s - jnp.max(s, axis=1, keepdims=True))
        p = e / jnp.sum(e, axis=1, keepdims=True)
        p_ref[head] = p
        add_tiles(tiles, head, dot(p.astype(BF16), head_only(v_ref[:, low:high], head)))
    return joined(tiles)


def softmax_backward(q_ref, k_ref, v_ref, g_ref, p_ref, heads):
    count = q_ref.shape[1] // LANES
    dq, dk, dv = [None] * count, [None] * count, [None] * count
    for head in range(heads):
        low, high = window(head)
        p = p_ref[head]
        g = head_only(g_ref[:, low:high], head)
        add_tiles(dv, head, dot_at(p.astype(BF16), g))
        dp = dot_bt(g, v_ref[:, low:high])
        ds = p * (dp - jnp.sum(p * dp, axis=1, keepdims=True)) * (1.0 / math.sqrt(DH))
        ds = ds.astype(BF16)
        add_tiles(dq, head, dot(ds, head_only(k_ref[:, low:high], head)))
        add_tiles(dk, head, dot_at(ds, head_only(q_ref[:, low:high], head)))
    return joined(dq), joined(dk), joined(dv)


def put(ref, value):
    width = value.shape[1]
    ref[:, width // LANES * LANES :] = jnp.zeros(
        (ref.shape[0], ref.shape[1] - width // LANES * LANES), ref.dtype
    )
    ref[:, :width] = value


def two_frames(ref, at, frames):
    return jnp.concatenate([ref[f, at].astype(F32) for f in range(frames)], axis=0).astype(BF16)


def pack_kernel(peers, idx, tok, cot, *outs):
    frames, width = tok.shape[0], tok.shape[3]
    for r in range(peers):
        at = idx[0] ^ r
        outs[r][:, :width] = two_frames(tok, at, frames)
        outs[r][:, width:] = two_frames(cot, at, frames)


def spatial_kernel(peers, patches, qkv, out, by_peer, p_ref, qs, ks, vs):
    inner = out.shape[1]
    rows = out.shape[0]
    x = qkv[...]
    put(qs, x[:, :inner])
    put(ks, x[:, inner : 2 * inner])
    put(vs, x[:, 2 * inner :])
    o = softmax_forward(qs, ks, vs, p_ref, inner // DH, ("block", patches))[:, :inner]
    out[...] = o
    each = patches // peers
    o = o.astype(F32)
    for at in range(peers):
        by_peer[at] = jnp.concatenate(
            [o[f * patches + at * each : f * patches + (at + 1) * each] for f in range(rows // patches)],
            axis=0,
        ).astype(BF16)


def temporal_forward_kernel(peers, shards, group, idx, so, wos, wot, *refs):
    packed, refs = refs[:peers], refs[peers:]
    weights, refs = refs[: len(shards)], refs[len(shards) :]
    q, k, v, g, p_ref, spat, cot, part = refs[:8]
    outs = refs[8 : 8 + peers]
    blocks, tok = refs[8 + peers :]
    width = wos.shape[1]
    inner = wos.shape[0]
    chunk = so.shape[1]
    for r in range(peers):
        rows = slice(r * chunk, (r + 1) * chunk)
        spat[rows] = so[idx[0] ^ r]
        tok[rows] = packed[r][:, :width]
        cot[rows] = packed[r][:, width:]
    hidden = (tok[...].astype(F32) + dot(spat[...], wos[...])).astype(BF16)
    for (place, count), w in zip(shards, weights):
        block = dot_bt(hidden, w[...]).astype(BF16)
        size = block.shape[1] // count
        for i in range(count):
            blocks[place(idx) + i] = block[:, i * size : (i + 1) * size]
    whole = jnp.concatenate([blocks[i] for i in range(blocks.shape[0])], axis=1)
    put(q, whole[:, :inner])
    put(k, whole[:, inner : 2 * inner])
    put(v, whole[:, 2 * inner :])
    o = softmax_forward(q, k, v, p_ref, inner // DH, ("cycle", group))[:, :inner]
    for r in range(peers):
        outs[r][...] = o[r * chunk : (r + 1) * chunk]
    part[...] = dot_at(o, cot[...]).astype(BF16)
    put(g, dot_bt(cot[...], wot[...]).astype(BF16))


def temporal_backward_kernel(peers, shards, idx, q, k, v, g, p_ref, spat, cot, *refs):
    weights, refs = refs[: len(shards)], refs[len(shards) :]
    outs = refs[:peers]
    part, blocks = refs[peers:]
    inner = spat.shape[1]
    chunk = outs[0].shape[0]
    dq, dk, dv = softmax_backward(q, k, v, g, p_ref, inner // DH)
    whole = jnp.concatenate([dq[:, :inner], dk[:, :inner], dv[:, :inner]], axis=1)
    size = blocks.shape[2]
    for i in range(blocks.shape[0]):
        blocks[i] = whole[:, i * size : (i + 1) * size]
    total = jnp.zeros(cot.shape, F32)
    for (place, count), w in zip(shards, weights):
        lhs = jnp.concatenate([blocks[place(idx) + i] for i in range(count)], axis=1)
        total += dot(lhs, w[...])
    grad = (cot[...].astype(F32) + total.astype(BF16).astype(F32)).astype(BF16)
    for r in range(peers):
        outs[r][...] = grad[r * chunk : (r + 1) * chunk]
    part[...] = dot_at(spat[...], grad).astype(BF16)


def block_out_kernel(peers, patches, idx, tok, spat, wos, wot, *refs):
    chunks, (out, rows) = refs[:peers], refs[peers:]
    each = patches // peers
    for r in range(peers):
        for f in range(chunks[r].shape[0] // each):
            low = pl.multiple_of(f * patches + (idx[0] ^ r) * each, each)
            rows[pl.ds(low, each)] = chunks[r][f * each : (f + 1) * each].astype(F32)
    hidden = (tok[...].astype(F32) + dot(spat[...], wos[...])).astype(BF16)
    out[...] = (hidden.astype(F32) + dot(rows[...].astype(BF16), wot[...])).astype(BF16)


def spatial_backward_kernel(peers, patches, idx, qkv, p_ref, wos, *refs):
    chunks, (out, grads, rows, qs, ks, vs, gs) = refs[:peers], refs[peers:]
    inner = wos.shape[0]
    each = patches // peers
    for r in range(peers):
        for f in range(chunks[r].shape[0] // each):
            low = pl.multiple_of(f * patches + (idx[0] ^ r) * each, each)
            rows[pl.ds(low, each)] = chunks[r][f * each : (f + 1) * each].astype(F32)
    grad = rows[...].astype(BF16)
    out[...] = grad
    put(gs, dot_bt(grad, wos[...]).astype(BF16))
    x = qkv[...]
    put(qs, x[:, :inner])
    put(ks, x[:, inner : 2 * inner])
    put(vs, x[:, 2 * inner :])
    dq, dk, dv = softmax_backward(qs, ks, vs, gs, p_ref, inner // DH)
    grads[...] = jnp.concatenate([dq[:, :inner], dk[:, :inner], dv[:, :inner]], axis=1)


def flip(value, axis, bit):
    return lax.ppermute(value, axis, [(i, i ^ bit) for i in range(lax.axis_size(axis))])


def gather_weight(weight, core):
    n = lax.axis_size("dp")
    if n != 4:
        return [lax.all_gather(weight, "dp", axis=0, tiled=True)], [(lambda idx: 0, 1)], 1
    half = weight.shape[0] // 2
    mine = lax.dynamic_slice_in_dim(weight, core * half, half, 0)
    near = [flip(mine, "dp", j) for j in range(1, n)]
    far = [flip(w, "seq", 1) for w in near]
    shards = [(lambda idx: 2 * idx[1], 2)]
    shards += [(lambda idx, j=j: 2 * (idx[1] ^ j) + idx[2], 1) for j in range(1, n)]
    shards += [(lambda idx, j=j: 2 * (idx[1] ^ j) + 1 - idx[2], 1) for j in range(1, n)]
    return [weight, *near, *far], shards, 2 * n


def reduced(part):
    over_seq = lax.psum_scatter(part, "seq", scatter_dimension=0, tiled=True)
    return lax.psum_scatter(over_seq, "dp", scatter_dimension=1, tiled=True).astype(F32)


def shards(tokens, spatial_qkv, wo_spatial, w_temporal, wo_temporal, cotangent):
    frames, patches, width = tokens.shape
    inner = wo_spatial.shape[0]
    heads = inner // DH
    padded = -(-inner // LANES) * LANES
    rows = frames * patches
    peers = FRAMES // frames
    each = patches // peers
    chunk = rows // peers
    n_seq = lax.axis_size("seq")
    seq = lax.axis_index("seq")
    idx = jnp.stack([seq % peers, lax.axis_index("dp"), seq % 2]).astype(jnp.int32)
    wide = pltpu.VMEM((rows, padded), BF16)

    weights, places, count = gather_weight(w_temporal.T, seq % 2)

    packed = call(
        functools.partial(pack_kernel, peers),
        [shape((chunk, 2 * width))] * peers,
        [
            idx,
            tokens.reshape(frames, peers, each, width),
            cotangent.reshape(frames, peers, each, width),
        ],
    )
    packed = [packed[0]] + [flip(packed[r], "seq", r) for r in range(1, peers)]

    qkv_rows = spatial_qkv.reshape(rows, 3 * inner)
    spatial_rows, by_peer, spatial_p = call(
        functools.partial(spatial_kernel, peers, patches),
        [shape((rows, inner)), shape((peers, chunk, inner)), shape((heads, rows, rows), F32)],
        [qkv_rows],
        [wide] * 3,
    )
    groups = None
    if n_seq > peers:
        groups = [list(range(i, i + peers)) for i in range(0, n_seq, peers)]
    by_peer = lax.all_to_all(
        by_peer, "seq", split_axis=0, concat_axis=0, tiled=True, axis_index_groups=groups
    )

    q, k, v, g, temporal_p, spat, cot, temporal_part, *outs = call(
        functools.partial(temporal_forward_kernel, peers, places, each),
        [shape((rows, padded))] * 4
        + [shape((heads, rows, rows), F32), shape((rows, inner)), shape((rows, width))]
        + [shape((inner, width))]
        + [shape((chunk, inner))] * peers,
        [idx, by_peer, wo_spatial, wo_temporal, *packed, *weights],
        [
            pltpu.VMEM((count, rows, 3 * inner // count), BF16),
            pltpu.VMEM((rows, width), BF16),
        ],
    )
    outs = [outs[0]] + [flip(outs[r], "seq", r) for r in range(1, peers)]

    *grads, spatial_part = call(
        functools.partial(temporal_backward_kernel, peers, places),
        [shape((chunk, width))] * peers + [shape((inner, width))],
        [idx, q, k, v, g, temporal_p, spat, cot, *weights],
        [pltpu.VMEM((count, rows, 3 * inner // count), BF16)],
    )
    grads = [grads[0]] + [flip(grads[r], "seq", r) for r in range(1, peers)]

    (block_out,) = call(
        functools.partial(block_out_kernel, peers, patches),
        [shape((rows, width))],
        [idx, tokens.reshape(rows, width), spatial_rows, wo_spatial, wo_temporal, *outs],
        [pltpu.VMEM((rows, inner), F32)],
    )
    tokens_grad, qkv_grad = call(
        functools.partial(spatial_backward_kernel, peers, patches),
        [shape((rows, width)), shape((rows, 3 * inner))],
        [idx, qkv_rows, spatial_p, wo_spatial, *grads],
        [pltpu.VMEM((rows, width), F32)] + [wide] * 4,
    )
    return (
        block_out.reshape(frames, patches, width),
        tokens_grad.reshape(frames, patches, width),
        qkv_grad.reshape(frames, patches, 3 * inner),
        reduced(spatial_part),
        reduced(temporal_part),
    )


def solution(mesh):
    placed = (
        P(("dp", "seq"), None, None),
        P(("dp", "seq"), None, None),
        P(),
        P(None, "dp"),
        P(),
        P(("dp", "seq"), None, None),
    )
    return jax.shard_map(
        shards,
        mesh=mesh,
        in_specs=placed,
        out_specs=(
            P(("dp", "seq"), None, None),
            P(("dp", "seq"), None, None),
            P(("dp", "seq"), None, None),
            P("seq", "dp"),
            P("seq", "dp"),
        ),
        check_vma=False,
    )
```

```python
import functools
import math

import jax
import jax.numpy as jnp
from jax import lax
from jax.experimental import pallas as pl
from jax.experimental.pallas import tpu as pltpu
from jax.sharding import PartitionSpec as P

DH = 72
FRAMES = 16
LANES = 128
BF16 = jnp.bfloat16
F32 = jnp.float32
VMEM = pl.BlockSpec(memory_space=pltpu.VMEM)
SMEM = pl.BlockSpec(memory_space=pltpu.SMEM)
LIMIT = 40 * 1024 * 1024


def dot(left, right):
    return jnp.dot(left, right, preferred_element_type=F32)


def dot_bt(left, right):
    return lax.dot_general(left, right, (((1,), (1,)), ((), ())), preferred_element_type=F32)


def dot_at(left, right):
    return lax.dot_general(left, right, (((0,), (0,)), ((), ())), preferred_element_type=F32)


def call(body, outs, args, scratch=(), us=1):
    moved = sum(math.prod(a.shape) * a.dtype.itemsize for a in (*args, *outs))
    return pl.pallas_call(
        body,
        out_shape=outs,
        in_specs=[SMEM if a.dtype == jnp.int32 else VMEM for a in args],
        out_specs=[VMEM] * len(outs),
        scratch_shapes=list(scratch),
        compiler_params=pltpu.CompilerParams(vmem_limit_bytes=LIMIT),
        cost_estimate=pl.CostEstimate(flops=us * 1150000000, bytes_accessed=moved, transcendentals=0),
    )(*args)


def shape(dims, dtype=BF16):
    return jax.ShapeDtypeStruct(dims, dtype)


def window(head):
    low = head * DH // LANES * LANES
    high = -(-(head + 1) * DH // LANES) * LANES
    return low, high


def head_only(block, head):
    low, high = window(head)
    lane = lax.broadcasted_iota(jnp.int32, (1, high - low), 1) + low
    keep = (lane >= head * DH) & (lane < (head + 1) * DH)
    return jnp.where(keep, block, jnp.zeros_like(block))


def add_tiles(tiles, head, value):
    low, high = window(head)
    for at in range(low // LANES, high // LANES):
        part = value[:, at * LANES - low : (at + 1) * LANES - low]
        tiles[at] = part if tiles[at] is None else tiles[at] + part


def joined(tiles):
    return jnp.concatenate([tile.astype(BF16) for tile in tiles], axis=1)


def same_group(rows, kind):
    row = lax.broadcasted_iota(jnp.int32, (rows, rows), 0)
    col = lax.broadcasted_iota(jnp.int32, (rows, rows), 1)
    how, size = kind
    return row // size == col // size if how == "block" else row % size == col % size


def softmax_forward(q_ref, k_ref, v_ref, p_ref, heads, kind):
    rows = q_ref.shape[0]
    mask = same_group(rows, kind)
    tiles = [None] * (q_ref.shape[1] // LANES)
    for head in range(heads):
        low, high = window(head)
        s = dot_bt(q_ref[:, low:high], head_only(k_ref[:, low:high], head)) * (1.0 / math.sqrt(DH))
        s = jnp.where(mask, s, -jnp.inf)
        e = jnp.exp(s - jnp.max(s, axis=1, keepdims=True))
        p = e / jnp.sum(e, axis=1, keepdims=True)
        p_ref[head] = p
        add_tiles(tiles, head, dot(p.astype(BF16), head_only(v_ref[:, low:high], head)))
    return joined(tiles)


def softmax_backward(q_ref, k_ref, v_ref, g_ref, p_ref, heads):
    count = q_ref.shape[1] // LANES
    dq, dk, dv = [None] * count, [None] * count, [None] * count
    for head in range(heads):
        low, high = window(head)
        p = p_ref[head]
        g = head_only(g_ref[:, low:high], head)
        add_tiles(dv, head, dot_at(p.astype(BF16), g))
        dp = dot_bt(g, v_ref[:, low:high])
        ds = p * (dp - jnp.sum(p * dp, axis=1, keepdims=True)) * (1.0 / math.sqrt(DH))
        ds = ds.astype(BF16)
        add_tiles(dq, head, dot(ds, head_only(k_ref[:, low:high], head)))
        add_tiles(dk, head, dot_at(ds, head_only(q_ref[:, low:high], head)))
    return joined(dq), joined(dk), joined(dv)


def put(ref, value):
    width = value.shape[1]
    ref[:, width // LANES * LANES :] = jnp.zeros(
        (ref.shape[0], ref.shape[1] - width // LANES * LANES), ref.dtype
    )
    ref[:, :width] = value


def emit_part(idx, left, right, outs, cols=None, full=None):
    if len(outs) == 1:
        outs[0][...] = dot_at(left, right).astype(BF16)
        return
    count, rows, width = outs[0].shape
    size = width // count
    for r in range(count):
        cols[r] = right[:, r * size : (r + 1) * size]
    for r in range(count):
        full[...] = dot_at(left, cols[idx[0] ^ r])
        for e, out in enumerate(outs):
            blocks = []
            for q in range(count):
                low = pl.multiple_of((idx[2] ^ (2 * q + e)) * rows, rows)
                blocks.append(full[pl.ds(low, rows)])
            out[r] = jnp.concatenate(blocks, axis=1).astype(BF16)


def spatial_kernel(peers, patches, tok, cot, qkv, wos, packed, hid, p_ref, qs, ks, vs):
    rows, width = tok.shape
    inner = wos.shape[0]
    x = qkv[...]
    put(qs, x[:, :inner])
    put(ks, x[:, inner : 2 * inner])
    put(vs, x[:, 2 * inner :])
    o = softmax_forward(qs, ks, vs, p_ref, inner // DH, ("block", patches))[:, :inner]
    hidden = (tok[...].astype(F32) + dot(o, wos[...])).astype(BF16)
    hid[...] = hidden
    each = patches // peers
    low = 0
    for value in (hidden, cot[...], o):
        value = value.astype(F32)
        for at in range(peers):
            cut = [
                value[f * patches + at * each : f * patches + (at + 1) * each]
                for f in range(rows // patches)
            ]
            packed[at, :, low : low + value.shape[1]] = jnp.concatenate(cut, axis=0).astype(BF16)
        low += value.shape[1]


def temporal_forward_kernel(shards, group, parts, idx, packed, wot, *refs):
    weights, refs = refs[: len(shards)], refs[len(shards) :]
    q, k, v, g, p_ref, spat, cot, out = refs[:8]
    part = refs[8 : 8 + parts]
    blocks, hid, *work = refs[8 + parts :]
    inner, width = wot.shape
    chunk = packed.shape[1]
    for at in range(packed.shape[0]):
        rows = slice(at * chunk, (at + 1) * chunk)
        hid[rows] = packed[at, :, :width]
        cot[rows] = packed[at, :, width : 2 * width]
        spat[rows] = packed[at, :, 2 * width :]
    hidden = hid[...]
    for (place, count), w in zip(shards, weights):
        block = dot_bt(hidden, w[...]).astype(BF16)
        size = block.shape[1] // count
        for i in range(count):
            blocks[place(idx) + i] = block[:, i * size : (i + 1) * size]
    whole = jnp.concatenate([blocks[i] for i in range(blocks.shape[0])], axis=1)
    put(q, whole[:, :inner])
    put(k, whole[:, inner : 2 * inner])
    put(v, whole[:, 2 * inner :])
    o = softmax_forward(q, k, v, p_ref, inner // DH, ("cycle", group))[:, :inner]
    out[...] = o
    emit_part(idx, o, cot[...], part, *work)
    put(g, dot_bt(cot[...], wot[...]).astype(BF16))


def temporal_backward_kernel(shards, parts, idx, q, k, v, g, p_ref, spat, cot, out, *refs):
    weights, refs = refs[: len(shards)], refs[len(shards) :]
    packed = refs[0]
    part = refs[1 : 1 + parts]
    blocks, *work = refs[1 + parts :]
    inner = spat.shape[1]
    width = cot.shape[1]
    dq, dk, dv = softmax_backward(q, k, v, g, p_ref, inner // DH)
    whole = jnp.concatenate([dq[:, :inner], dk[:, :inner], dv[:, :inner]], axis=1)
    size = blocks.shape[2]
    for i in range(blocks.shape[0]):
        blocks[i] = whole[:, i * size : (i + 1) * size]
    total = jnp.zeros(cot.shape, F32)
    for (place, count), w in zip(shards, weights):
        lhs = jnp.concatenate([blocks[place(idx) + i] for i in range(count)], axis=1)
        total += dot(lhs, w[...])
    grad = (cot[...].astype(F32) + total.astype(BF16).astype(F32)).astype(BF16)
    chunk = packed.shape[1]
    for at in range(packed.shape[0]):
        rows = slice(at * chunk, (at + 1) * chunk)
        packed[at, :, :width] = grad[rows]
        packed[at, :, width:] = out[rows]
    emit_part(idx, spat[...], grad, part, *work)


def last_kernel(patches, qkv, p_ref, hid, wos, wot, packed, block_out, out, grads, qs, ks, vs, gs):
    inner, width = wos.shape
    peers, chunk, _ = packed.shape
    each = patches // peers
    rows = [packed[at].astype(F32) for at in range(peers)]
    rows = [rows[at][f * each : (f + 1) * each] for f in range(chunk // each) for at in range(peers)]
    rows = jnp.concatenate(rows, axis=0).astype(BF16)
    grad, attended = rows[:, :width], rows[:, width:]
    out[...] = grad
    put(gs, dot_bt(grad, wos[...]).astype(BF16))
    x = qkv[...]
    put(qs, x[:, :inner])
    put(ks, x[:, inner : 2 * inner])
    put(vs, x[:, 2 * inner :])
    dq, dk, dv = softmax_backward(qs, ks, vs, gs, p_ref, inner // DH)
    grads[...] = jnp.concatenate([dq[:, :inner], dk[:, :inner], dv[:, :inner]], axis=1)
    block_out[...] = (hid[...].astype(F32) + dot(attended, wot[...])).astype(BF16)


def sum_cores_kernel(keep, got, own, *outs):
    for r in range(keep.shape[0]):
        total = keep[r].astype(F32) + got[r].astype(F32)
        if r == 0:
            own[...] = total
        else:
            outs[r - 1][...] = total.astype(BF16)


def sum_dp_kernel(own, *refs):
    got, outs = refs[: len(refs) // 2], refs[len(refs) // 2 :]
    total = own[...]
    for part in got:
        total += part[...].astype(F32)
    size = total.shape[1] // len(outs)
    for q, out in enumerate(outs):
        out[...] = total[:, q * size : (q + 1) * size].astype(out.dtype)


def sum_kernel(own, *refs):
    total = own[...]
    for part in refs[:-1]:
        total += part[...].astype(F32)
    refs[-1][...] = total


def flip(value, axis, bit):
    return lax.ppermute(value, axis, [(i, i ^ bit) for i in range(lax.axis_size(axis))])


def gather_weight(weight, core):
    n = lax.axis_size("dp")
    if n != 4:
        return [lax.all_gather(weight, "dp", axis=0, tiled=True)], [(lambda idx: 0, 1)], 1
    half = weight.shape[0] // 2
    mine = lax.dynamic_slice_in_dim(weight, core * half, half, 0)
    near = [flip(mine, "dp", j) for j in range(1, n)]
    far = [flip(w, "seq", 1) for w in near]
    shards = [(lambda idx: 2 * idx[0], 2)]
    shards += [(lambda idx, j=j: 2 * (idx[0] ^ j) + idx[1], 1) for j in range(1, n)]
    shards += [(lambda idx, j=j: 2 * (idx[0] ^ j) + 1 - idx[1], 1) for j in range(1, n)]
    return [weight, *near, *far], shards, 2 * n


def reduced(part):
    if len(part) == 1:
        over_seq = lax.psum_scatter(part[0], "seq", scatter_dimension=0, tiled=True)
        return lax.psum_scatter(over_seq, "dp", scatter_dimension=1, tiled=True).astype(F32)
    keep, send = part
    count, rows, width = keep.shape
    own, *sends = call(
        sum_cores_kernel,
        [shape((rows, width), F32)] + [shape((rows, width))] * (count - 1),
        [keep, flip(send, "seq", 1)],
    )
    got = [flip(value, "dp", r + 1) for r, value in enumerate(sends)]
    block = (rows, width // count)
    own, *sends = call(
        sum_dp_kernel, [shape(block, F32)] + [shape(block)] * (count - 1), [own, *got]
    )
    got = [flip(value, "seq", 2 * (q + 1)) for q, value in enumerate(sends)]
    return call(sum_kernel, [shape(block, F32)], [own, *got])[0]


def shards(tokens, spatial_qkv, wo_spatial, w_temporal, wo_temporal, cotangent):
    frames, patches, width = tokens.shape
    inner = wo_spatial.shape[0]
    heads = inner // DH
    padded = -(-inner // LANES) * LANES
    rows = frames * patches
    peers = FRAMES // frames
    each = patches // peers
    chunk = rows // peers
    n_seq = lax.axis_size("seq")
    n_dp = lax.axis_size("dp")
    seq = lax.axis_index("seq")
    idx = jnp.stack([lax.axis_index("dp"), seq % 2, seq]).astype(jnp.int32)
    wide = pltpu.VMEM((rows, padded), BF16)

    weights, places, count = gather_weight(w_temporal.T, seq % 2)
    blocks = pltpu.VMEM((count, rows, 3 * inner // count), BF16)
    part, work = [shape((inner, width))], []
    if n_dp == 4 and n_seq == 8:
        part = [shape((n_dp, inner // n_seq, width))] * 2
        work = [
            pltpu.VMEM((n_dp, rows, width // n_dp), BF16),
            pltpu.VMEM((inner, width // n_dp), F32),
        ]
    groups = None
    if n_seq > peers:
        groups = [list(range(i, i + peers)) for i in range(0, n_seq, peers)]

    def exchange(value):
        return lax.all_to_all(
            value, "seq", split_axis=0, concat_axis=0, tiled=True, axis_index_groups=groups
        )

    qkv_rows = spatial_qkv.reshape(rows, 3 * inner)
    packed, hidden, spatial_p = call(
        functools.partial(spatial_kernel, peers, patches),
        [
            shape((peers, chunk, 2 * width + inner)),
            shape((rows, width)),
            shape((heads, rows, rows), F32),
        ],
        [tokens.reshape(rows, width), cotangent.reshape(rows, width), qkv_rows, wo_spatial],
        [wide] * 3,
        us=3,
    )
    packed = exchange(packed)

    q, k, v, g, temporal_p, spat, cot, out, *temporal_part = call(
        functools.partial(temporal_forward_kernel, places, each, len(part)),
        [shape((rows, padded))] * 4
        + [shape((heads, rows, rows), F32), shape((rows, inner)), shape((rows, width))]
        + [shape((rows, inner)), *part],
        [idx, packed, wo_temporal, *weights],
        [blocks, pltpu.VMEM((rows, width), BF16), *work],
        us=7,
    )
    back, *spatial_part = call(
        functools.partial(temporal_backward_kernel, places, len(part)),
        [shape((peers, chunk, width + inner)), *part],
        [idx, q, k, v, g, temporal_p, spat, cot, out, *weights],
        [blocks, *work],
        us=7,
    )
    back = exchange(back)
    block_out, tokens_grad, qkv_grad = call(
        functools.partial(last_kernel, patches),
        [shape((rows, width)), shape((rows, width)), shape((rows, 3 * inner))],
        [qkv_rows, spatial_p, hidden, wo_spatial, wo_temporal, back],
        [wide] * 4,
        us=7,
    )
    return (
        block_out.reshape(frames, patches, width),
        tokens_grad.reshape(frames, patches, width),
        qkv_grad.reshape(frames, patches, 3 * inner),
        reduced(spatial_part),
        reduced(temporal_part),
    )


def solution(mesh):
    placed = (
        P(("dp", "seq"), None, None),
        P(("dp", "seq"), None, None),
        P(),
        P(None, "dp"),
        P(),
        P(("dp", "seq"), None, None),
    )
    return jax.shard_map(
        shards,
        mesh=mesh,
        in_specs=placed,
        out_specs=(
            P(("dp", "seq"), None, None),
            P(("dp", "seq"), None, None),
            P(("dp", "seq"), None, None),
            P("seq", "dp"),
            P("seq", "dp"),
        ),
        check_vma=False,
    )
```

```python
import functools
import math

import jax
import jax.numpy as jnp
from jax import lax
from jax.experimental import pallas as pl
from jax.experimental.pallas import tpu as pltpu
from jax.sharding import PartitionSpec as P

DH = 72
FRAMES = 16
LANES = 128
BF16 = jnp.bfloat16
F32 = jnp.float32
VMEM = pl.BlockSpec(memory_space=pltpu.VMEM)
SMEM = pl.BlockSpec(memory_space=pltpu.SMEM)
HBM = pl.BlockSpec(memory_space=pltpu.HBM)
LIMIT = 40 * 1024 * 1024
MOST = 60 * 1024 * 1024


def dot(left, right):
    return jnp.dot(left, right, preferred_element_type=F32)


def dot_bt(left, right):
    return lax.dot_general(left, right, (((1,), (1,)), ((), ())), preferred_element_type=F32)


def dot_at(left, right):
    return lax.dot_general(left, right, (((0,), (0,)), ((), ())), preferred_element_type=F32)


def call(body, outs, args, scratch=(), us=1, far_in=(), far_out=()):
    moved = sum(math.prod(a.shape) * a.dtype.itemsize for a in (*args, *outs))
    near = [SMEM if a.dtype == jnp.int32 else VMEM for a in args]
    return pl.pallas_call(
        body,
        out_shape=outs,
        in_specs=[HBM if i in far_in else spec for i, spec in enumerate(near)],
        out_specs=[HBM if i in far_out else VMEM for i in range(len(outs))],
        scratch_shapes=list(scratch),
        compiler_params=pltpu.CompilerParams(vmem_limit_bytes=MOST if far_in else LIMIT),
        cost_estimate=pl.CostEstimate(
            flops=us * 1150000000, bytes_accessed=moved, transcendentals=0
        ),
    )(*args)


def started(pairs, sems):
    copies = [pltpu.make_async_copy(a, b, sems.at[i]) for i, (a, b) in enumerate(pairs)]
    for copy in copies:
        copy.start()
    return copies


def shape(dims, dtype=BF16):
    return jax.ShapeDtypeStruct(dims, dtype)


def window(head):
    low = head * DH // LANES * LANES
    high = -(-(head + 1) * DH // LANES) * LANES
    return low, high


def head_only(block, head):
    low, high = window(head)
    lane = lax.broadcasted_iota(jnp.int32, (1, high - low), 1) + low
    keep = (lane >= head * DH) & (lane < (head + 1) * DH)
    return jnp.where(keep, block, jnp.zeros_like(block))


def add_tiles(tiles, head, value):
    low, high = window(head)
    for at in range(low // LANES, high // LANES):
        part = value[:, at * LANES - low : (at + 1) * LANES - low]
        tiles[at] = part if tiles[at] is None else tiles[at] + part


def joined(tiles):
    return jnp.concatenate([tile.astype(BF16) for tile in tiles], axis=1)


def same_group(rows, kind):
    row = lax.broadcasted_iota(jnp.int32, (rows, rows), 0)
    col = lax.broadcasted_iota(jnp.int32, (rows, rows), 1)
    how, size = kind
    return row // size == col // size if how == "block" else row % size == col % size


def softmax_forward(q_ref, k_ref, v_ref, p_ref, heads, kind):
    rows = q_ref.shape[0]
    mask = same_group(rows, kind)
    tiles = [None] * (q_ref.shape[1] // LANES)
    for head in range(heads):
        low, high = window(head)
        s = dot_bt(q_ref[:, low:high], head_only(k_ref[:, low:high], head)) * (1.0 / math.sqrt(DH))
        s = jnp.where(mask, s, -jnp.inf)
        e = jnp.exp(s - jnp.max(s, axis=1, keepdims=True))
        p = e / jnp.sum(e, axis=1, keepdims=True)
        p_ref[head] = p
        add_tiles(tiles, head, dot(p.astype(BF16), head_only(v_ref[:, low:high], head)))
    return joined(tiles)


def softmax_backward(q_ref, k_ref, v_ref, g_ref, p_ref, heads):
    count = q_ref.shape[1] // LANES
    dq, dk, dv = [None] * count, [None] * count, [None] * count
    for head in range(heads):
        low, high = window(head)
        p = p_ref[head]
        g = head_only(g_ref[:, low:high], head)
        add_tiles(dv, head, dot_at(p.astype(BF16), g))
        dp = dot_bt(g, v_ref[:, low:high])
        ds = p * (dp - jnp.sum(p * dp, axis=1, keepdims=True)) * (1.0 / math.sqrt(DH))
        ds = ds.astype(BF16)
        add_tiles(dq, head, dot(ds, head_only(k_ref[:, low:high], head)))
        add_tiles(dk, head, dot_at(ds, head_only(q_ref[:, low:high], head)))
    return joined(dq), joined(dk), joined(dv)


def put(ref, value):
    width = value.shape[1]
    ref[:, width // LANES * LANES :] = jnp.zeros(
        (ref.shape[0], ref.shape[1] - width // LANES * LANES), ref.dtype
    )
    ref[:, :width] = value


def chunks_of(value, peers, patches):
    rows = value.shape[0]
    each = patches // peers
    value = value.astype(F32)
    for at in range(peers):
        low = at * each
        cut = [value[low + f : low + f + each] for f in range(0, rows, patches)]
        yield at, jnp.concatenate(cut, axis=0).astype(BF16)


def spatial_kernel(peers, patches, *refs):
    far, (hid_out, back_out, hid_far, p_far), refs = refs[:4], refs[4:8], refs[8:]
    tok, cot, qkv, wos, ahead, behind, hid, p_ref, qs, ks, vs, sems = refs
    width = tok.shape[1]
    inner = wos.shape[0]
    loads = started(zip(far, (tok, cot, qkv, wos)), sems)
    loads[2].wait()
    x = qkv[...]
    put(qs, x[:, :inner])
    put(ks, x[:, inner : 2 * inner])
    put(vs, x[:, 2 * inner :])
    o = softmax_forward(qs, ks, vs, p_ref, inner // DH, ("block", patches))[:, :inner]
    loads[0].wait()
    loads[3].wait()
    hid[...] = (tok[...].astype(F32) + dot(o, wos[...])).astype(BF16)
    for at, rows in chunks_of(hid[...], peers, patches):
        ahead[at] = rows
    stores = started([(ahead, hid_out), (p_ref, p_far), (hid, hid_far)], sems.at[pl.ds(4, 3)])
    loads[1].wait()
    for at, rows in chunks_of(cot[...], peers, patches):
        behind[at, :, :width] = rows
    for at, rows in chunks_of(o, peers, patches):
        behind[at, :, width:] = rows
    stores += started([(behind, back_out)], sems.at[pl.ds(7, 1)])
    for copy in stores:
        copy.wait()


def split_kernel(near_x, near_y, _, from_x, from_y):
    cut = from_y.shape[1]
    from_y[...] = near_y[:, :cut]
    from_x[...] = near_x[:, cut:]


def pieces(shards, weights):
    weights = list(weights)
    for place, count, parts in shards:
        low, held = 0, []
        for _ in range(parts):
            w = weights.pop(0)
            held.append((low, w))
            low += w.shape[1]
        yield place, count, held


def temporal_forward_kernel(shards, total, group, inner, idx, packed, *refs):
    weights, (q, k, v, p_ref, out, blocks, hid) = refs[:total], refs[total:]
    chunk = packed.shape[1]
    for at in range(packed.shape[0]):
        hid[at * chunk : (at + 1) * chunk] = packed[at]
    for place, count, held in pieces(shards, weights):
        block = None
        for low, w in held:
            value = dot_bt(hid[:, low : low + w.shape[1]], w[...])
            block = value if block is None else block + value
        block = block.astype(BF16)
        size = block.shape[1] // count
        for i in range(count):
            blocks[place(idx) + i] = block[:, i * size : (i + 1) * size]
    whole = jnp.concatenate([blocks[i] for i in range(blocks.shape[0])], axis=1)
    put(q, whole[:, :inner])
    put(k, whole[:, inner : 2 * inner])
    put(v, whole[:, 2 * inner :])
    out[...] = softmax_forward(q, k, v, p_ref, inner // DH, ("cycle", group))[:, :inner]


def temporal_backward_kernel(shards, total, idx, q, k, v, p_ref, out, held_back, wot, *refs):
    weights, (packed, mine, blocks, cot, g) = refs[:total], refs[total:]
    inner, width = wot.shape
    chunk = packed.shape[1]
    for at in range(packed.shape[0]):
        rows = slice(at * chunk, (at + 1) * chunk)
        cot[rows] = held_back[at, :, :width]
        mine[rows, inner : 2 * inner] = held_back[at, :, width:]
    put(g, dot_bt(cot[...], wot[...]).astype(BF16))
    dq, dk, dv = softmax_backward(q, k, v, g, p_ref, inner // DH)
    whole = jnp.concatenate([dq[:, :inner], dk[:, :inner], dv[:, :inner]], axis=1)
    size = blocks.shape[2]
    for i in range(blocks.shape[0]):
        blocks[i] = whole[:, i * size : (i + 1) * size]
    grad = jnp.zeros(cot.shape, F32)
    for place, count, held in pieces(shards, weights):
        lhs = jnp.concatenate([blocks[place(idx) + i] for i in range(count)], axis=1)
        grad += jnp.concatenate([dot(lhs, w[...]) for _, w in held], axis=1)
    grad = (cot[...].astype(F32) + grad.astype(BF16).astype(F32)).astype(BF16)
    for at in range(packed.shape[0]):
        rows = slice(at * chunk, (at + 1) * chunk)
        packed[at, :, :width] = grad[rows]
        packed[at, :, width:] = out[rows]
    mine[:, :inner] = out[...]
    mine[:, 2 * inner : 2 * inner + width] = cot[...]
    mine[:, 2 * inner + width :] = grad


def whole_parts_kernel(inner, width, mine, out):
    for i in range(2):
        right = mine[:, 2 * inner + i * width : 2 * inner + (i + 1) * width]
        out[i] = dot_at(mine[:, i * inner : (i + 1) * inner], right).astype(BF16)


def parts_kernel(inner, width, idx, mine, other, own, *refs):
    outs, (heads, cols) = refs[:-2], refs[-2:]
    count = cols.shape[0]
    rows = mine.shape[0]
    size = heads.shape[2]
    wide = cols.shape[2]
    for i in range(2):
        for at, ref in enumerate((mine, other)):
            held = slice(at * rows, (at + 1) * rows)
            for h in range(heads.shape[0]):
                low = i * inner + h * size
                heads[h, held] = ref[:, low : low + size]
            for r in range(count):
                low = 2 * inner + i * width + r * wide
                cols[r, held] = ref[:, low : low + wide]
        left = jnp.concatenate([heads[idx[2] ^ (2 * q)] for q in range(count)], axis=1)
        for r in range(count):
            full = dot_at(left, cols[idx[0] ^ r])
            block = jnp.concatenate([full[q * size : (q + 1) * size] for q in range(count)], axis=1)
            if r == 0:
                own[i] = block
            else:
                outs[r - 1][i] = block.astype(BF16)


def sum_dp_kernel(own, *refs):
    got, outs = refs[: len(refs) // 2], refs[len(refs) // 2 :]
    for i in range(own.shape[0]):
        total = own[i]
        for part in got:
            total += part[i].astype(F32)
        size = total.shape[1] // len(outs)
        for q, out in enumerate(outs):
            out[i] = total[:, q * size : (q + 1) * size].astype(out.dtype)


def sum_kernel(own, *refs):
    got, outs = refs[:-2], refs[-2:]
    for i, out in enumerate(outs):
        total = own[i]
        for part in got:
            total += part[i].astype(F32)
        out[...] = total


def last_kernel(patches, qkv, p_ref, hid, wos, wot, packed, block_out, out, grads, *refs):
    here, (qs, ks, vs, gs, sems) = refs[:5], refs[5:]
    loads = started(zip((wos, qkv, p_ref, wot, hid), here), sems)
    wos, qkv, p_ref, wot, hid = here
    inner, width = wos.shape
    peers, chunk, _ = packed.shape
    each = patches // peers
    rows = [packed[at].astype(F32) for at in range(peers)]
    rows = [rows[at][f * each : (f + 1) * each] for f in range(chunk // each) for at in range(peers)]
    rows = jnp.concatenate(rows, axis=0).astype(BF16)
    grad, attended = rows[:, :width], rows[:, width:]
    out[...] = grad
    loads[0].wait()
    put(gs, dot_bt(grad, wos[...]).astype(BF16))
    loads[1].wait()
    x = qkv[...]
    put(qs, x[:, :inner])
    put(ks, x[:, inner : 2 * inner])
    put(vs, x[:, 2 * inner :])
    loads[2].wait()
    dq, dk, dv = softmax_backward(qs, ks, vs, gs, p_ref, inner // DH)
    grads[...] = jnp.concatenate([dq[:, :inner], dk[:, :inner], dv[:, :inner]], axis=1)
    loads[3].wait()
    loads[4].wait()
    block_out[...] = (hid[...].astype(F32) + dot(attended, wot[...])).astype(BF16)


def flip(value, axis, bit):
    return lax.ppermute(value, axis, [(i, i ^ bit) for i in range(lax.axis_size(axis))])


def gather_weight(weight, core, after):
    n = lax.axis_size("dp")
    if n != 4:
        return [lax.all_gather(weight, "dp", axis=0, tiled=True)], [(lambda idx: 0, 1, 1)], 1
    half, width = weight.shape[0] // 2, weight.shape[1]
    mine = lax.dynamic_slice_in_dim(weight, core * half, half, 0)
    near = [flip(mine, "dp", 1), flip(mine, "dp", 2)]
    cut = width // LANES // 2 * LANES
    from_x, from_y = call(
        split_kernel, [shape((half, width - cut)), shape((half, cut))], [*near, after]
    )
    corner = [flip(from_y, "dp", 1), flip(from_x, "dp", 2)]
    held = near + corner
    far = [flip(w, "seq", 1) for w in held]
    shards = [(lambda idx: 2 * idx[0], 2, 1)]
    for flipped in range(2):
        for j in range(1, n):
            shards.append(
                (
                    lambda idx, j=j, flipped=flipped: 2 * (idx[0] ^ j) + (idx[1] ^ flipped),
                    1,
                    1 if j < 3 else 2,
                )
            )
    return [weight, *held, *far], shards, 2 * n


def reduced(mine, inner, width, idx):
    n_dp, n_seq = lax.axis_size("dp"), lax.axis_size("seq")
    if n_dp != 4 or n_seq != 8:
        (both,) = call(
            functools.partial(whole_parts_kernel, inner, width), [shape((2, inner, width))], [mine]
        )
        both = lax.psum_scatter(both, "seq", scatter_dimension=1, tiled=True)
        both = lax.psum_scatter(both, "dp", scatter_dimension=2, tiled=True).astype(F32)
        return both[0], both[1]
    rows = mine.shape[0]
    size = inner // n_seq
    part = (2, size, width)
    own, *sends = call(
        functools.partial(parts_kernel, inner, width),
        [shape(part, F32)] + [shape(part)] * (n_dp - 1),
        [idx, mine, flip(mine, "seq", 1)],
        [
            pltpu.VMEM((n_seq, 2 * rows, size), BF16),
            pltpu.VMEM((n_dp, 2 * rows, width // n_dp), BF16),
        ],
        us=3,
    )
    got = [flip(value, "dp", r + 1) for r, value in enumerate(sends)]
    block = (2, size, width // n_dp)
    own, *sends = call(
        sum_dp_kernel, [shape(block, F32)] + [shape(block)] * (n_dp - 1), [own, *got]
    )
    got = [flip(value, "seq", 2 * (q + 1)) for q, value in enumerate(sends)]
    return call(sum_kernel, [shape(block[1:], F32)] * 2, [own, *got])


def shards(tokens, spatial_qkv, wo_spatial, w_temporal, wo_temporal, cotangent):
    frames, patches, width = tokens.shape
    inner = wo_spatial.shape[0]
    heads = inner // DH
    padded = -(-inner // LANES) * LANES
    rows = frames * patches
    peers = FRAMES // frames
    each = patches // peers
    chunk = rows // peers
    n_seq = lax.axis_size("seq")
    seq = lax.axis_index("seq")
    idx = jnp.stack([lax.axis_index("dp"), seq % 2, seq]).astype(jnp.int32)
    wide = pltpu.VMEM((rows, padded), BF16)
    weights_of = pltpu.VMEM((heads, rows, rows), F32)
    model = pltpu.VMEM((rows, width), BF16)
    projection = pltpu.VMEM((inner, width), BF16)
    groups = None
    if n_seq > peers:
        groups = [list(range(i, i + peers)) for i in range(0, n_seq, peers)]

    def exchange(value):
        return lax.all_to_all(
            value, "seq", split_axis=0, concat_axis=0, tiled=True, axis_index_groups=groups
        )

    qkv_rows = spatial_qkv.reshape(rows, 3 * inner)
    ahead = (peers, chunk, width)
    behind = (peers, chunk, width + inner)
    ahead_sent, behind_sent, hidden, spatial_p = call(
        functools.partial(spatial_kernel, peers, patches),
        [shape(ahead), shape(behind), shape((rows, width)), shape((heads, rows, rows), F32)],
        [tokens.reshape(rows, width), cotangent.reshape(rows, width), qkv_rows, wo_spatial],
        [model, model, pltpu.VMEM((rows, 3 * inner), BF16), projection]
        + [pltpu.VMEM(ahead, BF16), pltpu.VMEM(behind, BF16), model, weights_of]
        + [wide] * 3
        + [pltpu.SemaphoreType.DMA((8,))],
        us=3,
        far_in=range(4),
        far_out=range(4),
    )
    weights, places, count = gather_weight(w_temporal.T, seq % 2, hidden[:8, :LANES])
    blocks = pltpu.VMEM((count, rows, 3 * inner // count), BF16)
    q, k, v, temporal_p, out = call(
        functools.partial(temporal_forward_kernel, places, len(weights), each, inner),
        [shape((rows, padded))] * 3 + [shape((heads, rows, rows), F32), shape((rows, inner))],
        [idx, exchange(ahead_sent), *weights],
        [blocks, model],
        us=6,
    )
    back, mine = call(
        functools.partial(temporal_backward_kernel, places, len(weights)),
        [shape(behind), shape((rows, 2 * (inner + width)))],
        [idx, q, k, v, temporal_p, out, exchange(behind_sent), wo_temporal, *weights],
        [blocks, model, wide],
        us=6,
    )
    block_out, tokens_grad, qkv_grad = call(
        functools.partial(last_kernel, patches),
        [shape((rows, width)), shape((rows, width)), shape((rows, 3 * inner))],
        [qkv_rows, spatial_p, hidden, wo_spatial, wo_temporal, exchange(back)],
        [projection, pltpu.VMEM((rows, 3 * inner), BF16), weights_of, projection, model]
        + [wide] * 4
        + [pltpu.SemaphoreType.DMA((5,))],
        us=6,
        far_in=range(5),
    )
    temporal_grad, spatial_grad = reduced(mine, inner, width, idx)
    return (
        block_out.reshape(frames, patches, width),
        tokens_grad.reshape(frames, patches, width),
        qkv_grad.reshape(frames, patches, 3 * inner),
        spatial_grad,
        temporal_grad,
    )


def solution(mesh):
    placed = (
        P(("dp", "seq"), None, None),
        P(("dp", "seq"), None, None),
        P(),
        P(None, "dp"),
        P(),
        P(("dp", "seq"), None, None),
    )
    return jax.shard_map(
        shards,
        mesh=mesh,
        in_specs=placed,
        out_specs=(
            P(("dp", "seq"), None, None),
            P(("dp", "seq"), None, None),
            P(("dp", "seq"), None, None),
            P("seq", "dp"),
            P("seq", "dp"),
        ),
        check_vma=False,
    )
```

```python
import functools
import math

import jax
import jax.numpy as jnp
from jax import lax
from jax.experimental import pallas as pl
from jax.experimental.pallas import tpu as pltpu
from jax.sharding import PartitionSpec as P

DH = 72
FRAMES = 16
LANES = 128
BF16 = jnp.bfloat16
F32 = jnp.float32
VMEM = pl.BlockSpec(memory_space=pltpu.VMEM)
SMEM = pl.BlockSpec(memory_space=pltpu.SMEM)
HBM = pl.BlockSpec(memory_space=pltpu.HBM)
LIMIT = 16 * 1024 * 1024
MOST = 60 * 1024 * 1024


def dot(left, right):
    return jnp.dot(left, right, preferred_element_type=F32)


def dot_bt(left, right):
    return lax.dot_general(left, right, (((1,), (1,)), ((), ())), preferred_element_type=F32)


def dot_at(left, right):
    return lax.dot_general(left, right, (((0,), (0,)), ((), ())), preferred_element_type=F32)


def call(body, outs, args, scratch=(), us=1, far_in=(), far_out=(), small=False):
    moved = sum(math.prod(a.shape) * a.dtype.itemsize for a in (*args, *outs))
    near = [SMEM if a.dtype == jnp.int32 else VMEM for a in args]
    return pl.pallas_call(
        body,
        out_shape=outs,
        in_specs=[HBM if i in far_in else spec for i, spec in enumerate(near)],
        out_specs=[HBM if i in far_out else VMEM for i in range(len(outs))],
        scratch_shapes=list(scratch),
        compiler_params=pltpu.CompilerParams(vmem_limit_bytes=LIMIT if small else MOST),
        cost_estimate=pl.CostEstimate(
            flops=us * 1150000000, bytes_accessed=moved, transcendentals=0
        ),
    )(*args)


def started(pairs, sems):
    copies = [pltpu.make_async_copy(a, b, sems.at[i]) for i, (a, b) in enumerate(pairs)]
    for copy in copies:
        copy.start()
    return copies


def shape(dims, dtype=BF16):
    return jax.ShapeDtypeStruct(dims, dtype)


TOKEN = shape((8, LANES), F32)


def window(head):
    low = head * DH // LANES * LANES
    high = -(-(head + 1) * DH // LANES) * LANES
    return low, high


def head_only(block, head):
    low, high = window(head)
    lane = lax.broadcasted_iota(jnp.int32, (1, high - low), 1) + low
    keep = (lane >= head * DH) & (lane < (head + 1) * DH)
    return jnp.where(keep, block, jnp.zeros_like(block))


def add_tiles(tiles, head, value):
    low, high = window(head)
    for at in range(low // LANES, high // LANES):
        part = value[:, at * LANES - low : (at + 1) * LANES - low]
        tiles[at] = part if tiles[at] is None else tiles[at] + part


def joined(tiles):
    return jnp.concatenate([tile.astype(BF16) for tile in tiles], axis=1)


def same_group(rows, kind):
    row = lax.broadcasted_iota(jnp.int32, (rows, rows), 0)
    col = lax.broadcasted_iota(jnp.int32, (rows, rows), 1)
    how, size = kind
    return row // size == col // size if how == "block" else row % size == col % size


def softmax_forward(q_ref, k_ref, v_ref, p_ref, heads, kind):
    rows = q_ref.shape[0]
    mask = same_group(rows, kind)
    tiles = [None] * (q_ref.shape[1] // LANES)
    for head in range(heads):
        low, high = window(head)
        s = dot_bt(q_ref[:, low:high], head_only(k_ref[:, low:high], head)) * (1.0 / math.sqrt(DH))
        s = jnp.where(mask, s, -jnp.inf)
        e = jnp.exp(s - jnp.max(s, axis=1, keepdims=True))
        p = e / jnp.sum(e, axis=1, keepdims=True)
        p_ref[head] = p
        add_tiles(tiles, head, dot(p.astype(BF16), head_only(v_ref[:, low:high], head)))
    return joined(tiles)


def softmax_backward(q_ref, k_ref, v_ref, g_ref, p_ref, heads):
    count = q_ref.shape[1] // LANES
    dq, dk, dv = [None] * count, [None] * count, [None] * count
    for head in range(heads):
        low, high = window(head)
        p = p_ref[head]
        g = head_only(g_ref[:, low:high], head)
        add_tiles(dv, head, dot_at(p.astype(BF16), g))
        dp = dot_bt(g, v_ref[:, low:high])
        ds = p * (dp - jnp.sum(p * dp, axis=1, keepdims=True)) * (1.0 / math.sqrt(DH))
        ds = ds.astype(BF16)
        add_tiles(dq, head, dot(ds, head_only(k_ref[:, low:high], head)))
        add_tiles(dk, head, dot_at(ds, head_only(q_ref[:, low:high], head)))
    return joined(dq), joined(dk), joined(dv)


def put(ref, value):
    width = value.shape[1]
    ref[:, width // LANES * LANES :] = jnp.zeros(
        (ref.shape[0], ref.shape[1] - width // LANES * LANES), ref.dtype
    )
    ref[:, :width] = value


def pack(value, out, low, peers, patches):
    rows, width = value.shape
    each = patches // peers
    value = value.astype(F32)
    cut = [
        value[f + at * each : f + (at + 1) * each]
        for at in range(peers)
        for f in range(0, rows, patches)
    ]
    out[:, low : low + width] = jnp.concatenate(cut, axis=0).astype(BF16)


def pack_kernel(peers, patches, tok_far, cot_far, out_far, tok, cot, out, sems):
    width = tok.shape[1]
    loads = started([(tok_far, tok), (cot_far, cot)], sems)
    loads[0].wait()
    pack(tok[...], out, 0, peers, patches)
    loads[1].wait()
    pack(cot[...], out, width, peers, patches)
    started([(out, out_far)], sems.at[pl.ds(2, 1)])[0].wait()


def spatial_kernel(peers, patches, *refs):
    far, (packed_far, hid_far, p_far, done), refs = refs[:3], refs[3:7], refs[7:]
    done[...] = jnp.zeros_like(done)
    tok, qkv, wos, packed, hid, p_ref, qs, ks, vs, sems = refs
    inner = wos.shape[0]
    loads = started(zip(far, (tok, qkv, wos)), sems)
    loads[1].wait()
    x = qkv[...]
    put(qs, x[:, :inner])
    put(ks, x[:, inner : 2 * inner])
    put(vs, x[:, 2 * inner :])
    o = softmax_forward(qs, ks, vs, p_ref, inner // DH, ("block", patches))[:, :inner]
    pack(o, packed, 0, peers, patches)
    stores = started([(packed, packed_far), (p_ref, p_far)], sems.at[pl.ds(3, 2)])
    loads[0].wait()
    loads[2].wait()
    hid[...] = (tok[...].astype(F32) + dot(o, wos[...])).astype(BF16)
    stores += started([(hid, hid_far)], sems.at[pl.ds(5, 1)])
    for copy in stores:
        copy.wait()


def split_kernel(near_x, near_y, _, from_x, from_y):
    cut = from_y.shape[1]
    from_y[...] = near_y[:, :cut]
    from_x[...] = near_x[:, cut:]


def pieces(shards, weights, loads):
    weights, loads = list(weights), list(loads)
    for place, count, parts in shards:
        low, held = 0, []
        for _ in range(parts):
            w = weights.pop(0)
            loads.pop(0)()
            held.append((low, w))
            low += w.shape[1]
        yield place, count, held


def temporal_kernel(shards, total, group, idx, *refs):
    far, (back_far, mine_far), refs = refs[: 4 + total], refs[4 + total : 6 + total], refs[6 + total :]
    here, refs = refs[: 4 + total], refs[4 + total :]
    back, mine, q, k, v, g, p_ref, blocks, sems = refs
    (packed, so, wos, wot), weights = here[:4], here[4:]
    inner, width = wos.shape
    heads = inner // DH
    loads = started(zip(far, here), sems)
    for at in range(3):
        loads[at].wait()
    mine[:, inner : 2 * inner] = so[...]
    hidden = (packed[:, :width].astype(F32) + dot(so[...], wos[...])).astype(BF16)
    for place, count, held in pieces(shards, weights, [copy.wait for copy in loads[4:]]):
        block = None
        for low, w in held:
            value = dot_bt(hidden[:, low : low + w.shape[1]], w[...])
            block = value if block is None else block + value
        block = block.astype(BF16)
        size = block.shape[1] // count
        for i in range(count):
            blocks[place(idx) + i] = block[:, i * size : (i + 1) * size]
    whole = jnp.concatenate([blocks[i] for i in range(blocks.shape[0])], axis=1)
    put(q, whole[:, :inner])
    put(k, whole[:, inner : 2 * inner])
    put(v, whole[:, 2 * inner :])
    out = softmax_forward(q, k, v, p_ref, heads, ("cycle", group))[:, :inner]
    mine[:, :inner] = out
    back[:, width:] = out
    cot = packed[:, width:]
    mine[:, 2 * inner : 2 * inner + width] = cot
    loads[3].wait()
    put(g, dot_bt(cot, wot[...]).astype(BF16))
    dq, dk, dv = softmax_backward(q, k, v, g, p_ref, heads)
    whole = jnp.concatenate([dq[:, :inner], dk[:, :inner], dv[:, :inner]], axis=1)
    size = blocks.shape[2]
    for i in range(blocks.shape[0]):
        blocks[i] = whole[:, i * size : (i + 1) * size]
    grad = jnp.zeros(cot.shape, F32)
    for place, count, held in pieces(shards, weights, [lambda: None] * total):
        lhs = jnp.concatenate([blocks[place(idx) + i] for i in range(count)], axis=1)
        grad += jnp.concatenate([dot(lhs, w[...]) for _, w in held], axis=1)
    grad = (cot.astype(F32) + grad.astype(BF16).astype(F32)).astype(BF16)
    back[:, :width] = grad
    mine[:, 2 * inner + width :] = grad
    for copy in started([(back, back_far), (mine, mine_far)], sems.at[pl.ds(4 + total, 2)]):
        copy.wait()


def whole_parts_kernel(inner, width, mine, out):
    for i in range(2):
        right = mine[:, 2 * inner + i * width : 2 * inner + (i + 1) * width]
        out[i] = dot_at(mine[:, i * inner : (i + 1) * inner], right).astype(BF16)


def parts_kernel(inner, width, idx, mine, other, own, *refs):
    outs, (heads, cols) = refs[:-2], refs[-2:]
    count = cols.shape[0]
    rows = mine.shape[0]
    size = heads.shape[2]
    wide = cols.shape[2]
    for i in range(2):
        for at, ref in enumerate((mine, other)):
            held = slice(at * rows, (at + 1) * rows)
            for h in range(heads.shape[0]):
                low = i * inner + h * size
                heads[h, held] = ref[:, low : low + size]
            for r in range(count):
                low = 2 * inner + i * width + r * wide
                cols[r, held] = ref[:, low : low + wide]
        left = jnp.concatenate([heads[idx[2] ^ (2 * q)] for q in range(count)], axis=1)
        for r in range(count):
            full = dot_at(left, cols[idx[0] ^ r])
            block = jnp.concatenate([full[q * size : (q + 1) * size] for q in range(count)], axis=1)
            if r == 0:
                own[i] = block
            else:
                outs[r - 1][i] = block.astype(BF16)


def sum_dp_kernel(_, own, *refs):
    got, outs = refs[: len(refs) // 2], refs[len(refs) // 2 :]
    for i in range(own.shape[0]):
        total = own[i]
        for part in got:
            total += part[i].astype(F32)
        size = total.shape[1] // len(outs)
        for q, out in enumerate(outs):
            out[i] = total[:, q * size : (q + 1) * size].astype(out.dtype)


def sum_kernel(own, *refs):
    got, outs = refs[:-2], refs[-2:]
    for i, out in enumerate(outs):
        total = own[i]
        for part in got:
            total += part[i].astype(F32)
        out[...] = total


def last_kernel(patches, *refs):
    far, outs_far, done, refs = refs[:6], refs[6:9], refs[9], refs[10:]
    done[...] = jnp.zeros_like(done)
    packed, wos, qkv, p_ref, wot, hid, out, block_out, grads, qs, ks, vs, gs, sems = refs
    inner, width = wos.shape
    loads = started(zip(far, refs[:6]), sems)
    loads[0].wait()
    rows = packed.shape[0]
    each = rows // FRAMES
    frames = rows // patches
    value = packed[...].astype(F32)
    cut = [
        value[(at * frames + f) * each : (at * frames + f + 1) * each]
        for f in range(frames)
        for at in range(patches // each)
    ]
    value = jnp.concatenate(cut, axis=0).astype(BF16)
    grad, attended = value[:, :width], value[:, width:]
    out[...] = grad
    stores = started([(out, outs_far[1])], sems.at[pl.ds(6, 1)])
    loads[1].wait()
    put(gs, dot_bt(grad, wos[...]).astype(BF16))
    loads[2].wait()
    x = qkv[...]
    put(qs, x[:, :inner])
    put(ks, x[:, inner : 2 * inner])
    put(vs, x[:, 2 * inner :])
    loads[4].wait()
    loads[5].wait()
    block_out[...] = (hid[...].astype(F32) + dot(attended, wot[...])).astype(BF16)
    stores += started([(block_out, outs_far[0])], sems.at[pl.ds(7, 1)])
    loads[3].wait()
    dq, dk, dv = softmax_backward(qs, ks, vs, gs, p_ref, inner // DH)
    grads[...] = jnp.concatenate([dq[:, :inner], dk[:, :inner], dv[:, :inner]], axis=1)
    stores += started([(grads, outs_far[2])], sems.at[pl.ds(8, 1)])
    for copy in stores:
        copy.wait()


def flip(value, axis, bit):
    return lax.ppermute(value, axis, [(i, i ^ bit) for i in range(lax.axis_size(axis))])


def gather_weight(weight, core, after):
    n = lax.axis_size("dp")
    if n != 4:
        return [lax.all_gather(weight, "dp", axis=0, tiled=True)], [(lambda idx: 0, 1, 1)], 1
    half, width = weight.shape[0] // 2, weight.shape[1]
    mine = lax.dynamic_slice_in_dim(weight, core * half, half, 0)
    near = [flip(mine, "dp", 1), flip(mine, "dp", 2)]
    cut = width // LANES // 2 * LANES
    from_x, from_y = call(
        split_kernel, [shape((half, width - cut)), shape((half, cut))], [*near, after],
        small=True,
    )
    corner = [flip(from_y, "dp", 1), flip(from_x, "dp", 2)]
    held = near + corner
    far = [flip(w, "seq", 1) for w in held]
    shards = [(lambda idx: 2 * idx[0], 2, 1)]
    for flipped in range(2):
        for j in range(1, n):
            shards.append(
                (
                    lambda idx, j=j, flipped=flipped: 2 * (idx[0] ^ j) + (idx[1] ^ flipped),
                    1,
                    1 if j < 3 else 2,
                )
            )
    return [weight, *held, *far], shards, 2 * n


def reduced(mine, inner, width, idx, after):
    n_dp, n_seq = lax.axis_size("dp"), lax.axis_size("seq")
    if n_dp != 4 or n_seq != 8:
        (both,) = call(
            functools.partial(whole_parts_kernel, inner, width), [shape((2, inner, width))], [mine]
        )
        both = lax.psum_scatter(both, "seq", scatter_dimension=1, tiled=True)
        both = lax.psum_scatter(both, "dp", scatter_dimension=2, tiled=True).astype(F32)
        return both[0], both[1]
    rows = mine.shape[0]
    size = inner // n_seq
    part = (2, size, width)
    own, *sends = call(
        functools.partial(parts_kernel, inner, width),
        [shape(part, F32)] + [shape(part)] * (n_dp - 1),
        [idx, mine, flip(mine, "seq", 1)],
        [
            pltpu.VMEM((n_seq, 2 * rows, size), BF16),
            pltpu.VMEM((n_dp, 2 * rows, width // n_dp), BF16),
        ],
        us=3,
        small=True,
    )
    got = [flip(value, "dp", r + 1) for r, value in enumerate(sends)]
    block = (2, size, width // n_dp)
    own, *sends = call(
        sum_dp_kernel,
        [shape(block, F32)] + [shape(block)] * (n_dp - 1),
        [after, own, *got],
        small=True,
    )
    got = [flip(value, "seq", 2 * (q + 1)) for q, value in enumerate(sends)]
    return call(sum_kernel, [shape(block[1:], F32)] * 2, [own, *got], small=True)


def shards(tokens, spatial_qkv, wo_spatial, w_temporal, wo_temporal, cotangent):
    frames, patches, width = tokens.shape
    inner = wo_spatial.shape[0]
    heads = inner // DH
    padded = -(-inner // LANES) * LANES
    rows = frames * patches
    peers = FRAMES // frames
    n_seq = lax.axis_size("seq")
    seq = lax.axis_index("seq")
    idx = jnp.stack([lax.axis_index("dp"), seq % 2, seq]).astype(jnp.int32)
    groups = None
    if n_seq > peers:
        groups = [list(range(i, i + peers)) for i in range(0, n_seq, peers)]

    def exchange(value):
        return lax.all_to_all(
            value, "seq", split_axis=0, concat_axis=0, tiled=True, axis_index_groups=groups
        )

    def held(columns, dtype=BF16):
        return pltpu.VMEM((rows, columns), dtype)

    def sems(n):
        return pltpu.SemaphoreType.DMA((n,))

    wide = held(padded)
    attended = pltpu.VMEM((heads, rows, rows), F32)
    projection = pltpu.VMEM((inner, width), BF16)
    token_rows = tokens.reshape(rows, width)
    qkv_rows = spatial_qkv.reshape(rows, 3 * inner)

    (packed,) = call(
        functools.partial(pack_kernel, peers, patches),
        [shape((rows, 2 * width))],
        [token_rows, cotangent.reshape(rows, width)],
        [held(width), held(width), held(2 * width), sems(3)],
        us=2,
        far_in=range(2),
        far_out=range(1),
    )
    spatial_sent, hidden, spatial_p, spatial_done = call(
        functools.partial(spatial_kernel, peers, patches),
        [shape((rows, inner)), shape((rows, width)), shape((heads, rows, rows), F32), TOKEN],
        [token_rows, qkv_rows, wo_spatial],
        [held(width), held(3 * inner), projection, held(inner), held(width), attended]
        + [wide] * 3
        + [sems(6)],
        us=4,
        far_in=range(3),
        far_out=range(3),
    )
    weights, places, count = gather_weight(w_temporal.T, seq % 2, spatial_done)
    blocks = pltpu.VMEM((count, rows, 3 * inner // count), BF16)
    total = len(weights)
    back, mine = call(
        functools.partial(temporal_kernel, places, total, patches // peers),
        [shape((rows, width + inner)), shape((rows, 2 * (inner + width)))],
        [idx, exchange(packed), exchange(spatial_sent), wo_spatial, wo_temporal, *weights],
        [held(2 * width), held(inner), projection, projection]
        + [pltpu.VMEM(w.shape, BF16) for w in weights]
        + [held(width + inner), held(2 * (inner + width))]
        + [wide] * 4
        + [attended, blocks, sems(6 + total)],
        us=10,
        far_in=range(1, 5 + total),
        far_out=range(2),
    )
    block_out, tokens_grad, qkv_grad, last_done = call(
        functools.partial(last_kernel, patches),
        [shape((rows, width)), shape((rows, width)), shape((rows, 3 * inner)), TOKEN],
        [exchange(back), wo_spatial, qkv_rows, spatial_p, wo_temporal, hidden],
        [held(width + inner), projection, held(3 * inner), attended, projection, held(width)]
        + [held(width), held(width), held(3 * inner)]
        + [wide] * 4
        + [sems(9)],
        us=6,
        far_in=range(6),
        far_out=range(3),
    )
    temporal_grad, spatial_grad = reduced(mine, inner, width, idx, last_done)
    return (
        block_out.reshape(frames, patches, width),
        tokens_grad.reshape(frames, patches, width),
        qkv_grad.reshape(frames, patches, 3 * inner),
        spatial_grad,
        temporal_grad,
    )


def solution(mesh):
    placed = (
        P(("dp", "seq"), None, None),
        P(("dp", "seq"), None, None),
        P(),
        P(None, "dp"),
        P(),
        P(("dp", "seq"), None, None),
    )
    return jax.shard_map(
        shards,
        mesh=mesh,
        in_specs=placed,
        out_specs=(
            P(("dp", "seq"), None, None),
            P(("dp", "seq"), None, None),
            P(("dp", "seq"), None, None),
            P("seq", "dp"),
            P("seq", "dp"),
        ),
        check_vma=False,
    )
```

```python
import functools
import math

import jax
import jax.numpy as jnp
from jax import lax
from jax.experimental import pallas as pl
from jax.experimental.pallas import tpu as pltpu
from jax.sharding import PartitionSpec as P

DH = 72
FRAMES = 16
LANES = 128
BF16 = jnp.bfloat16
F32 = jnp.float32
VMEM = pl.BlockSpec(memory_space=pltpu.VMEM)
SMEM = pl.BlockSpec(memory_space=pltpu.SMEM)
HBM = pl.BlockSpec(memory_space=pltpu.HBM)
LIMIT = 16 * 1024 * 1024
MOST = 60 * 1024 * 1024


def dot(left, right):
    return jnp.dot(left, right, preferred_element_type=F32)


def dot_bt(left, right):
    return lax.dot_general(left, right, (((1,), (1,)), ((), ())), preferred_element_type=F32)


def dot_at(left, right):
    return lax.dot_general(left, right, (((0,), (0,)), ((), ())), preferred_element_type=F32)


def call(body, outs, args, scratch=(), us=0, far_in=(), far_out=(), small=False):
    moved = sum(math.prod(a.shape) * a.dtype.itemsize for a in (*args, *outs))
    near = [SMEM if a.dtype == jnp.int32 else VMEM for a in args]
    return pl.pallas_call(
        body,
        out_shape=outs,
        in_specs=[HBM if i in far_in else spec for i, spec in enumerate(near)],
        out_specs=[HBM if i in far_out else VMEM for i in range(len(outs))],
        scratch_shapes=list(scratch),
        compiler_params=pltpu.CompilerParams(vmem_limit_bytes=LIMIT if small else MOST),
        cost_estimate=pl.CostEstimate(
            flops=us * 1150000000, bytes_accessed=moved if us else 0, transcendentals=0
        ),
    )(*args)


def started(pairs, sems):
    copies = [pltpu.make_async_copy(a, b, sems.at[i]) for i, (a, b) in enumerate(pairs)]
    for copy in copies:
        copy.start()
    return copies


def shape(dims, dtype=BF16):
    return jax.ShapeDtypeStruct(dims, dtype)


TOKEN = shape((8, LANES), F32)


def window(head):
    low = head * DH // LANES * LANES
    high = -(-(head + 1) * DH // LANES) * LANES
    return low, high


def head_only(block, head):
    low, high = window(head)
    lane = lax.broadcasted_iota(jnp.int32, (1, high - low), 1) + low
    keep = (lane >= head * DH) & (lane < (head + 1) * DH)
    return jnp.where(keep, block, jnp.zeros_like(block))


def add_tiles(tiles, head, value):
    low, high = window(head)
    for at in range(low // LANES, high // LANES):
        part = value[:, at * LANES - low : (at + 1) * LANES - low]
        tiles[at] = part if tiles[at] is None else tiles[at] + part


def joined(tiles):
    return jnp.concatenate([tile.astype(BF16) for tile in tiles], axis=1)


def same_group(rows, kind):
    row = lax.broadcasted_iota(jnp.int32, (rows, rows), 0)
    col = lax.broadcasted_iota(jnp.int32, (rows, rows), 1)
    how, size = kind
    return row // size == col // size if how == "block" else row % size == col % size


def softmax_forward(q_ref, k_ref, v_ref, p_ref, heads, kind):
    rows = q_ref.shape[0]
    mask = same_group(rows, kind)
    tiles = [None] * (q_ref.shape[1] // LANES)
    for head in range(heads):
        low, high = window(head)
        s = dot_bt(q_ref[:, low:high], head_only(k_ref[:, low:high], head)) * (1.0 / math.sqrt(DH))
        s = jnp.where(mask, s, -jnp.inf)
        e = jnp.exp(s - jnp.max(s, axis=1, keepdims=True))
        p = e / jnp.sum(e, axis=1, keepdims=True)
        p_ref[head] = p
        add_tiles(tiles, head, dot(p.astype(BF16), head_only(v_ref[:, low:high], head)))
    return joined(tiles)


def softmax_backward(q_ref, k_ref, v_ref, g_ref, p_ref, heads):
    count = q_ref.shape[1] // LANES
    dq, dk, dv = [None] * count, [None] * count, [None] * count
    for head in range(heads):
        low, high = window(head)
        p = p_ref[head]
        g = head_only(g_ref[:, low:high], head)
        add_tiles(dv, head, dot_at(p.astype(BF16), g))
        dp = dot_bt(g, v_ref[:, low:high])
        ds = p * (dp - jnp.sum(p * dp, axis=1, keepdims=True)) * (1.0 / math.sqrt(DH))
        ds = ds.astype(BF16)
        add_tiles(dq, head, dot(ds, head_only(k_ref[:, low:high], head)))
        add_tiles(dk, head, dot_at(ds, head_only(q_ref[:, low:high], head)))
    return joined(dq), joined(dk), joined(dv)


def put(ref, value):
    width = value.shape[1]
    ref[:, width // LANES * LANES :] = jnp.zeros(
        (ref.shape[0], ref.shape[1] - width // LANES * LANES), ref.dtype
    )
    ref[:, :width] = value


def spatial_kernel(chips, patches, idx, *refs):
    far, outs, refs = refs[:4], refs[4 : 4 + chips], refs[4 + chips :]
    hid_far, p_far, done, tok, cot, qkv, wos, held, hid, p_ref, qs, ks, vs, sems = refs
    done[...] = jnp.zeros_like(done)
    inner, width = wos.shape
    count, block, _ = held.shape
    loads = started(zip(far, (qkv, tok, wos, cot)), sems)
    loads[0].wait()
    x = qkv[...]
    put(qs, x[:, :inner])
    put(ks, x[:, inner : 2 * inner])
    put(vs, x[:, 2 * inner :])
    o = softmax_forward(qs, ks, vs, p_ref, inner // DH, ("block", patches))[:, :inner]
    stores = started([(p_ref, p_far)], sems.at[pl.ds(4, 1)])
    for at in range(3):
        loads[1 + at].wait()
    hid[...] = (tok[...].astype(F32) + dot(o, wos[...])).astype(BF16)
    for at in range(count):
        rows = slice(at * block, (at + 1) * block)
        held[at, :, :width] = hid[rows]
        held[at, :, width : 2 * width] = cot[rows]
        held[at, :, 2 * width :] = o[rows]
    pairs = [(hid, hid_far)]
    for q in range(chips):
        for f in range(count // chips):
            rows = pl.ds(f * block, block)
            pairs.append((held.at[f * chips + (idx[2] ^ q)], outs[q].at[rows]))
    stores += started(pairs, sems.at[pl.ds(5, len(pairs))])
    for copy in stores:
        copy.wait()


def own_patches(refs, core, block):
    value = jnp.concatenate([ref[...] for ref in refs], axis=0)
    rows, width = value.shape
    value = value.astype(F32).reshape(rows // block, block, width)
    value = jnp.where(core == 0, value[:, : block // 2], value[:, block // 2 :])
    return value.reshape(rows // 2, width)


def all_patches(mine, other, core, block):
    rows, width = mine.shape
    mine = mine.astype(F32).reshape(2 * rows // block, block // 2, width)
    other = other.astype(F32).reshape(2 * rows // block, block // 2, width)
    first, second = jnp.where(core == 0, mine, other), jnp.where(core == 0, other, mine)
    return jnp.concatenate([first, second], axis=1).reshape(2 * rows, width).astype(BF16)


def split_kernel(near_x, near_y, _, from_x, from_y):
    cut = from_y.shape[1]
    from_y[...] = near_y[:, :cut]
    from_x[...] = near_x[:, cut:]


def pieces(shards, weights):
    weights = list(weights)
    for place, count, parts in shards:
        low, held = 0, []
        for _ in range(parts):
            w = weights.pop(0)
            held.append((low, w))
            low += w.shape[1]
        yield place, count, held


def temporal_kernel(shards, total, chips, group, idx, *refs):
    near, far, wot, refs = refs[:chips], refs[chips : 2 * chips], refs[2 * chips], refs[2 * chips + 1 :]
    weights, (mine, cot, q, k, v, g, p_ref, blocks) = refs[:total], refs[total:]
    inner, width = wot.shape
    heads = inner // DH
    value = [own_patches(refs, idx[1], 2 * group) for refs in (near, far)]
    value = jnp.concatenate(value, axis=0).astype(BF16)
    hidden = value[:, :width]
    cot[...] = value[:, width : 2 * width]
    for place, count, held in pieces(shards, weights):
        block = None
        for low, w in held:
            value = dot_bt(hidden[:, low : low + w.shape[1]], w[...])
            block = value if block is None else block + value
        block = block.astype(BF16)
        size = block.shape[1] // count
        for i in range(count):
            blocks[place(idx) + i] = block[:, i * size : (i + 1) * size]
    whole = jnp.concatenate([blocks[i] for i in range(blocks.shape[0])], axis=1)
    put(q, whole[:, :inner])
    put(k, whole[:, inner : 2 * inner])
    put(v, whole[:, 2 * inner :])
    mine[:, width:] = softmax_forward(q, k, v, p_ref, heads, ("cycle", group))[:, :inner]
    put(g, dot_bt(cot[...], wot[...]).astype(BF16))
    dq, dk, dv = softmax_backward(q, k, v, g, p_ref, heads)
    whole = jnp.concatenate([dq[:, :inner], dk[:, :inner], dv[:, :inner]], axis=1)
    size = blocks.shape[2]
    for i in range(blocks.shape[0]):
        blocks[i] = whole[:, i * size : (i + 1) * size]
    grad = jnp.zeros(cot.shape, F32)
    for place, count, held in pieces(shards, weights):
        lhs = jnp.concatenate([blocks[place(idx) + i] for i in range(count)], axis=1)
        grad += jnp.concatenate([dot(lhs, w[...]) for _, w in held], axis=1)
    mine[:, :width] = (cot[...].astype(F32) + grad.astype(BF16).astype(F32)).astype(BF16)


def whole_return_kernel(chips, block, inner, width, idx, mine, other, *refs):
    held, outs, part = refs[:chips], refs[chips : 2 * chips], refs[2 * chips]
    held = jnp.concatenate([ref[...] for ref in held], axis=0)
    cot, so = held[:, width : 2 * width], held[:, 2 * width :]
    half = mine.shape[0] // 2
    near = all_patches(mine[:half], other[half:], idx[1], block)
    for q, out in enumerate(outs):
        out[...] = near[q * out.shape[0] : (q + 1) * out.shape[0]]
    part[0] = dot_at(near[:, width:], cot).astype(BF16)
    part[1] = dot_at(so, near[:, :width]).astype(BF16)


def return_kernel(chips, block, inner, width, idx, mine, other, *refs):
    sent, refs = (refs[:chips], refs[chips : 2 * chips]), refs[2 * chips :]
    sent = [jnp.concatenate([ref[...] for ref in parts], axis=0) for parts in sent]
    outs, (keep, send_x, send_y, heads, cols) = refs[:chips], refs[chips:]
    half = mine.shape[0] // 2
    near = all_patches(mine[:half], other[half:], idx[1], block)
    for q, out in enumerate(outs):
        out[...] = near[q * out.shape[0] : (q + 1) * out.shape[0]]
    far = all_patches(mine[half:], other[:half], idx[1], block)
    rows = near.shape[0]
    size = heads.shape[2]
    count, _, wide = cols.shape
    for i in range(2):
        if i == 0:
            lefts = [near[:, width:], far[:, width:]]
            rights = [part[:, width : 2 * width] for part in sent]
        else:
            lefts = [part[:, 2 * width :] for part in sent]
            rights = [near[:, :width], far[:, :width]]
        for at in range(2):
            held = slice(at * rows, (at + 1) * rows)
            for h in range(heads.shape[0]):
                heads[h, held] = lefts[at][:, h * size : (h + 1) * size]
            for r in range(count):
                cols[r, held] = rights[at][:, r * wide : (r + 1) * wide]
        left = jnp.concatenate([heads[idx[3] ^ (2 * q)] for q in range(chips)], axis=1)
        first = 1 if i == 0 else 2
        for r in range(count):
            full = dot_at(left, cols[idx[0] ^ r])
            value = jnp.concatenate([full[q * size : (q + 1) * size] for q in range(chips)], axis=1)
            if r & first:
                (send_x, send_y)[i][r // 2 if i == 0 else r - 2] = value.astype(BF16)
            else:
                keep[2 * i + (r > 0)] = value


def sum_first_kernel(keep, got_x, got_y, own, send_y, send_x):
    for i, (got, send) in enumerate(((got_x, send_y), (got_y, send_x))):
        own[i] = keep[2 * i] + got[0].astype(F32)
        send[...] = (keep[2 * i + 1] + got[1].astype(F32)).astype(BF16)


def sum_second_kernel(own, got_y, got_x, kept, *outs):
    totals = [own[0] + got_y[...].astype(F32), own[1] + got_x[...].astype(F32)]
    size = totals[0].shape[1] // (1 + len(outs))
    for q, out in enumerate((kept, *outs)):
        cut = [total[:, q * size : (q + 1) * size] for total in totals]
        out[...] = jnp.concatenate(cut, axis=1).astype(out.dtype)


def sum_kernel(own, *refs):
    got, outs = refs[:-2], refs[-2:]
    total = own[...]
    for part in got:
        total += part[...].astype(F32)
    size = outs[0].shape[1]
    for i, out in enumerate(outs):
        out[...] = total[:, i * size : (i + 1) * size]


def last_kernel(chips, patches, idx, *refs):
    loaded = 5 + chips
    far, (block_far, out_far, grads_far), refs = refs[:loaded], refs[loaded : loaded + 3], refs[loaded + 3 :]
    rows, wos, qkv, p_ref, wot, hid, block_out, grads, qs, ks, vs, gs, sems = refs
    inner, width = wos.shape
    frames = rows.shape[0] // patches
    block = patches // chips
    pairs = list(zip(far[chips:], (wos, qkv, p_ref, wot, hid)))
    for q in range(chips):
        for f in range(frames):
            low = pl.multiple_of(f * patches + (idx[2] ^ q) * block, block)
            pairs.append((far[q].at[pl.ds(f * block, block)], rows.at[pl.ds(low, block)]))
    loads = started(pairs, sems)
    for copy in loads[5:]:
        copy.wait()
    value = rows[...]
    grad, attended = value[:, :width], value[:, width:]
    base = len(pairs)
    stores = started([(rows.at[:, pl.ds(0, width)], out_far)], sems.at[pl.ds(base, 1)])
    loads[0].wait()
    put(gs, dot_bt(grad, wos[...]).astype(BF16))
    loads[1].wait()
    x = qkv[...]
    put(qs, x[:, :inner])
    put(ks, x[:, inner : 2 * inner])
    put(vs, x[:, 2 * inner :])
    loads[3].wait()
    loads[4].wait()
    block_out[...] = (hid[...].astype(F32) + dot(attended, wot[...])).astype(BF16)
    stores += started([(block_out, block_far)], sems.at[pl.ds(base + 1, 1)])
    loads[2].wait()
    dq, dk, dv = softmax_backward(qs, ks, vs, gs, p_ref, inner // DH)
    grads[...] = jnp.concatenate([dq[:, :inner], dk[:, :inner], dv[:, :inner]], axis=1)
    stores += started([(grads, grads_far)], sems.at[pl.ds(base + 2, 1)])
    for copy in stores:
        copy.wait()


def flip(value, axis, bit):
    return lax.ppermute(value, axis, [(i, i ^ bit) for i in range(lax.axis_size(axis))])


def sems(n):
    return pltpu.SemaphoreType.DMA((n,))


def gather_weight(weight, core, after):
    n = lax.axis_size("dp")
    if n != 4:
        return [lax.all_gather(weight, "dp", axis=0, tiled=True)], [(lambda idx: 0, 1, 1)], 1
    half, width = weight.shape[0] // 2, weight.shape[1]
    mine = lax.dynamic_slice_in_dim(weight, core * half, half, 0)
    near = [flip(mine, "dp", 1), flip(mine, "dp", 2)]
    cut = width // LANES // 2 * LANES
    from_x, from_y = call(
        split_kernel,
        [shape((half, width - cut)), shape((half, cut))],
        [*near, after],
        small=True,
    )
    corner = [flip(from_y, "dp", 1), flip(from_x, "dp", 2)]
    held = near + corner
    far = [flip(w, "seq", 1) for w in held]
    shards = [(lambda idx: 2 * idx[0], 2, 1)]
    for flipped in range(2):
        for j in range(1, n):
            shards.append(
                (
                    lambda idx, j=j, flipped=flipped: 2 * (idx[0] ^ j) + (idx[1] ^ flipped),
                    1,
                    1 if j < 3 else 2,
                )
            )
    return [weight, *held, *far], shards, 2 * n


def from_chips(parts):
    return [parts[0]] + [flip(parts[q], "seq", 2 * q) for q in range(1, len(parts))]


def reduced(keep, send_x, send_y):
    _, size, width = keep.shape
    step = shape((size, width))
    own, send_t, send_s = call(
        sum_first_kernel,
        [shape((2, size, width), F32), step, step],
        [keep, flip(send_x, "dp", 1), flip(send_y, "dp", 2)],
        small=True,
    )
    n = lax.axis_size("seq") // 2
    block = (size, 2 * width // n)
    own, *sends = call(
        sum_second_kernel,
        [shape(block, F32)] + [shape(block)] * (n - 1),
        [own, flip(send_t, "dp", 2), flip(send_s, "dp", 1)],
        small=True,
    )
    got = [flip(value, "seq", 2 * (q + 1)) for q, value in enumerate(sends)]
    return call(sum_kernel, [shape((size, width // n), F32)] * 2, [own, *got], small=True)


def shards(tokens, spatial_qkv, wo_spatial, w_temporal, wo_temporal, cotangent):
    frames, patches, width = tokens.shape
    inner = wo_spatial.shape[0]
    heads = inner // DH
    padded = -(-inner // LANES) * LANES
    rows = frames * patches
    peers = FRAMES // frames
    chips = peers // 2
    group = patches // peers
    block = 2 * group
    n_dp, n_seq = lax.axis_size("dp"), lax.axis_size("seq")
    seq = lax.axis_index("seq")
    idx = jnp.stack([lax.axis_index("dp"), seq % 2, seq % peers // 2, seq]).astype(jnp.int32)

    def held(columns, dtype=BF16):
        return pltpu.VMEM((rows, columns), dtype)

    wide = held(padded)
    attended = pltpu.VMEM((heads, rows, rows), F32)
    projection = pltpu.VMEM((inner, width), BF16)
    per_chip = rows // chips
    qkv_rows = spatial_qkv.reshape(rows, 3 * inner)
    sent = 2 * width + inner
    *near, hidden, spatial_p, done = call(
        functools.partial(spatial_kernel, chips, patches),
        [shape((per_chip, sent))] * chips
        + [shape((rows, width)), shape((heads, rows, rows), F32), TOKEN],
        [idx, qkv_rows, tokens.reshape(rows, width), wo_spatial, cotangent.reshape(rows, width)],
        [held(width), held(width), held(3 * inner), projection]
        + [pltpu.VMEM((frames * chips, block, sent), BF16), held(width), attended]
        + [wide] * 3
        + [sems(6 + chips * frames)],
        us=4,
        far_in=range(1, 5),
        far_out=range(chips + 2),
    )
    weights, places, count = gather_weight(w_temporal.T, seq % 2, done)
    near = from_chips(near)
    far = [flip(value, "seq", 1) for value in near]
    blocks = pltpu.VMEM((count, rows, 3 * inner // count), BF16)
    (mine,) = call(
        functools.partial(temporal_kernel, places, len(weights), chips, group),
        [shape((rows, width + inner))],
        [idx, *near, *far, wo_temporal, *weights],
        [held(width)] + [wide] * 4 + [attended, blocks],
        us=10,
        small=True,
    )
    other = flip(mine, "seq", 1)
    back = [shape((per_chip, width + inner))] * chips
    if n_dp == 4 and n_seq == peers:
        size = inner // n_seq
        *back, keep, send_x, send_y = call(
            functools.partial(return_kernel, chips, block, inner, width),
            back
            + [shape((n_dp, size, width), F32)]
            + [shape((2, size, width))] * 2,
            [idx, mine, other, *near, *far],
            [
                pltpu.VMEM((n_seq, 2 * rows, size), BF16),
                pltpu.VMEM((n_dp, 2 * rows, width // n_dp), BF16),
            ],
            us=0,
            small=True,
        )
        temporal_grad, spatial_grad = reduced(keep, send_x, send_y)
    else:
        *back, both = call(
            functools.partial(whole_return_kernel, chips, block, inner, width),
            back + [shape((2, inner, width))],
            [idx, mine, other, *near],
            us=0,
            small=True,
        )
        both = lax.psum_scatter(both, "seq", scatter_dimension=1, tiled=True)
        both = lax.psum_scatter(both, "dp", scatter_dimension=2, tiled=True).astype(F32)
        temporal_grad, spatial_grad = both[0], both[1]
    block_out, tokens_grad, qkv_grad = call(
        functools.partial(last_kernel, chips, patches),
        [shape((rows, width)), shape((rows, width)), shape((rows, 3 * inner))],
        [idx, *from_chips(back), wo_spatial, qkv_rows, spatial_p, wo_temporal, hidden],
        [held(width + inner), projection, held(3 * inner), attended, projection, held(width)]
        + [held(width), held(3 * inner)]
        + [wide] * 4
        + [sems(8 + chips * frames)],
        us=6,
        far_in=range(1, 6 + chips),
        far_out=range(3),
    )
    return (
        block_out.reshape(frames, patches, width),
        tokens_grad.reshape(frames, patches, width),
        qkv_grad.reshape(frames, patches, 3 * inner),
        spatial_grad,
        temporal_grad,
    )


def solution(mesh):
    placed = (
        P(("dp", "seq"), None, None),
        P(("dp", "seq"), None, None),
        P(),
        P(None, "dp"),
        P(),
        P(("dp", "seq"), None, None),
    )
    return jax.shard_map(
        shards,
        mesh=mesh,
        in_specs=placed,
        out_specs=(
            P(("dp", "seq"), None, None),
            P(("dp", "seq"), None, None),
            P(("dp", "seq"), None, None),
            P("seq", "dp"),
            P("seq", "dp"),
        ),
        check_vma=False,
    )
```

```python
import functools
import math

import jax
import jax.numpy as jnp
from jax import lax
from jax.experimental import pallas as pl
from jax.experimental.pallas import tpu as pltpu
from jax.sharding import PartitionSpec as P

DH = 72
FRAMES = 16
LANES = 128
BF16 = jnp.bfloat16
F32 = jnp.float32
VMEM = pl.BlockSpec(memory_space=pltpu.VMEM)
SMEM = pl.BlockSpec(memory_space=pltpu.SMEM)
HBM = pl.BlockSpec(memory_space=pltpu.HBM)
LIMIT = 16 * 1024 * 1024
MOST = 60 * 1024 * 1024


def dot(left, right):
    return jnp.dot(left, right, preferred_element_type=F32)


def dot_bt(left, right):
    return lax.dot_general(left, right, (((1,), (1,)), ((), ())), preferred_element_type=F32)


def dot_at(left, right):
    return lax.dot_general(left, right, (((0,), (0,)), ((), ())), preferred_element_type=F32)


def call(body, outs, args, scratch=(), us=0, far_in=(), far_out=(), small=False):
    moved = sum(math.prod(a.shape) * a.dtype.itemsize for a in (*args, *outs))
    near = [SMEM if a.dtype == jnp.int32 else VMEM for a in args]
    return pl.pallas_call(
        body,
        out_shape=outs,
        in_specs=[HBM if i in far_in else spec for i, spec in enumerate(near)],
        out_specs=[
            HBM if i in far_out else SMEM if out.dtype == jnp.int32 else VMEM
            for i, out in enumerate(outs)
        ],
        scratch_shapes=list(scratch),
        compiler_params=pltpu.CompilerParams(vmem_limit_bytes=LIMIT if small else MOST),
        cost_estimate=pl.CostEstimate(
            flops=us * 1150000000, bytes_accessed=moved if us else 0, transcendentals=0
        ),
    )(*args)


def started(pairs, sems):
    copies = [pltpu.make_async_copy(a, b, sems.at[i]) for i, (a, b) in enumerate(pairs)]
    for copy in copies:
        copy.start()
    return copies


def shape(dims, dtype=BF16):
    return jax.ShapeDtypeStruct(dims, dtype)


TOKEN = shape((1,), jnp.int32)


def window(head):
    low = head * DH // LANES * LANES
    high = -(-(head + 1) * DH // LANES) * LANES
    return low, high


def head_only(block, head):
    low, high = window(head)
    lane = lax.broadcasted_iota(jnp.int32, (1, high - low), 1) + low
    keep = (lane >= head * DH) & (lane < (head + 1) * DH)
    return jnp.where(keep, block, jnp.zeros_like(block))


def add_tiles(tiles, head, value):
    low, high = window(head)
    for at in range(low // LANES, high // LANES):
        part = value[:, at * LANES - low : (at + 1) * LANES - low]
        tiles[at] = part if tiles[at] is None else tiles[at] + part


def joined(tiles):
    return jnp.concatenate([tile.astype(BF16) for tile in tiles], axis=1)


def same_group(rows, kind):
    row = lax.broadcasted_iota(jnp.int32, (rows, rows), 0)
    col = lax.broadcasted_iota(jnp.int32, (rows, rows), 1)
    how, size = kind
    return row // size == col // size if how == "block" else row % size == col % size


def softmax_forward(q_ref, k_ref, v_ref, p_ref, heads, kind):
    rows = q_ref.shape[0]
    mask = same_group(rows, kind)
    tiles = [None] * (q_ref.shape[1] // LANES)
    for head in range(heads):
        low, high = window(head)
        s = dot_bt(q_ref[:, low:high], head_only(k_ref[:, low:high], head)) * (1.0 / math.sqrt(DH))
        s = jnp.where(mask, s, -jnp.inf)
        e = jnp.exp(s - jnp.max(s, axis=1, keepdims=True))
        p = e / jnp.sum(e, axis=1, keepdims=True)
        p_ref[head] = p
        add_tiles(tiles, head, dot(p.astype(BF16), head_only(v_ref[:, low:high], head)))
    return joined(tiles)


def softmax_backward(q_ref, k_ref, v_ref, g_ref, p_ref, heads):
    count = q_ref.shape[1] // LANES
    dq, dk, dv = [None] * count, [None] * count, [None] * count
    for head in range(heads):
        low, high = window(head)
        p = p_ref[head]
        g = head_only(g_ref[:, low:high], head)
        add_tiles(dv, head, dot_at(p.astype(BF16), g))
        dp = dot_bt(g, v_ref[:, low:high])
        ds = p * (dp - jnp.sum(p * dp, axis=1, keepdims=True)) * (1.0 / math.sqrt(DH))
        ds = ds.astype(BF16)
        add_tiles(dq, head, dot(ds, head_only(k_ref[:, low:high], head)))
        add_tiles(dk, head, dot_at(ds, head_only(q_ref[:, low:high], head)))
    return joined(dq), joined(dk), joined(dv)


def put(ref, value):
    width = value.shape[1]
    ref[:, width // LANES * LANES :] = jnp.zeros(
        (ref.shape[0], ref.shape[1] - width // LANES * LANES), ref.dtype
    )
    ref[:, :width] = value


def place(chips):
    seq = lax.axis_index("seq")
    return lax.axis_index("dp"), seq % 2, seq % (2 * chips) // 2, seq


def spatial_kernel(chips, patches, *refs):
    idx = place(chips)
    far, outs, refs = refs[:4], refs[4 : 4 + chips], refs[4 + chips :]
    hid_far, p_far, tok, cot, qkv, wos, held, hid, p_ref, qs, ks, vs, sems = refs
    inner, width = wos.shape
    count, block, _ = held.shape
    loads = started(zip(far, (qkv, tok, wos, cot)), sems)
    loads[0].wait()
    x = qkv[...]
    put(qs, x[:, :inner])
    put(ks, x[:, inner : 2 * inner])
    put(vs, x[:, 2 * inner :])
    o = softmax_forward(qs, ks, vs, p_ref, inner // DH, ("block", patches))[:, :inner]
    stores = started([(p_ref, p_far)], sems.at[pl.ds(4, 1)])
    for at in range(3):
        loads[1 + at].wait()
    hid[...] = (tok[...].astype(F32) + dot(o, wos[...])).astype(BF16)
    for at in range(count):
        rows = slice(at * block, (at + 1) * block)
        held[at, :, :width] = hid[rows]
        held[at, :, width : 2 * width] = cot[rows]
        held[at, :, 2 * width : 2 * width + inner] = o[rows]
    stores += started([(hid, hid_far)], sems.at[pl.ds(5, 1)])
    for q in range(chips):
        for f in range(count // chips):
            rows = slice(f * block, (f + 1) * block)
            outs[q][rows] = held[f * chips + (idx[2] ^ q)]
    for copy in stores:
        copy.wait()


def own_patches(ref, core, block):
    rows, width = ref.shape
    value = ref[...].astype(F32).reshape(rows // block, block, width)
    value = jnp.where(core == 0, value[:, : block // 2], value[:, block // 2 :])
    return value.reshape(rows // 2, width)


def all_patches(mine, other, core, block):
    rows, width = mine.shape
    mine = mine.astype(F32).reshape(2 * rows // block, block // 2, width)
    other = other.astype(F32).reshape(2 * rows // block, block // 2, width)
    first, second = jnp.where(core == 0, mine, other), jnp.where(core == 0, other, mine)
    return jnp.concatenate([first, second], axis=1).reshape(2 * rows, width).astype(BF16)


def cut_kernel(chips, whole, out, left, right, sem):
    copy = pltpu.make_async_copy(whole.at[place(chips)[1]], out, sem.at[0])
    copy.start()
    copy.wait()
    cut = left.shape[1]
    left[...] = out[:, :cut]
    right[...] = out[:, cut:]


def second_kernel(mine, got_x, got_y, own, left, right, kept):
    half, cut = got_x.shape
    left[:half] = mine[:, :cut]
    left[half:] = got_x[...]
    right[:half] = mine[:, cut:]
    right[half:] = got_y[...]
    kept[...] = own[...]


def join_rows_kernel(*refs):
    out, rows = refs[-1], refs[0].shape[0]
    for at, ref in enumerate(refs[:-1]):
        out[at * rows : (at + 1) * rows] = ref[...]


def projected(hidden, shards, weights, idx, blocks, sums):
    size = blocks.shape[2]
    sums[...] = jnp.zeros_like(sums)
    for held, w in zip(shards, weights):
        low = held[0][1]
        value = dot_bt(hidden[:, low : low + w.shape[1]], w[...])
        for at, _, i in held:
            sums[at(idx)] += value if i is None else value[:, i * size : (i + 1) * size]
    blocks[...] = sums[...].astype(BF16)


def projected_back(blocks, shards, weights, idx, total):
    total[...] = jnp.zeros_like(total)
    for held, w in zip(shards, weights):
        low = held[0][1]
        lhs = jnp.concatenate([blocks[at(idx)] for at, _, _ in held], axis=1)
        total[:, low : low + w.shape[1]] += dot(lhs, w[...])


def temporal_kernel(shards, chips, group, near, far, wot, *refs):
    idx = place(chips)
    weights, refs = refs[: len(shards)], refs[len(shards) :]
    mine, cot, q, k, v, g, p_ref, blocks, sums, total = refs
    inner, width = wot.shape
    heads = inner // DH
    value = [own_patches(ref, idx[1], 2 * group) for ref in (near, far)]
    value = jnp.concatenate(value, axis=0).astype(BF16)
    hidden = value[:, :width]
    cot[...] = value[:, width : 2 * width]
    size = blocks.shape[2]
    projected(hidden, shards, weights, idx, blocks, sums)
    whole = jnp.concatenate([blocks[i] for i in range(blocks.shape[0])], axis=1)
    put(q, whole[:, :inner])
    put(k, whole[:, inner : 2 * inner])
    put(v, whole[:, 2 * inner :])
    mine[:, width:] = softmax_forward(q, k, v, p_ref, heads, ("cycle", group))[:, :inner]
    put(g, dot_bt(cot[...], wot[...]).astype(BF16))
    dq, dk, dv = softmax_backward(q, k, v, g, p_ref, heads)
    whole = jnp.concatenate([dq[:, :inner], dk[:, :inner], dv[:, :inner]], axis=1)
    for i in range(blocks.shape[0]):
        blocks[i] = whole[:, i * size : (i + 1) * size]
    projected_back(blocks, shards, weights, idx, total)
    grad = total[...]
    mine[:, :width] = (cot[...].astype(F32) + grad.astype(BF16).astype(F32)).astype(BF16)


def whole_return_kernel(chips, block, inner, width, mine, other, *refs):
    idx = place(chips)
    held, outs, part = refs[0], refs[1 : 1 + chips], refs[1 + chips]
    cot, so = held[:, width : 2 * width], held[:, 2 * width : 2 * width + inner]
    half = mine.shape[0] // 2
    near = all_patches(mine[:half], other[half:], idx[1], block)
    for q, out in enumerate(outs):
        out[...] = near[q * out.shape[0] : (q + 1) * out.shape[0]]
    part[0] = dot_at(near[:, width:], cot).astype(BF16)
    part[1] = dot_at(so, near[:, :width]).astype(BF16)


def return_kernel(chips, block, inner, width, mine, other, *refs):
    idx = place(chips)
    sent, refs = refs[:2], refs[2:]
    outs, (keep, send_x, send_y, heads, cols, kept, sem) = refs[:chips], refs[chips:]
    half = mine.shape[0] // 2
    near = all_patches(mine[:half], other[half:], idx[1], block)
    rows = kept.shape[0]
    kept[...] = near[:rows]
    copy = pltpu.make_async_copy(kept, outs[0], sem.at[0])
    copy.start()
    for q in range(1, chips):
        outs[q][...] = near[q * rows : (q + 1) * rows]
    far = all_patches(mine[half:], other[:half], idx[1], block)
    rows = near.shape[0]
    size = heads.shape[2]
    count, _, wide = cols.shape
    for i in range(2):
        if i == 0:
            lefts = [near[:, width:], far[:, width:]]
            rights = [part[:, width : 2 * width] for part in sent]
        else:
            lefts = [part[:, 2 * width : 2 * width + inner] for part in sent]
            rights = [near[:, :width], far[:, :width]]
        for at in range(2):
            held = slice(at * rows, (at + 1) * rows)
            for h in range(heads.shape[0]):
                heads[h, held] = lefts[at][:, h * size : (h + 1) * size]
            for r in range(count):
                cols[r, held] = rights[at][:, r * wide : (r + 1) * wide]
        left = jnp.concatenate([heads[idx[3] ^ (2 * q)] for q in range(chips)], axis=1)
        first = 1 if i == 0 else 2
        for r in range(count):
            full = dot_at(left, cols[idx[0] ^ r])
            value = jnp.concatenate([full[q * size : (q + 1) * size] for q in range(chips)], axis=1)
            if r & first:
                (send_x, send_y)[i][r // 2 if i == 0 else r - 2] = value.astype(BF16)
            else:
                keep[2 * i + (r > 0)] = value
    copy.wait()


def sum_first_kernel(_, keep, got_x, got_y, own, send_y, send_x):
    for i, (got, send) in enumerate(((got_x, send_y), (got_y, send_x))):
        own[i] = keep[2 * i] + got[0].astype(F32)
        send[...] = (keep[2 * i + 1] + got[1].astype(F32)).astype(BF16)


def sum_second_kernel(own, got_y, got_x, kept, *outs):
    totals = [own[0] + got_y[...].astype(F32), own[1] + got_x[...].astype(F32)]
    size = totals[0].shape[1] // (1 + len(outs))
    for q, out in enumerate((kept, *outs)):
        cut = [total[:, q * size : (q + 1) * size] for total in totals]
        out[...] = jnp.concatenate(cut, axis=1).astype(out.dtype)


def sum_kernel(own, *refs):
    got, outs = refs[:-2], refs[-2:]
    total = own[...]
    for part in got:
        total += part[...].astype(F32)
    size = outs[0].shape[1]
    for i, out in enumerate(outs):
        out[...] = total[:, i * size : (i + 1) * size]


def last_kernel(chips, patches, *refs):
    idx = place(chips)
    loaded = 5 + chips
    far, outs, refs = refs[:loaded], refs[loaded : loaded + 4], refs[loaded + 4 :]
    block_far, out_far, grads_far, done = outs
    done[0] = 0
    rows, wos, qkv, p_ref, wot, hid, block_out, grads, qs, ks, vs, gs, sems = refs
    inner, width = wos.shape
    frames = rows.shape[0] // patches
    block = patches // chips
    pairs = list(zip(far[chips:], (wos, qkv, p_ref, wot, hid)))
    for q in range(chips):
        for f in range(frames):
            low = pl.multiple_of(f * patches + (idx[2] ^ q) * block, block)
            pairs.append((far[q].at[pl.ds(f * block, block)], rows.at[pl.ds(low, block)]))
    loads = started(pairs, sems)
    for copy in loads[5:]:
        copy.wait()
    value = rows[...]
    grad, attended = value[:, :width], value[:, width:]
    base = len(pairs)
    stores = started([(rows.at[:, pl.ds(0, width)], out_far)], sems.at[pl.ds(base, 1)])
    loads[0].wait()
    put(gs, dot_bt(grad, wos[...]).astype(BF16))
    loads[1].wait()
    x = qkv[...]
    put(qs, x[:, :inner])
    put(ks, x[:, inner : 2 * inner])
    put(vs, x[:, 2 * inner :])
    loads[3].wait()
    loads[4].wait()
    block_out[...] = (hid[...].astype(F32) + dot(attended, wot[...])).astype(BF16)
    stores += started([(block_out, block_far)], sems.at[pl.ds(base + 1, 1)])
    loads[2].wait()
    dq, dk, dv = softmax_backward(qs, ks, vs, gs, p_ref, inner // DH)
    grads[...] = jnp.concatenate([dq[:, :inner], dk[:, :inner], dv[:, :inner]], axis=1)
    stores += started([(grads, grads_far)], sems.at[pl.ds(base + 2, 1)])
    for copy in stores:
        copy.wait()


def flip(value, axis, bit):
    return lax.ppermute(value, axis, [(i, i ^ bit) for i in range(lax.axis_size(axis))])


def sems(n):
    return pltpu.SemaphoreType.DMA((n,))


def gather(weight, parts, chips):
    n = lax.axis_size("dp")
    rows, sent = parts[0].shape
    whole = [shape((len(parts) * rows, sent))]
    if n != 4:
        (near,) = call(join_rows_kernel, whole, from_chips(parts), small=True)
        weights = [lax.all_gather(weight, "dp", axis=0, tiled=True)]
        return near, flip(near, "seq", 1), weights, [[(lambda idx: 0, 0, None)]], 1
    half, width = weight.shape[0] // 2, weight.shape[1]
    cut = -(-width // LANES // 2) * LANES
    mine, left, right = call(
        functools.partial(cut_kernel, chips),
        [shape((half, width)), shape((half, cut)), shape((half, width - cut))],
        [weight.reshape(2, half, width)],
        [sems(1)],
        far_in=range(1),
    )
    got_x, got_y = flip(left, "dp", 1), flip(right, "dp", 2)
    left, right, own = call(
        second_kernel,
        [shape((2 * half, cut)), shape((2 * half, width - cut)), shape((rows, sent))],
        [mine, got_x, got_y, parts[0]],
        small=True,
    )
    (near,) = call(join_rows_kernel, whole, [own, *from_chips(parts)[1:]], small=True)
    held = [got_x, got_y, flip(left, "dp", 2), flip(right, "dp", 1)]
    weights = [weight, *held, *[flip(w, "seq", 1) for w in held]]

    def block(j, other):
        return lambda idx: 2 * (idx[0] ^ j) + (idx[1] ^ other)

    shards = [[(lambda idx: 2 * idx[0], 0, 0), (lambda idx: 2 * idx[0] + 1, 0, 1)]]
    for other in (0, 1):
        shards += [[(block(1, other), 0, None)], [(block(2, other), cut, None)]]
        shards.append([(block(2, other), 0, 0), (block(3, other), 0, 1)])
        shards.append([(block(1, other), cut, 0), (block(3, other), cut, 1)])
    return near, flip(near, "seq", 1), weights, shards, 2 * n


def from_chips(parts):
    return [parts[0]] + [flip(parts[q], "seq", 2 * q) for q in range(1, len(parts))]


def reduced(keep, send_x, send_y, after):
    _, size, width = keep.shape
    step = shape((size, width))
    own, send_t, send_s = call(
        sum_first_kernel,
        [shape((2, size, width), F32), step, step],
        [after, keep, flip(send_x, "dp", 1), flip(send_y, "dp", 2)],
        small=True,
    )
    n = lax.axis_size("seq") // 2
    block = (size, 2 * width // n)
    own, *sends = call(
        sum_second_kernel,
        [shape(block, F32)] + [shape(block)] * (n - 1),
        [own, flip(send_t, "dp", 2), flip(send_s, "dp", 1)],
        small=True,
    )
    got = [flip(value, "seq", 2 * (q + 1)) for q, value in enumerate(sends)]
    return call(sum_kernel, [shape((size, width // n), F32)] * 2, [own, *got], small=True)


def shards(tokens, spatial_qkv, wo_spatial, w_temporal, wo_temporal, cotangent):
    frames, patches, width = tokens.shape
    inner = wo_spatial.shape[0]
    heads = inner // DH
    padded = -(-inner // LANES) * LANES
    rows = frames * patches
    peers = FRAMES // frames
    chips = peers // 2
    group = patches // peers
    block = 2 * group
    n_dp, n_seq = lax.axis_size("dp"), lax.axis_size("seq")

    def held(columns, dtype=BF16):
        return pltpu.VMEM((rows, columns), dtype)

    wide = held(padded)
    attended = pltpu.VMEM((heads, rows, rows), F32)
    projection = pltpu.VMEM((inner, width), BF16)
    per_chip = rows // chips
    qkv_rows = spatial_qkv.reshape(rows, 3 * inner)
    sent = -(-(2 * width + inner) // LANES) * LANES
    *near, hidden, spatial_p = call(
        functools.partial(spatial_kernel, chips, patches),
        [shape((per_chip, sent))] * chips
        + [shape((rows, width)), shape((heads, rows, rows), F32)],
        [qkv_rows, tokens.reshape(rows, width), wo_spatial, cotangent.reshape(rows, width)],
        [held(width), held(width), held(3 * inner), projection]
        + [pltpu.VMEM((frames * chips, block, sent), BF16), held(width), attended]
        + [wide] * 3
        + [sems(6)],
        far_in=range(4),
        far_out=(chips, chips + 1),
    )
    near, far, weights, places, count = gather(w_temporal.T, near, chips)

    def blocks(dtype):
        return pltpu.VMEM((count, rows, 3 * inner // count), dtype)

    (mine,) = call(
        functools.partial(temporal_kernel, places, chips, group),
        [shape((rows, width + inner))],
        [near, far, wo_temporal, *weights],
        [held(width)] + [wide] * 4 + [attended, blocks(BF16), blocks(F32), held(width, F32)],
        small=True,
    )
    other = flip(mine, "seq", 1)
    back = [shape((per_chip, width + inner))] * chips
    if n_dp == 4 and n_seq == peers:
        size = inner // n_seq
        *back, keep, send_x, send_y = call(
            functools.partial(return_kernel, chips, block, inner, width),
            back
            + [shape((n_dp, size, width), F32)]
            + [shape((2, size, width))] * 2,
            [mine, other, near, far],
            [
                pltpu.VMEM((n_seq, 2 * rows, size), BF16),
                pltpu.VMEM((n_dp, 2 * rows, width // n_dp), BF16),
                pltpu.VMEM((per_chip, width + inner), BF16),
                sems(1),
            ],
            far_out=range(1),
            small=True,
        )
    else:
        *back, both = call(
            functools.partial(whole_return_kernel, chips, block, inner, width),
            back + [shape((2, inner, width))],
            [mine, other, near],
            small=True,
        )
    block_out, tokens_grad, qkv_grad, done = call(
        functools.partial(last_kernel, chips, patches),
        [shape((rows, width)), shape((rows, width)), shape((rows, 3 * inner)), TOKEN],
        [*from_chips(back), wo_spatial, qkv_rows, spatial_p, wo_temporal, hidden],
        [held(width + inner), projection, held(3 * inner), attended, projection, held(width)]
        + [held(width), held(3 * inner)]
        + [wide] * 4
        + [sems(8 + chips * frames)],
        far_in=range(5 + chips),
        far_out=range(3),
    )
    if n_dp == 4 and n_seq == peers:
        temporal_grad, spatial_grad = reduced(keep, send_x, send_y, done)
    else:
        both = lax.psum_scatter(both, "seq", scatter_dimension=1, tiled=True)
        both = lax.psum_scatter(both, "dp", scatter_dimension=2, tiled=True).astype(F32)
        temporal_grad, spatial_grad = both[0], both[1]
    return (
        block_out.reshape(frames, patches, width),
        tokens_grad.reshape(frames, patches, width),
        qkv_grad.reshape(frames, patches, 3 * inner),
        spatial_grad,
        temporal_grad,
    )


def solution(mesh):
    placed = (
        P(("dp", "seq"), None, None),
        P(("dp", "seq"), None, None),
        P(),
        P(None, "dp"),
        P(),
        P(("dp", "seq"), None, None),
    )
    return jax.shard_map(
        shards,
        mesh=mesh,
        in_specs=placed,
        out_specs=(
            P(("dp", "seq"), None, None),
            P(("dp", "seq"), None, None),
            P(("dp", "seq"), None, None),
            P("seq", "dp"),
            P("seq", "dp"),
        ),
        check_vma=False,
    )
```

```python
import functools
import math

import jax
import jax.numpy as jnp
from jax import lax
from jax.experimental import pallas as pl
from jax.experimental.pallas import tpu as pltpu
from jax.sharding import PartitionSpec as P

DH = 72
FRAMES = 16
LANES = 128
BF16 = jnp.bfloat16
F32 = jnp.float32
VMEM = pl.BlockSpec(memory_space=pltpu.VMEM)
SMEM = pl.BlockSpec(memory_space=pltpu.SMEM)
HBM = pl.BlockSpec(memory_space=pltpu.HBM)
PAD = 8 * LANES
LIMIT = 16 * 1024 * 1024
MOST = 60 * 1024 * 1024


def dot(left, right):
    return jnp.dot(left, right, preferred_element_type=F32)


def dot_bt(left, right):
    return lax.dot_general(left, right, (((1,), (1,)), ((), ())), preferred_element_type=F32)


def dot_at(left, right):
    return lax.dot_general(left, right, (((0,), (0,)), ((), ())), preferred_element_type=F32)


def call(body, outs, args, scratch=(), us=0, far_in=(), far_out=(), small=False):
    moved = sum(math.prod(a.shape) * a.dtype.itemsize for a in (*args, *outs))
    near = [SMEM if a.dtype == jnp.int32 else VMEM for a in args]
    return pl.pallas_call(
        body,
        out_shape=outs,
        in_specs=[HBM if i in far_in else spec for i, spec in enumerate(near)],
        out_specs=[
            HBM if i in far_out else SMEM if out.dtype == jnp.int32 else VMEM
            for i, out in enumerate(outs)
        ],
        scratch_shapes=list(scratch),
        compiler_params=pltpu.CompilerParams(vmem_limit_bytes=LIMIT if small else MOST),
        cost_estimate=pl.CostEstimate(
            flops=us * 1150000000, bytes_accessed=moved if us else 0, transcendentals=0
        ),
    )(*args)


def started(pairs, sems):
    copies = [pltpu.make_async_copy(a, b, sems.at[i]) for i, (a, b) in enumerate(pairs)]
    for copy in copies:
        copy.start()
    return copies


def shape(dims, dtype=BF16):
    return jax.ShapeDtypeStruct(dims, dtype)


TOKEN = shape((1,), jnp.int32)


def window(head):
    low = head * DH // LANES * LANES
    high = -(-(head + 1) * DH // LANES) * LANES
    return low, high


def head_only(block, head):
    low, high = window(head)
    lane = lax.broadcasted_iota(jnp.int32, (1, high - low), 1) + low
    keep = (lane >= head * DH) & (lane < (head + 1) * DH)
    return jnp.where(keep, block, jnp.zeros_like(block))


def add_tiles(tiles, head, value):
    low, high = window(head)
    for at in range(low // LANES, high // LANES):
        part = value[:, at * LANES - low : (at + 1) * LANES - low]
        tiles[at] = part if tiles[at] is None else tiles[at] + part


def joined(tiles):
    return jnp.concatenate([tile.astype(BF16) for tile in tiles], axis=1)


def same_group(rows, kind):
    row = lax.broadcasted_iota(jnp.int32, (rows, rows), 0)
    col = lax.broadcasted_iota(jnp.int32, (rows, rows), 1)
    how, size = kind
    return row // size == col // size if how == "block" else row % size == col % size


def softmax_forward(q_ref, k_ref, v_ref, p_ref, heads, kind):
    rows = q_ref.shape[0]
    mask = same_group(rows, kind)
    tiles = [None] * (q_ref.shape[1] // LANES)
    for head in range(heads):
        low, high = window(head)
        s = dot_bt(q_ref[:, low:high], head_only(k_ref[:, low:high], head)) * (1.0 / math.sqrt(DH))
        s = jnp.where(mask, s, -jnp.inf)
        e = jnp.exp(s - jnp.max(s, axis=1, keepdims=True))
        p = e / jnp.sum(e, axis=1, keepdims=True)
        p_ref[head] = p
        add_tiles(tiles, head, dot(p.astype(BF16), head_only(v_ref[:, low:high], head)))
    return joined(tiles)


def softmax_backward(q_ref, k_ref, v_ref, g_ref, p_ref, heads):
    count = q_ref.shape[1] // LANES
    dq, dk, dv = [None] * count, [None] * count, [None] * count
    for head in range(heads):
        low, high = window(head)
        p = p_ref[head]
        g = head_only(g_ref[:, low:high], head)
        add_tiles(dv, head, dot_at(p.astype(BF16), g))
        dp = dot_bt(g, v_ref[:, low:high])
        ds = p * (dp - jnp.sum(p * dp, axis=1, keepdims=True)) * (1.0 / math.sqrt(DH))
        ds = ds.astype(BF16)
        add_tiles(dq, head, dot(ds, head_only(k_ref[:, low:high], head)))
        add_tiles(dk, head, dot_at(ds, head_only(q_ref[:, low:high], head)))
    return joined(dq), joined(dk), joined(dv)


def put(ref, value):
    width = value.shape[1]
    ref[:, width // LANES * LANES :] = jnp.zeros(
        (ref.shape[0], ref.shape[1] - width // LANES * LANES), ref.dtype
    )
    ref[:, :width] = value


def place(chips):
    seq = lax.axis_index("seq")
    return lax.axis_index("dp"), seq % 2, seq % (2 * chips) // 2, seq


def spatial_kernel(chips, patches, *refs):
    idx = place(chips)
    far, outs, refs = refs[:4], refs[4 : 4 + chips], refs[4 + chips :]
    hid_far, p_far, tok, cot, qkv, wos, held, hid, p_ref, qs, ks, vs, sems = refs
    inner, width = wos.shape
    count, block, _ = held.shape
    loads = started(zip(far, (qkv, tok, wos, cot)), sems)
    loads[0].wait()
    x = qkv[...]
    put(qs, x[:, :inner])
    put(ks, x[:, inner : 2 * inner])
    put(vs, x[:, 2 * inner :])
    o = softmax_forward(qs, ks, vs, p_ref, inner // DH, ("block", patches))[:, :inner]
    stores = started([(p_ref, p_far)], sems.at[pl.ds(4, 1)])
    for at in range(3):
        loads[1 + at].wait()
    hid[...] = (tok[...].astype(F32) + dot(o, wos[...])).astype(BF16)
    for at in range(count):
        rows = slice(at * block, (at + 1) * block)
        held[at, :, :width] = hid[rows]
        held[at, :, width : 2 * width] = cot[rows]
        held[at, :, 2 * width : 2 * width + inner] = o[rows]
    stores += started([(hid, hid_far)], sems.at[pl.ds(5, 1)])
    for q in range(chips):
        for f in range(count // chips):
            rows = slice(f * block, (f + 1) * block)
            outs[q][rows] = held[f * chips + (idx[2] ^ q)]
    for copy in stores:
        copy.wait()


def own_patches(ref, core, block):
    rows, width = ref.shape
    value = ref[...].astype(F32).reshape(rows // block, block, width)
    value = jnp.where(core == 0, value[:, : block // 2], value[:, block // 2 :])
    return value.reshape(rows // 2, width)


def all_patches(mine, other, core, block):
    rows, width = mine.shape
    mine = mine.astype(F32).reshape(2 * rows // block, block // 2, width)
    other = other.astype(F32).reshape(2 * rows // block, block // 2, width)
    first, second = jnp.where(core == 0, mine, other), jnp.where(core == 0, other, mine)
    return jnp.concatenate([first, second], axis=1).reshape(2 * rows, width).astype(BF16)


def cut_kernel(chips, whole, left, right, sem):
    core, cut = place(chips)[1], left.shape[1]
    pairs = [(whole.at[core, :, pl.ds(0, cut)], left)]
    pairs.append((whole.at[core, :, pl.ds(cut, right.shape[1])], right))
    for copy in started(pairs, sem):
        copy.wait()


def second_kernel(own_left, own_right, got_x, got_y, own, left, right, kept):
    half = got_x.shape[0]
    left[:half] = own_left[...]
    left[half:] = got_x[...]
    right[:half] = own_right[...]
    right[half:] = got_y[...]
    kept[...] = own[...]


def join_rows_kernel(*refs):
    out, low = refs[-1], 0
    for ref in refs[:-1]:
        out[low : low + ref.shape[0], : ref.shape[1]] = ref[...]
        low += ref.shape[0]


def projected(hidden, shards, weights, idx, blocks, sums):
    size = blocks.shape[2]
    sums[...] = jnp.zeros_like(sums)
    for held, w in zip(shards, weights):
        low = held[0][1]
        value = dot_bt(hidden[:, low : low + w.shape[1]], w[...])
        for at, _, i in held:
            sums[at(idx)] += value if i is None else value[:, i * size : (i + 1) * size]
    blocks[...] = sums[...].astype(BF16)


def projected_back(blocks, shards, weights, idx, total):
    total[...] = jnp.zeros_like(total)
    for held, w in zip(shards, weights):
        low = held[0][1]
        lhs = jnp.concatenate([blocks[at(idx)] for at, _, _ in held], axis=1)
        total[:, low : low + w.shape[1]] += dot(lhs, w[...])


def temporal_kernel(shards, chips, group, near, far, wot, *refs):
    idx = place(chips)
    weights, refs = refs[: len(shards)], refs[len(shards) :]
    mine, cot, q, k, v, g, p_ref, blocks, sums, total = refs
    inner, width = wot.shape
    heads = inner // DH
    value = [own_patches(ref, idx[1], 2 * group) for ref in (near, far)]
    value = jnp.concatenate(value, axis=0).astype(BF16)
    hidden = value[:, :width]
    cot[...] = value[:, width : 2 * width]
    size = blocks.shape[2]
    projected(hidden, shards, weights, idx, blocks, sums)
    whole = jnp.concatenate([blocks[i] for i in range(blocks.shape[0])], axis=1)
    put(q, whole[:, :inner])
    put(k, whole[:, inner : 2 * inner])
    put(v, whole[:, 2 * inner :])
    mine[:, width:] = softmax_forward(q, k, v, p_ref, heads, ("cycle", group))[:, :inner]
    put(g, dot_bt(cot[...], wot[...]).astype(BF16))
    dq, dk, dv = softmax_backward(q, k, v, g, p_ref, heads)
    whole = jnp.concatenate([dq[:, :inner], dk[:, :inner], dv[:, :inner]], axis=1)
    for i in range(blocks.shape[0]):
        blocks[i] = whole[:, i * size : (i + 1) * size]
    projected_back(blocks, shards, weights, idx, total)
    grad = total[...]
    mine[:, :width] = (cot[...].astype(F32) + grad.astype(BF16).astype(F32)).astype(BF16)


def whole_return_kernel(chips, block, inner, width, mine, other, *refs):
    idx = place(chips)
    held, outs, part = refs[0], refs[1 : 1 + chips], refs[1 + chips]
    cot, so = held[:, width : 2 * width], held[:, 2 * width : 2 * width + inner]
    half = mine.shape[0] // 2
    near = all_patches(mine[:half], other[half:], idx[1], block)
    for q, out in enumerate(outs):
        out[...] = near[q * out.shape[0] : (q + 1) * out.shape[0]]
    part[0] = dot_at(near[:, width:], cot).astype(BF16)
    part[1] = dot_at(so, near[:, :width]).astype(BF16)


def return_kernel(chips, block, inner, width, mine, other, *refs):
    idx = place(chips)
    sent, refs = refs[:2], refs[2:]
    outs, (keep, send_x, send_y, heads, cols, kept, sem) = refs[:chips], refs[chips:]
    half = mine.shape[0] // 2
    near = all_patches(mine[:half], other[half:], idx[1], block)
    rows = kept.shape[0]
    kept[...] = near[:rows]
    copy = pltpu.make_async_copy(kept, outs[0], sem.at[0])
    copy.start()
    for q in range(1, chips):
        outs[q][...] = near[q * rows : (q + 1) * rows]
    far = all_patches(mine[half:], other[:half], idx[1], block)
    rows = near.shape[0]
    size = heads.shape[2]
    count, _, wide = cols.shape
    for i in range(2):
        if i == 0:
            lefts = [near[:, width:], far[:, width:]]
            rights = [part[:, width : 2 * width] for part in sent]
        else:
            lefts = [part[:, 2 * width : 2 * width + inner] for part in sent]
            rights = [near[:, :width], far[:, :width]]
        for at in range(2):
            held = slice(at * rows, (at + 1) * rows)
            for h in range(heads.shape[0]):
                heads[h, held] = lefts[at][:, h * size : (h + 1) * size]
            for r in range(count):
                cols[r, held] = rights[at][:, r * wide : (r + 1) * wide]
        left = jnp.concatenate([heads[idx[3] ^ (2 * q)] for q in range(chips)], axis=1)
        first = 1 if i == 0 else 2
        for r in range(count):
            full = dot_at(left, cols[idx[0] ^ r])
            value = jnp.concatenate([full[q * size : (q + 1) * size] for q in range(chips)], axis=1)
            if r & first:
                (send_x, send_y)[i][r // 2 if i == 0 else r - 2] = value.astype(BF16)
            else:
                keep[2 * i + (r > 0)] = value
    copy.wait()


def sum_first_kernel(keep, got_x, got_y, _, own, send_y, send_x):
    for i, (got, send) in enumerate(((got_x, send_y), (got_y, send_x))):
        own[i] = keep[2 * i] + got[0].astype(F32)
        send[...] = (keep[2 * i + 1] + got[1].astype(F32)).astype(BF16)


def sum_second_kernel(own, got_y, got_x, kept, *outs):
    totals = [own[0] + got_y[...].astype(F32), own[1] + got_x[...].astype(F32)]
    size = totals[0].shape[1] // (1 + len(outs))
    for q, out in enumerate((kept, *outs)):
        cut = [total[:, q * size : (q + 1) * size] for total in totals]
        out[...] = jnp.concatenate(cut, axis=1).astype(out.dtype)


def sum_kernel(own, *refs):
    got, outs = refs[:-2], refs[-2:]
    total = own[...]
    for part in got:
        total += part[...].astype(F32)
    size = outs[0].shape[1]
    for i, out in enumerate(outs):
        out[...] = total[:, i * size : (i + 1) * size]


def last_kernel(chips, patches, *refs):
    idx = place(chips)
    loaded = 5 + chips
    far, outs, refs = refs[:loaded], refs[loaded : loaded + 3], refs[loaded + 3 :]
    block_far, out_far, grads_far = outs
    rows, wos, qkv, p_ref, wot, hid, block_out, grads, qs, ks, vs, gs, sems = refs
    inner, width = wos.shape
    frames = rows.shape[0] // patches
    block = patches // chips
    pairs = []
    for q in range(chips):
        for f in range(frames):
            low = pl.multiple_of(f * patches + (idx[2] ^ q) * block, block)
            pairs.append((far[q].at[pl.ds(f * block, block)], rows.at[pl.ds(low, block)]))
    first = len(pairs)
    pairs += zip(far[chips:], (wos, qkv, p_ref, wot, hid))
    loads = started(pairs, sems)
    for copy in loads[:first]:
        copy.wait()
    value = rows[...]
    grad, attended = value[:, :width], value[:, width:]
    base = len(pairs)
    stores = started([(rows.at[:, pl.ds(0, width)], out_far)], sems.at[pl.ds(base, 1)])
    loads[first].wait()
    put(gs, dot_bt(grad, wos[...]).astype(BF16))
    loads[first + 1].wait()
    x = qkv[...]
    put(qs, x[:, :inner])
    put(ks, x[:, inner : 2 * inner])
    put(vs, x[:, 2 * inner :])
    loads[first + 2].wait()
    dq, dk, dv = softmax_backward(qs, ks, vs, gs, p_ref, inner // DH)
    grads[...] = jnp.concatenate([dq[:, :inner], dk[:, :inner], dv[:, :inner]], axis=1)
    stores += started([(grads, grads_far)], sems.at[pl.ds(base + 2, 1)])
    loads[first + 3].wait()
    loads[first + 4].wait()
    block_out[...] = (hid[...].astype(F32) + dot(attended, wot[...])).astype(BF16)
    stores += started([(block_out, block_far)], sems.at[pl.ds(base + 1, 1)])
    for copy in stores:
        copy.wait()


def flip(value, axis, bit):
    return lax.ppermute(value, axis, [(i, i ^ bit) for i in range(lax.axis_size(axis))])


def sems(n):
    return pltpu.SemaphoreType.DMA((n,))


def gather(weight, parts, chips):
    n = lax.axis_size("dp")
    rows, sent = parts[0].shape
    whole = [shape((len(parts) * rows, sent + PAD))]
    if n != 4:
        (near,) = call(join_rows_kernel, whole, from_chips(parts), small=True)
        weights = [lax.all_gather(weight, "dp", axis=0, tiled=True)]
        return near, flip(near, "seq", 1), weights, [[(lambda idx: 0, 0, None)]], 1
    half, width = weight.shape[0] // 2, weight.shape[1]
    cut = -(-width // LANES // 2) * LANES
    left, right = call(
        functools.partial(cut_kernel, chips),
        [shape((half, cut)), shape((half, width - cut))],
        [weight.reshape(2, half, width)],
        [sems(2)],
        far_in=range(1),
        far_out=range(2),
    )
    got_x, got_y = flip(left, "dp", 1), flip(right, "dp", 2)
    left, right, own = call(
        second_kernel,
        [shape((2 * half, cut)), shape((2 * half, width - cut)), shape((rows, sent))],
        [left, right, got_x, got_y, parts[0]],
        small=True,
    )
    (near,) = call(join_rows_kernel, whole, [own, *from_chips(parts)[1:]], small=True)
    (right,) = call(
        join_rows_kernel,
        [shape((3 * half, width - cut))],
        [got_y, flip(right, "dp", 1)],
        small=True,
    )
    held = [got_x, flip(left, "dp", 2), right]
    weights = [weight, *held, *[flip(w, "seq", 1) for w in held]]

    def block(j, other):
        return lambda idx: 2 * (idx[0] ^ j) + (idx[1] ^ other)

    shards = [[(lambda idx: 2 * idx[0], 0, 0), (lambda idx: 2 * idx[0] + 1, 0, 1)]]
    for other in (0, 1):
        shards += [[(block(1, other), 0, None)]]
        shards.append([(block(2, other), 0, 0), (block(3, other), 0, 1)])
        shards.append([(block(j, other), cut, i) for i, j in enumerate((2, 1, 3))])
    return near, flip(near, "seq", 1), weights, shards, 2 * n


def from_chips(parts):
    return [parts[0]] + [flip(parts[q], "seq", 2 * q) for q in range(1, len(parts))]


def reduced(keep, send_x, send_y, after):
    _, size, width = keep.shape
    step = shape((size, width))
    own, send_t, send_s = call(
        sum_first_kernel,
        [shape((2, size, width), F32), step, step],
        [keep, flip(send_x, "dp", 1), flip(send_y, "dp", 2), after],
        small=True,
    )
    n = lax.axis_size("seq") // 2
    block = (size, 2 * width // n)
    own, *sends = call(
        sum_second_kernel,
        [shape(block, F32)] + [shape(block)] * (n - 1),
        [own, flip(send_t, "dp", 2), flip(send_s, "dp", 1)],
        small=True,
    )
    got = [flip(value, "seq", 2 * (q + 1)) for q, value in enumerate(sends)]
    return call(sum_kernel, [shape((size, width // n), F32)] * 2, [own, *got], small=True)


def shards(tokens, spatial_qkv, wo_spatial, w_temporal, wo_temporal, cotangent):
    frames, patches, width = tokens.shape
    inner = wo_spatial.shape[0]
    heads = inner // DH
    padded = -(-inner // LANES) * LANES
    rows = frames * patches
    peers = FRAMES // frames
    chips = peers // 2
    group = patches // peers
    block = 2 * group
    n_dp, n_seq = lax.axis_size("dp"), lax.axis_size("seq")

    def held(columns, dtype=BF16):
        return pltpu.VMEM((rows, columns), dtype)

    wide = held(padded)
    attended = pltpu.VMEM((heads, rows, rows), F32)
    projection = pltpu.VMEM((inner, width), BF16)
    per_chip = rows // chips
    qkv_rows = spatial_qkv.reshape(rows, 3 * inner)
    sent = -(-(2 * width + inner) // LANES) * LANES
    *near, hidden, spatial_p = call(
        functools.partial(spatial_kernel, chips, patches),
        [shape((per_chip, sent))] * chips
        + [shape((rows, width)), shape((heads, rows, rows), F32)],
        [qkv_rows, tokens.reshape(rows, width), wo_spatial, cotangent.reshape(rows, width)],
        [held(width), held(width), held(3 * inner), projection]
        + [pltpu.VMEM((frames * chips, block, sent), BF16), held(width), attended]
        + [wide] * 3
        + [sems(6)],
        far_in=range(4),
        far_out=(chips, chips + 1),
    )
    near, far, weights, places, count = gather(w_temporal.T, near, chips)

    def blocks(dtype):
        return pltpu.VMEM((count, rows, 3 * inner // count), dtype)

    (mine,) = call(
        functools.partial(temporal_kernel, places, chips, group),
        [shape((rows, width + inner))],
        [near, far, wo_temporal, *weights],
        [held(width)] + [wide] * 4 + [attended, blocks(BF16), blocks(F32), held(width, F32)],
        small=True,
    )
    other = flip(mine, "seq", 1)
    back = [shape((per_chip, width + inner))] * chips
    if n_dp == 4 and n_seq == peers:
        size = inner // n_seq
        *back, keep, send_x, send_y = call(
            functools.partial(return_kernel, chips, block, inner, width),
            back
            + [shape((n_dp, size, width), F32)]
            + [shape((2, size, width))] * 2,
            [mine, other, near, far],
            [
                pltpu.VMEM((n_seq, 2 * rows, size), BF16),
                pltpu.VMEM((n_dp, 2 * rows, width // n_dp), BF16),
                pltpu.VMEM((per_chip, width + inner), BF16),
                sems(1),
            ],
            far_out=range(1),
            small=True,
        )
    else:
        *back, both = call(
            functools.partial(whole_return_kernel, chips, block, inner, width),
            back + [shape((2, inner, width))],
            [mine, other, near],
            small=True,
        )
    back = from_chips(back)
    block_out, tokens_grad, qkv_grad = call(
        functools.partial(last_kernel, chips, patches),
        [shape((rows, width)), shape((rows, width)), shape((rows, 3 * inner))],
        [*back, wo_spatial, qkv_rows, spatial_p, wo_temporal, hidden],
        [held(width + inner), projection, held(3 * inner), attended, projection, held(width)]
        + [held(width), held(3 * inner)]
        + [wide] * 4
        + [sems(8 + chips * frames)],
        far_in=range(5 + chips),
        far_out=range(3),
    )
    if n_dp == 4 and n_seq == peers:
        temporal_grad, spatial_grad = reduced(keep, send_x, send_y, back[1])
    else:
        both = lax.psum_scatter(both, "seq", scatter_dimension=1, tiled=True)
        both = lax.psum_scatter(both, "dp", scatter_dimension=2, tiled=True).astype(F32)
        temporal_grad, spatial_grad = both[0], both[1]
    return (
        block_out.reshape(frames, patches, width),
        tokens_grad.reshape(frames, patches, width),
        qkv_grad.reshape(frames, patches, 3 * inner),
        spatial_grad,
        temporal_grad,
    )


def solution(mesh):
    placed = (
        P(("dp", "seq"), None, None),
        P(("dp", "seq"), None, None),
        P(),
        P(None, "dp"),
        P(),
        P(("dp", "seq"), None, None),
    )
    return jax.shard_map(
        shards,
        mesh=mesh,
        in_specs=placed,
        out_specs=(
            P(("dp", "seq"), None, None),
            P(("dp", "seq"), None, None),
            P(("dp", "seq"), None, None),
            P("seq", "dp"),
            P("seq", "dp"),
        ),
        check_vma=False,
    )
```

```python
import functools
import math

import jax
import jax.numpy as jnp
from jax import lax
from jax.experimental import pallas as pl
from jax.experimental.pallas import tpu as pltpu
from jax.sharding import PartitionSpec as P

DH = 72
FRAMES = 16
LANES = 128
BF16 = jnp.bfloat16
F32 = jnp.float32
VMEM = pl.BlockSpec(memory_space=pltpu.VMEM)
SMEM = pl.BlockSpec(memory_space=pltpu.SMEM)
HBM = pl.BlockSpec(memory_space=pltpu.HBM)
PAD = 8 * LANES
LIMIT = 16 * 1024 * 1024
MOST = 60 * 1024 * 1024


def dot(left, right):
    return jnp.dot(left, right, preferred_element_type=F32)


def dot_bt(left, right):
    return lax.dot_general(left, right, (((1,), (1,)), ((), ())), preferred_element_type=F32)


def dot_at(left, right):
    return lax.dot_general(left, right, (((0,), (0,)), ((), ())), preferred_element_type=F32)


def call(body, outs, args, scratch=(), us=0, far_in=(), far_out=(), small=False):
    moved = sum(math.prod(a.shape) * a.dtype.itemsize for a in (*args, *outs))
    near = [SMEM if a.dtype == jnp.int32 else VMEM for a in args]
    return pl.pallas_call(
        body,
        out_shape=outs,
        in_specs=[HBM if i in far_in else spec for i, spec in enumerate(near)],
        out_specs=[
            HBM if i in far_out else SMEM if out.dtype == jnp.int32 else VMEM
            for i, out in enumerate(outs)
        ],
        scratch_shapes=list(scratch),
        compiler_params=pltpu.CompilerParams(vmem_limit_bytes=LIMIT if small else MOST),
        cost_estimate=pl.CostEstimate(
            flops=us * 1150000000, bytes_accessed=moved if us else 0, transcendentals=0
        ),
    )(*args)


def started(pairs, sems):
    copies = [pltpu.make_async_copy(a, b, sems.at[i]) for i, (a, b) in enumerate(pairs)]
    for copy in copies:
        copy.start()
    return copies


def shape(dims, dtype=BF16):
    return jax.ShapeDtypeStruct(dims, dtype)


TOKEN = shape((1,), jnp.int32)


def window(head):
    low = head * DH // LANES * LANES
    high = -(-(head + 1) * DH // LANES) * LANES
    return low, high


def head_only(block, head):
    low, high = window(head)
    lane = lax.broadcasted_iota(jnp.int32, (1, high - low), 1) + low
    keep = (lane >= head * DH) & (lane < (head + 1) * DH)
    return jnp.where(keep, block, jnp.zeros_like(block))


def add_tiles(tiles, head, value):
    low, high = window(head)
    for at in range(low // LANES, high // LANES):
        part = value[:, at * LANES - low : (at + 1) * LANES - low]
        tiles[at] = part if tiles[at] is None else tiles[at] + part


def joined(tiles):
    return jnp.concatenate([tile.astype(BF16) for tile in tiles], axis=1)


def same_group(rows, kind):
    row = lax.broadcasted_iota(jnp.int32, (rows, rows), 0)
    col = lax.broadcasted_iota(jnp.int32, (rows, rows), 1)
    how, size = kind
    return row // size == col // size if how == "block" else row % size == col % size


def softmax_forward(q_ref, k_ref, v_ref, p_ref, heads, kind):
    rows = q_ref.shape[0]
    mask = same_group(rows, kind)
    tiles = [None] * (q_ref.shape[1] // LANES)
    for head in range(heads):
        low, high = window(head)
        s = dot_bt(q_ref[:, low:high], head_only(k_ref[:, low:high], head)) * (1.0 / math.sqrt(DH))
        s = jnp.where(mask, s, -jnp.inf)
        e = jnp.exp(s - jnp.max(s, axis=1, keepdims=True))
        p = e / jnp.sum(e, axis=1, keepdims=True)
        p_ref[head] = p
        add_tiles(tiles, head, dot(p.astype(BF16), head_only(v_ref[:, low:high], head)))
    return joined(tiles)


def softmax_backward(q_ref, k_ref, v_ref, g_ref, p_ref, heads):
    count = q_ref.shape[1] // LANES
    dq, dk, dv = [None] * count, [None] * count, [None] * count
    for head in range(heads):
        low, high = window(head)
        p = p_ref[head]
        g = head_only(g_ref[:, low:high], head)
        add_tiles(dv, head, dot_at(p.astype(BF16), g))
        dp = dot_bt(g, v_ref[:, low:high])
        ds = p * (dp - jnp.sum(p * dp, axis=1, keepdims=True)) * (1.0 / math.sqrt(DH))
        ds = ds.astype(BF16)
        add_tiles(dq, head, dot(ds, head_only(k_ref[:, low:high], head)))
        add_tiles(dk, head, dot_at(ds, head_only(q_ref[:, low:high], head)))
    return joined(dq), joined(dk), joined(dv)


def put(ref, value):
    width = value.shape[1]
    ref[:, width // LANES * LANES :] = jnp.zeros(
        (ref.shape[0], ref.shape[1] - width // LANES * LANES), ref.dtype
    )
    ref[:, :width] = value


def place(chips):
    seq = lax.axis_index("seq")
    return lax.axis_index("dp"), seq % 2, seq % (2 * chips) // 2, seq


def spatial_kernel(chips, patches, *refs):
    idx = place(chips)
    far, outs, refs = refs[:4], refs[4 : 4 + chips], refs[4 + chips :]
    hid_far, p_far, tok, cot, qkv, wos, held, hid, p_ref, qs, ks, vs, sems = refs
    inner, width = wos.shape
    count, block, _ = held.shape
    loads = started(zip(far, (qkv, tok, wos, cot)), sems)
    loads[0].wait()
    x = qkv[...]
    put(qs, x[:, :inner])
    put(ks, x[:, inner : 2 * inner])
    put(vs, x[:, 2 * inner :])
    o = softmax_forward(qs, ks, vs, p_ref, inner // DH, ("block", patches))[:, :inner]
    stores = started([(p_ref, p_far)], sems.at[pl.ds(4, 1)])
    for at in range(3):
        loads[1 + at].wait()
    hid[...] = (tok[...].astype(F32) + dot(o, wos[...])).astype(BF16)
    for at in range(count):
        rows = slice(at * block, (at + 1) * block)
        held[at, :, :width] = hid[rows]
        held[at, :, width : 2 * width] = cot[rows]
        held[at, :, 2 * width : 2 * width + inner] = o[rows]
    stores += started([(hid, hid_far)], sems.at[pl.ds(5, 1)])
    for q in range(chips):
        for f in range(count // chips):
            rows = slice(f * block, (f + 1) * block)
            outs[q][rows] = held[f * chips + (idx[2] ^ q)]
    for copy in stores:
        copy.wait()


def own_patches(ref, core, block):
    rows, width = ref.shape
    value = ref[...].astype(F32).reshape(rows // block, block, width)
    value = jnp.where(core == 0, value[:, : block // 2], value[:, block // 2 :])
    return value.reshape(rows // 2, width)


def all_patches(mine, other, core, block):
    rows, width = mine.shape
    mine = mine.astype(F32).reshape(2 * rows // block, block // 2, width)
    other = other.astype(F32).reshape(2 * rows // block, block // 2, width)
    first, second = jnp.where(core == 0, mine, other), jnp.where(core == 0, other, mine)
    return jnp.concatenate([first, second], axis=1).reshape(2 * rows, width).astype(BF16)


def cut_kernel(chips, whole, left, right, sem):
    core, cut = place(chips)[1], left.shape[1]
    pairs = [(whole.at[core, :, pl.ds(0, cut)], left)]
    pairs.append((whole.at[core, :, pl.ds(cut, right.shape[1])], right))
    for copy in started(pairs, sem):
        copy.wait()


def second_kernel(own_left, own_right, got_x, got_y, own, left, right, kept):
    half = got_x.shape[0]
    left[:half] = own_left[...]
    left[half:] = got_x[...]
    right[:half] = own_right[...]
    right[half:] = got_y[...]
    kept[...] = own[...]


def join_rows_kernel(*refs):
    out, low = refs[-1], 0
    for ref in refs[:-1]:
        out[low : low + ref.shape[0], : ref.shape[1]] = ref[...]
        low += ref.shape[0]


def projected(hidden, shards, weights, idx, blocks, sums):
    size = blocks.shape[2]
    sums[...] = jnp.zeros_like(sums)
    for held, w in zip(shards, weights):
        low = held[0][1]
        value = dot_bt(hidden[:, low : low + w.shape[1]], w[...])
        for at, _, i in held:
            sums[at(idx)] += value if i is None else value[:, i * size : (i + 1) * size]
    blocks[...] = sums[...].astype(BF16)


def projected_back(blocks, shards, weights, idx, total):
    total[...] = jnp.zeros_like(total)
    for held, w in zip(shards, weights):
        low = held[0][1]
        lhs = jnp.concatenate([blocks[at(idx)] for at, _, _ in held], axis=1)
        total[:, low : low + w.shape[1]] += dot(lhs, w[...])


def temporal_kernel(shards, chips, group, near, far, wot, *refs):
    idx = place(chips)
    weights, refs = refs[: len(shards)], refs[len(shards) :]
    mine, cot, q, k, v, g, p_ref, blocks, sums, total = refs
    inner, width = wot.shape
    heads = inner // DH
    value = [own_patches(ref, idx[1], 2 * group) for ref in (near, far)]
    value = jnp.concatenate(value, axis=0).astype(BF16)
    hidden = value[:, :width]
    cot[...] = value[:, width : 2 * width]
    size = blocks.shape[2]
    projected(hidden, shards, weights, idx, blocks, sums)
    whole = jnp.concatenate([blocks[i] for i in range(blocks.shape[0])], axis=1)
    put(q, whole[:, :inner])
    put(k, whole[:, inner : 2 * inner])
    put(v, whole[:, 2 * inner :])
    mine[:, width:] = softmax_forward(q, k, v, p_ref, heads, ("cycle", group))[:, :inner]
    put(g, dot_bt(cot[...], wot[...]).astype(BF16))
    dq, dk, dv = softmax_backward(q, k, v, g, p_ref, heads)
    whole = jnp.concatenate([dq[:, :inner], dk[:, :inner], dv[:, :inner]], axis=1)
    for i in range(blocks.shape[0]):
        blocks[i] = whole[:, i * size : (i + 1) * size]
    projected_back(blocks, shards, weights, idx, total)
    grad = total[...]
    mine[:, :width] = (cot[...].astype(F32) + grad.astype(BF16).astype(F32)).astype(BF16)


def whole_return_kernel(chips, block, inner, width, mine, other, *refs):
    idx = place(chips)
    held, outs, part = refs[0], refs[1 : 1 + chips], refs[1 + chips]
    cot, so = held[:, width : 2 * width], held[:, 2 * width : 2 * width + inner]
    half = mine.shape[0] // 2
    near = all_patches(mine[:half], other[half:], idx[1], block)
    for q, out in enumerate(outs):
        out[...] = near[q * out.shape[0] : (q + 1) * out.shape[0]]
    part[0] = dot_at(near[:, width:], cot).astype(BF16)
    part[1] = dot_at(so, near[:, :width]).astype(BF16)


def return_kernel(chips, block, inner, width, mine, other, *refs):
    idx = place(chips)
    sent, refs = refs[:2], refs[2:]
    outs, (keep, send_x, send_y, heads, cols, kept, sem) = refs[:chips], refs[chips:]
    half = mine.shape[0] // 2
    near = all_patches(mine[:half], other[half:], idx[1], block)
    rows = kept.shape[0]
    kept[...] = near[:rows]
    copy = pltpu.make_async_copy(kept, outs[0], sem.at[0])
    copy.start()
    for q in range(1, chips):
        outs[q][...] = near[q * rows : (q + 1) * rows]
    far = all_patches(mine[half:], other[:half], idx[1], block)
    rows = near.shape[0]
    size = heads.shape[2]
    count, _, wide = cols.shape
    for i in range(2):
        if i == 0:
            lefts = [near[:, width:], far[:, width:]]
            rights = [part[:, width : 2 * width] for part in sent]
        else:
            lefts = [part[:, 2 * width : 2 * width + inner] for part in sent]
            rights = [near[:, :width], far[:, :width]]
        for at in range(2):
            held = slice(at * rows, (at + 1) * rows)
            for h in range(heads.shape[0]):
                heads[h, held] = lefts[at][:, h * size : (h + 1) * size]
            for r in range(count):
                cols[r, held] = rights[at][:, r * wide : (r + 1) * wide]
        left = jnp.concatenate([heads[idx[3] ^ (2 * q)] for q in range(chips)], axis=1)
        first = 1 if i == 0 else 2
        for r in range(count):
            full = dot_at(left, cols[idx[0] ^ r])
            value = jnp.concatenate([full[q * size : (q + 1) * size] for q in range(chips)], axis=1)
            if r & first:
                (send_x, send_y)[i][r // 2 if i == 0 else r - 2] = value.astype(BF16)
            else:
                keep[2 * i + (r > 0)] = value
    copy.wait()


def sum_first_kernel(keep, got_x, got_y, _, own, send_y, send_x):
    for i, (got, send) in enumerate(((got_x, send_y), (got_y, send_x))):
        own[i] = keep[2 * i] + got[0].astype(F32)
        send[...] = (keep[2 * i + 1] + got[1].astype(F32)).astype(BF16)


def sum_second_kernel(own, got_y, got_x, kept, *outs):
    totals = [own[0] + got_y[...].astype(F32), own[1] + got_x[...].astype(F32)]
    size = totals[0].shape[1] // (1 + len(outs))
    for q, out in enumerate((kept, *outs)):
        cut = [total[:, q * size : (q + 1) * size] for total in totals]
        out[...] = jnp.concatenate(cut, axis=1).astype(out.dtype)


def sum_kernel(own, *refs):
    got, outs = refs[:-2], refs[-2:]
    total = own[...]
    for part in got:
        total += part[...].astype(F32)
    size = outs[0].shape[1]
    for i, out in enumerate(outs):
        out[...] = total[:, i * size : (i + 1) * size]


def last_kernel(chips, patches, *refs):
    idx = place(chips)
    held, (wos, qkv, p_ref, wot, hid), refs = refs[:chips], refs[chips : chips + 5], refs[chips + 5 :]
    block_far, out_far, grads_far, rows, block_out, grads, qs, ks, vs, gs, sems = refs
    inner, width = wos.shape
    frames = rows.shape[0] // patches
    block = patches // chips
    for q in range(chips):
        for f in range(frames):
            low = pl.multiple_of(f * patches + (idx[2] ^ q) * block, block)
            rows[pl.ds(low, block)] = held[q][f * block : (f + 1) * block]
    value = rows[...]
    grad, attended = value[:, :width], value[:, width:]
    stores = started([(rows.at[:, pl.ds(0, width)], out_far)], sems.at[pl.ds(0, 1)])
    block_out[...] = (hid[...].astype(F32) + dot(attended, wot[...])).astype(BF16)
    stores += started([(block_out, block_far)], sems.at[pl.ds(1, 1)])
    put(gs, dot_bt(grad, wos[...]).astype(BF16))
    x = qkv[...]
    put(qs, x[:, :inner])
    put(ks, x[:, inner : 2 * inner])
    put(vs, x[:, 2 * inner :])
    dq, dk, dv = softmax_backward(qs, ks, vs, gs, p_ref, inner // DH)
    grads[...] = jnp.concatenate([dq[:, :inner], dk[:, :inner], dv[:, :inner]], axis=1)
    stores += started([(grads, grads_far)], sems.at[pl.ds(2, 1)])
    for copy in stores:
        copy.wait()


def flip(value, axis, bit):
    return lax.ppermute(value, axis, [(i, i ^ bit) for i in range(lax.axis_size(axis))])


def sems(n):
    return pltpu.SemaphoreType.DMA((n,))


def gather(weight, parts, chips):
    n = lax.axis_size("dp")
    rows, sent = parts[0].shape
    whole = [shape((len(parts) * rows, sent + PAD))]
    if n != 4:
        (near,) = call(join_rows_kernel, whole, from_chips(parts), small=True)
        weights = [lax.all_gather(weight, "dp", axis=0, tiled=True)]
        return near, flip(near, "seq", 1), weights, [[(lambda idx: 0, 0, None)]], 1
    half, width = weight.shape[0] // 2, weight.shape[1]
    cut = -(-width // LANES // 2) * LANES
    left, right = call(
        functools.partial(cut_kernel, chips),
        [shape((half, cut)), shape((half, width - cut))],
        [weight.reshape(2, half, width)],
        [sems(2)],
        far_in=range(1),
    )
    got_x, got_y = flip(left, "dp", 1), flip(right, "dp", 2)
    left, right, own = call(
        second_kernel,
        [shape((2 * half, cut)), shape((2 * half, width - cut)), shape((rows, sent))],
        [left, right, got_x, got_y, parts[0]],
        small=True,
    )
    (near,) = call(join_rows_kernel, whole, from_chips(parts), small=True)
    (right,) = call(
        join_rows_kernel,
        [shape((3 * half, width - cut))],
        [got_y, flip(right, "dp", 1)],
        small=True,
    )
    held = [got_x, flip(left, "dp", 2), right]
    weights = [weight, *held, *[flip(w, "seq", 1) for w in held]]

    def block(j, other):
        return lambda idx: 2 * (idx[0] ^ j) + (idx[1] ^ other)

    shards = [[(lambda idx: 2 * idx[0], 0, 0), (lambda idx: 2 * idx[0] + 1, 0, 1)]]
    for other in (0, 1):
        shards += [[(block(1, other), 0, None)]]
        shards.append([(block(2, other), 0, 0), (block(3, other), 0, 1)])
        shards.append([(block(j, other), cut, i) for i, j in enumerate((2, 1, 3))])
    return near, flip(near, "seq", 1), weights, shards, 2 * n


def from_chips(parts):
    return [parts[0]] + [flip(parts[q], "seq", 2 * q) for q in range(1, len(parts))]


def reduced(keep, send_x, send_y, after):
    _, size, width = keep.shape
    step = shape((size, width))
    own, send_t, send_s = call(
        sum_first_kernel,
        [shape((2, size, width), F32), step, step],
        [keep, flip(send_x, "dp", 1), flip(send_y, "dp", 2), after],
        small=True,
    )
    n = lax.axis_size("seq") // 2
    block = (size, 2 * width // n)
    own, *sends = call(
        sum_second_kernel,
        [shape(block, F32)] + [shape(block)] * (n - 1),
        [own, flip(send_t, "dp", 2), flip(send_s, "dp", 1)],
        small=True,
    )
    got = [flip(value, "seq", 2 * (q + 1)) for q, value in enumerate(sends)]
    return call(sum_kernel, [shape((size, width // n), F32)] * 2, [own, *got], small=True)


def shards(tokens, spatial_qkv, wo_spatial, w_temporal, wo_temporal, cotangent):
    frames, patches, width = tokens.shape
    inner = wo_spatial.shape[0]
    heads = inner // DH
    padded = -(-inner // LANES) * LANES
    rows = frames * patches
    peers = FRAMES // frames
    chips = peers // 2
    group = patches // peers
    block = 2 * group
    n_dp, n_seq = lax.axis_size("dp"), lax.axis_size("seq")

    def held(columns, dtype=BF16):
        return pltpu.VMEM((rows, columns), dtype)

    wide = held(padded)
    attended = pltpu.VMEM((heads, rows, rows), F32)
    projection = pltpu.VMEM((inner, width), BF16)
    per_chip = rows // chips
    qkv_rows = spatial_qkv.reshape(rows, 3 * inner)
    sent = -(-(2 * width + inner) // LANES) * LANES
    *near, hidden, spatial_p = call(
        functools.partial(spatial_kernel, chips, patches),
        [shape((per_chip, sent))] * chips
        + [shape((rows, width)), shape((heads, rows, rows), F32)],
        [qkv_rows, tokens.reshape(rows, width), wo_spatial, cotangent.reshape(rows, width)],
        [held(width), held(width), held(3 * inner), projection]
        + [pltpu.VMEM((frames * chips, block, sent), BF16), held(width), attended]
        + [wide] * 3
        + [sems(6)],
        far_in=range(4),
        far_out=(chips, chips + 1),
    )
    near, far, weights, places, count = gather(w_temporal.T, near, chips)

    def blocks(dtype):
        return pltpu.VMEM((count, rows, 3 * inner // count), dtype)

    (mine,) = call(
        functools.partial(temporal_kernel, places, chips, group),
        [shape((rows, width + inner))],
        [near, far, wo_temporal, *weights],
        [held(width)] + [wide] * 4 + [attended, blocks(BF16), blocks(F32), held(width, F32)],
        small=True,
    )
    other = flip(mine, "seq", 1)
    back = [shape((per_chip, width + inner))] * chips
    if n_dp == 4 and n_seq == peers:
        size = inner // n_seq
        *back, keep, send_x, send_y = call(
            functools.partial(return_kernel, chips, block, inner, width),
            back
            + [shape((n_dp, size, width), F32)]
            + [shape((2, size, width))] * 2,
            [mine, other, near, far],
            [
                pltpu.VMEM((n_seq, 2 * rows, size), BF16),
                pltpu.VMEM((n_dp, 2 * rows, width // n_dp), BF16),
                pltpu.VMEM((per_chip, width + inner), BF16),
                sems(1),
            ],
            far_out=range(1),
            small=True,
        )
    else:
        *back, both = call(
            functools.partial(whole_return_kernel, chips, block, inner, width),
            back + [shape((2, inner, width))],
            [mine, other, near],
            small=True,
        )
    back = from_chips(back)
    block_out, tokens_grad, qkv_grad = call(
        functools.partial(last_kernel, chips, patches),
        [shape((rows, width)), shape((rows, width)), shape((rows, 3 * inner))],
        [*back, wo_spatial, qkv_rows, spatial_p, wo_temporal, hidden],
        [held(width + inner), held(width), held(3 * inner)] + [wide] * 4 + [sems(3)],
        far_out=range(3),
        small=True,
    )
    if n_dp == 4 and n_seq == peers:
        temporal_grad, spatial_grad = reduced(keep, send_x, send_y, back[1])
    else:
        both = lax.psum_scatter(both, "seq", scatter_dimension=1, tiled=True)
        both = lax.psum_scatter(both, "dp", scatter_dimension=2, tiled=True).astype(F32)
        temporal_grad, spatial_grad = both[0], both[1]
    return (
        block_out.reshape(frames, patches, width),
        tokens_grad.reshape(frames, patches, width),
        qkv_grad.reshape(frames, patches, 3 * inner),
        spatial_grad,
        temporal_grad,
    )


def solution(mesh):
    placed = (
        P(("dp", "seq"), None, None),
        P(("dp", "seq"), None, None),
        P(),
        P(None, "dp"),
        P(),
        P(("dp", "seq"), None, None),
    )
    return jax.shard_map(
        shards,
        mesh=mesh,
        in_specs=placed,
        out_specs=(
            P(("dp", "seq"), None, None),
            P(("dp", "seq"), None, None),
            P(("dp", "seq"), None, None),
            P("seq", "dp"),
            P("seq", "dp"),
        ),
        check_vma=False,
    )
```

```python
import functools
import math

import jax
import jax.numpy as jnp
from jax import lax
from jax.experimental import pallas as pl
from jax.experimental.pallas import tpu as pltpu
from jax.sharding import PartitionSpec as P

DH = 72
FRAMES = 16
LANES = 128
BF16 = jnp.bfloat16
F32 = jnp.float32
VMEM = pl.BlockSpec(memory_space=pltpu.VMEM)
SMEM = pl.BlockSpec(memory_space=pltpu.SMEM)
HBM = pl.BlockSpec(memory_space=pltpu.HBM)
PAD = 2 * LANES
LIMIT = 16 * 1024 * 1024
MOST = 60 * 1024 * 1024


def dot(left, right):
    return jnp.dot(left, right, preferred_element_type=F32)


def dot_bt(left, right):
    return lax.dot_general(left, right, (((1,), (1,)), ((), ())), preferred_element_type=F32)


def dot_at(left, right):
    return lax.dot_general(left, right, (((0,), (0,)), ((), ())), preferred_element_type=F32)


def call(body, outs, args, scratch=(), us=0, far_in=(), far_out=(), small=False):
    moved = sum(math.prod(a.shape) * a.dtype.itemsize for a in (*args, *outs))
    near = [SMEM if a.dtype == jnp.int32 else VMEM for a in args]
    return pl.pallas_call(
        body,
        out_shape=outs,
        in_specs=[HBM if i in far_in else spec for i, spec in enumerate(near)],
        out_specs=[
            HBM if i in far_out else SMEM if out.dtype == jnp.int32 else VMEM
            for i, out in enumerate(outs)
        ],
        scratch_shapes=list(scratch),
        compiler_params=pltpu.CompilerParams(vmem_limit_bytes=LIMIT if small else MOST),
        cost_estimate=pl.CostEstimate(
            flops=us * 1150000000, bytes_accessed=moved if us else 0, transcendentals=0
        ),
    )(*args)


def started(pairs, sems):
    copies = [pltpu.make_async_copy(a, b, sems.at[i]) for i, (a, b) in enumerate(pairs)]
    for copy in copies:
        copy.start()
    return copies


def shape(dims, dtype=BF16):
    return jax.ShapeDtypeStruct(dims, dtype)


TOKEN = shape((1,), jnp.int32)


def window(head):
    low = head * DH // LANES * LANES
    high = -(-(head + 1) * DH // LANES) * LANES
    return low, high


def head_only(block, head):
    low, high = window(head)
    lane = lax.broadcasted_iota(jnp.int32, (1, high - low), 1) + low
    keep = (lane >= head * DH) & (lane < (head + 1) * DH)
    return jnp.where(keep, block, jnp.zeros_like(block))


def add_tiles(tiles, head, value):
    low, high = window(head)
    for at in range(low // LANES, high // LANES):
        part = value[:, at * LANES - low : (at + 1) * LANES - low]
        tiles[at] = part if tiles[at] is None else tiles[at] + part


def joined(tiles):
    return jnp.concatenate([tile.astype(BF16) for tile in tiles], axis=1)


def same_group(rows, kind):
    row = lax.broadcasted_iota(jnp.int32, (rows, rows), 0)
    col = lax.broadcasted_iota(jnp.int32, (rows, rows), 1)
    how, size = kind
    return row // size == col // size if how == "block" else row % size == col % size


def softmax_forward(q_ref, k_ref, v_ref, p_ref, heads, kind):
    rows = q_ref.shape[0]
    mask = same_group(rows, kind)
    tiles = [None] * (q_ref.shape[1] // LANES)
    for head in range(heads):
        low, high = window(head)
        s = dot_bt(q_ref[:, low:high], head_only(k_ref[:, low:high], head)) * (1.0 / math.sqrt(DH))
        s = jnp.where(mask, s, -jnp.inf)
        e = jnp.exp(s - jnp.max(s, axis=1, keepdims=True))
        p = e / jnp.sum(e, axis=1, keepdims=True)
        p_ref[head] = p
        add_tiles(tiles, head, dot(p.astype(BF16), head_only(v_ref[:, low:high], head)))
    return joined(tiles)


def softmax_backward(q_ref, k_ref, v_ref, g_ref, p_ref, heads):
    count = q_ref.shape[1] // LANES
    dq, dk, dv = [None] * count, [None] * count, [None] * count
    for head in range(heads):
        low, high = window(head)
        p = p_ref[head]
        g = head_only(g_ref[:, low:high], head)
        add_tiles(dv, head, dot_at(p.astype(BF16), g))
        dp = dot_bt(g, v_ref[:, low:high])
        ds = p * (dp - jnp.sum(p * dp, axis=1, keepdims=True)) * (1.0 / math.sqrt(DH))
        ds = ds.astype(BF16)
        add_tiles(dq, head, dot(ds, head_only(k_ref[:, low:high], head)))
        add_tiles(dk, head, dot_at(ds, head_only(q_ref[:, low:high], head)))
    return joined(dq), joined(dk), joined(dv)


def put(ref, value):
    width = value.shape[1]
    ref[:, width // LANES * LANES :] = jnp.zeros(
        (ref.shape[0], ref.shape[1] - width // LANES * LANES), ref.dtype
    )
    ref[:, :width] = value


def place(chips):
    seq = lax.axis_index("seq")
    return lax.axis_index("dp"), seq % 2, seq % (2 * chips) // 2, seq


def spatial_kernel(chips, patches, *refs):
    idx = place(chips)
    far, outs, refs = refs[:4], refs[4 : 4 + chips], refs[4 + chips :]
    hid_far, p_far, tok, cot, qkv, wos, held, hid, p_ref, qs, ks, vs, sems = refs
    inner, width = wos.shape
    count, block, _ = held.shape
    loads = started(zip(far, (qkv, tok, wos, cot)), sems)
    loads[0].wait()
    x = qkv[...]
    put(qs, x[:, :inner])
    put(ks, x[:, inner : 2 * inner])
    put(vs, x[:, 2 * inner :])
    o = softmax_forward(qs, ks, vs, p_ref, inner // DH, ("block", patches))[:, :inner]
    stores = started([(p_ref, p_far)], sems.at[pl.ds(4, 1)])
    for at in range(3):
        loads[1 + at].wait()
    hid[...] = (tok[...].astype(F32) + dot(o, wos[...])).astype(BF16)
    for at in range(count):
        rows = slice(at * block, (at + 1) * block)
        held[at, :, :width] = hid[rows]
        held[at, :, width : 2 * width] = cot[rows]
        held[at, :, 2 * width : 2 * width + inner] = o[rows]
    stores += started([(hid, hid_far)], sems.at[pl.ds(5, 1)])
    for q in range(chips):
        for f in range(count // chips):
            rows = slice(f * block, (f + 1) * block)
            outs[q][rows] = held[f * chips + (idx[2] ^ q)]
    for copy in stores:
        copy.wait()


def own_patches(ref, core, block):
    rows, width = ref.shape
    value = ref[...].astype(F32).reshape(rows // block, block, width)
    value = jnp.where(core == 0, value[:, : block // 2], value[:, block // 2 :])
    return value.reshape(rows // 2, width)


def all_patches(mine, other, core, block):
    rows, width = mine.shape
    mine = mine.astype(F32).reshape(2 * rows // block, block // 2, width)
    other = other.astype(F32).reshape(2 * rows // block, block // 2, width)
    first, second = jnp.where(core == 0, mine, other), jnp.where(core == 0, other, mine)
    return jnp.concatenate([first, second], axis=1).reshape(2 * rows, width).astype(BF16)


def half_kernel(chips, got, own, half, kept):
    rows = half.shape[0]
    core = place(chips)[1]
    half[...] = jnp.where(core == 0, got[:rows].astype(F32), got[rows:].astype(F32)).astype(BF16)
    kept[...] = own[...]


def join_rows_kernel(*refs):
    out, low = refs[-1], 0
    for ref in refs[:-1]:
        out[low : low + ref.shape[0], : ref.shape[1]] = ref[...]
        low += ref.shape[0]


def temporal_kernel(shards, chips, group, near, far, wot, *refs):
    idx = place(chips)
    weights, refs = refs[: len(shards)], refs[len(shards) :]
    mine, cot, q, k, v, g, p_ref, blocks = refs
    inner, width = wot.shape
    heads = inner // DH
    value = [own_patches(ref, idx[1], 2 * group) for ref in (near, far)]
    value = jnp.concatenate(value, axis=0).astype(BF16)
    hidden = value[:, :width]
    cot[...] = value[:, width : 2 * width]
    size = blocks.shape[2]
    for at, w in zip(shards, weights):
        value = dot_bt(hidden, w[...]).astype(BF16)
        for i, block in enumerate(at(idx)):
            blocks[block] = value[:, i * size : (i + 1) * size]
    whole = jnp.concatenate([blocks[i] for i in range(blocks.shape[0])], axis=1)
    put(q, whole[:, :inner])
    put(k, whole[:, inner : 2 * inner])
    put(v, whole[:, 2 * inner :])
    mine[:, width:] = softmax_forward(q, k, v, p_ref, heads, ("cycle", group))[:, :inner]
    put(g, dot_bt(cot[...], wot[...]).astype(BF16))
    dq, dk, dv = softmax_backward(q, k, v, g, p_ref, heads)
    whole = jnp.concatenate([dq[:, :inner], dk[:, :inner], dv[:, :inner]], axis=1)
    for i in range(blocks.shape[0]):
        blocks[i] = whole[:, i * size : (i + 1) * size]
    grad = jnp.zeros(cot.shape, F32)
    for at, w in zip(shards, weights):
        lhs = jnp.concatenate([blocks[block] for block in at(idx)], axis=1)
        grad += dot(lhs, w[...])
    mine[:, :width] = (cot[...].astype(F32) + grad.astype(BF16).astype(F32)).astype(BF16)


def whole_return_kernel(chips, block, inner, width, mine, other, *refs):
    idx = place(chips)
    held, outs, part = refs[0], refs[1 : 1 + chips], refs[1 + chips]
    cot, so = held[:, width : 2 * width], held[:, 2 * width : 2 * width + inner]
    half = mine.shape[0] // 2
    near = all_patches(mine[:half], other[half:], idx[1], block)
    for q, out in enumerate(outs):
        out[...] = near[q * out.shape[0] : (q + 1) * out.shape[0]]
    part[0] = dot_at(near[:, width:], cot).astype(BF16)
    part[1] = dot_at(so, near[:, :width]).astype(BF16)


def return_kernel(chips, block, inner, width, mine, other, *refs):
    idx = place(chips)
    sent, refs = refs[:2], refs[2:]
    outs, (keep, send_x, send_y, heads, cols, kept, sem) = refs[:chips], refs[chips:]
    half = mine.shape[0] // 2
    near = all_patches(mine[:half], other[half:], idx[1], block)
    rows = kept.shape[0]
    kept[...] = near[:rows]
    copy = pltpu.make_async_copy(kept, outs[0], sem.at[0])
    copy.start()
    for q in range(1, chips):
        outs[q][...] = near[q * rows : (q + 1) * rows]
    far = all_patches(mine[half:], other[:half], idx[1], block)
    rows = near.shape[0]
    size = heads.shape[2]
    count, _, wide = cols.shape
    for i in range(2):
        if i == 0:
            lefts = [near[:, width:], far[:, width:]]
            rights = [part[:, width : 2 * width] for part in sent]
        else:
            lefts = [part[:, 2 * width : 2 * width + inner] for part in sent]
            rights = [near[:, :width], far[:, :width]]
        for at in range(2):
            held = slice(at * rows, (at + 1) * rows)
            for h in range(heads.shape[0]):
                heads[h, held] = lefts[at][:, h * size : (h + 1) * size]
            for r in range(count):
                cols[r, held] = rights[at][:, r * wide : (r + 1) * wide]
        left = jnp.concatenate([heads[idx[3] ^ (2 * q)] for q in range(chips)], axis=1)
        first = 1 if i == 0 else 2
        for r in range(count):
            full = dot_at(left, cols[idx[0] ^ r])
            value = jnp.concatenate([full[q * size : (q + 1) * size] for q in range(chips)], axis=1)
            if r & first:
                (send_x, send_y)[i][r // 2 if i == 0 else r - 2] = value.astype(BF16)
            else:
                keep[2 * i + (r > 0)] = value
    copy.wait()


def sum_first_kernel(keep, got_x, got_y, _, own, send_y, send_x):
    for i, (got, send) in enumerate(((got_x, send_y), (got_y, send_x))):
        own[i] = keep[2 * i] + got[0].astype(F32)
        send[...] = (keep[2 * i + 1] + got[1].astype(F32)).astype(BF16)


def sum_second_kernel(own, got_y, got_x, kept, *outs):
    totals = [own[0] + got_y[...].astype(F32), own[1] + got_x[...].astype(F32)]
    size = totals[0].shape[1] // (1 + len(outs))
    for q, out in enumerate((kept, *outs)):
        cut = [total[:, q * size : (q + 1) * size] for total in totals]
        out[...] = jnp.concatenate(cut, axis=1).astype(out.dtype)


def sum_kernel(own, *refs):
    got, outs = refs[:-2], refs[-2:]
    total = own[...]
    for part in got:
        total += part[...].astype(F32)
    size = outs[0].shape[1]
    for i, out in enumerate(outs):
        out[...] = total[:, i * size : (i + 1) * size]


def last_kernel(chips, patches, *refs):
    idx = place(chips)
    held, (wos, qkv, p_ref, wot, hid), refs = refs[:chips], refs[chips : chips + 5], refs[chips + 5 :]
    block_far, out_far, grads_far, rows, block_out, grads, qs, ks, vs, gs, sems = refs
    inner, width = wos.shape
    frames = rows.shape[0] // patches
    block = patches // chips
    for q in range(chips):
        for f in range(frames):
            low = pl.multiple_of(f * patches + (idx[2] ^ q) * block, block)
            rows[pl.ds(low, block)] = held[q][f * block : (f + 1) * block]
    value = rows[...]
    grad, attended = value[:, :width], value[:, width:]
    stores = started([(rows.at[:, pl.ds(0, width)], out_far)], sems.at[pl.ds(0, 1)])
    block_out[...] = (hid[...].astype(F32) + dot(attended, wot[...])).astype(BF16)
    stores += started([(block_out, block_far)], sems.at[pl.ds(1, 1)])
    put(gs, dot_bt(grad, wos[...]).astype(BF16))
    x = qkv[...]
    put(qs, x[:, :inner])
    put(ks, x[:, inner : 2 * inner])
    put(vs, x[:, 2 * inner :])
    dq, dk, dv = softmax_backward(qs, ks, vs, gs, p_ref, inner // DH)
    grads[...] = jnp.concatenate([dq[:, :inner], dk[:, :inner], dv[:, :inner]], axis=1)
    stores += started([(grads, grads_far)], sems.at[pl.ds(2, 1)])
    for copy in stores:
        copy.wait()


def flip(value, axis, bit):
    return lax.ppermute(value, axis, [(i, i ^ bit) for i in range(lax.axis_size(axis))])


def sems(n):
    return pltpu.SemaphoreType.DMA((n,))


def across(value, bits):
    n = lax.axis_size("seq")
    pairs = [
        (d * n + i, (d ^ bits[i % 2]) * n + i) for d in range(lax.axis_size("dp")) for i in range(n)
    ]
    return lax.ppermute(value, ("dp", "seq"), pairs)


def gather(weight, parts, chips):
    n = lax.axis_size("dp")
    rows, sent = parts[0].shape
    whole = [shape((len(parts) * rows, sent + PAD))]
    if n != 4:
        (near,) = call(join_rows_kernel, whole, from_chips(parts), small=True)
        weights = [lax.all_gather(weight, "dp", axis=0, tiled=True)]
        return near, flip(near, "seq", 1), weights, [lambda idx: [0]], 1
    half, width = weight.shape[0] // 2, weight.shape[1]
    side = across(weight, (1, 2))
    corner, own = call(
        functools.partial(half_kernel, chips),
        [shape((half, width)), shape((rows, sent))],
        [side, parts[0]],
        small=True,
    )
    corner = across(corner, (2, 1))
    (near,) = call(join_rows_kernel, whole, [own, *from_chips(parts)[1:]], small=True)
    weights = [weight, side, flip(side, "seq", 1), corner, flip(corner, "seq", 1)]

    def both(shard):
        return lambda idx: [2 * shard(idx), 2 * shard(idx) + 1]

    shards = [
        both(lambda idx: idx[0]),
        both(lambda idx: idx[0] ^ (1 + idx[1])),
        both(lambda idx: idx[0] ^ (2 - idx[1])),
        lambda idx: [2 * (idx[0] ^ 3) + idx[1]],
        lambda idx: [2 * (idx[0] ^ 3) + 1 - idx[1]],
    ]
    return near, flip(near, "seq", 1), weights, shards, 2 * n


def from_chips(parts):
    return [parts[0]] + [flip(parts[q], "seq", 2 * q) for q in range(1, len(parts))]


def reduced(keep, send_x, send_y, after):
    _, size, width = keep.shape
    step = shape((size, width))
    own, send_t, send_s = call(
        sum_first_kernel,
        [shape((2, size, width), F32), step, step],
        [keep, flip(send_x, "dp", 1), flip(send_y, "dp", 2), after],
        small=True,
    )
    n = lax.axis_size("seq") // 2
    block = (size, 2 * width // n)
    own, *sends = call(
        sum_second_kernel,
        [shape(block, F32)] + [shape(block)] * (n - 1),
        [own, flip(send_t, "dp", 2), flip(send_s, "dp", 1)],
        small=True,
    )
    got = [flip(value, "seq", 2 * (q + 1)) for q, value in enumerate(sends)]
    return call(sum_kernel, [shape((size, width // n), F32)] * 2, [own, *got], small=True)


def shards(tokens, spatial_qkv, wo_spatial, w_temporal, wo_temporal, cotangent):
    frames, patches, width = tokens.shape
    inner = wo_spatial.shape[0]
    heads = inner // DH
    padded = -(-inner // LANES) * LANES
    rows = frames * patches
    peers = FRAMES // frames
    chips = peers // 2
    group = patches // peers
    block = 2 * group
    n_dp, n_seq = lax.axis_size("dp"), lax.axis_size("seq")

    def held(columns, dtype=BF16):
        return pltpu.VMEM((rows, columns), dtype)

    wide = held(padded)
    attended = pltpu.VMEM((heads, rows, rows), F32)
    projection = pltpu.VMEM((inner, width), BF16)
    per_chip = rows // chips
    qkv_rows = spatial_qkv.reshape(rows, 3 * inner)
    sent = -(-(2 * width + inner) // LANES) * LANES
    *near, hidden, spatial_p = call(
        functools.partial(spatial_kernel, chips, patches),
        [shape((per_chip, sent))] * chips
        + [shape((rows, width)), shape((heads, rows, rows), F32)],
        [qkv_rows, tokens.reshape(rows, width), wo_spatial, cotangent.reshape(rows, width)],
        [held(width), held(width), held(3 * inner), projection]
        + [pltpu.VMEM((frames * chips, block, sent), BF16), held(width), attended]
        + [wide] * 3
        + [sems(6)],
        far_in=range(4),
        far_out=(chips, chips + 1),
    )
    near, far, weights, places, count = gather(w_temporal.T, near, chips)
    blocks = pltpu.VMEM((count, rows, 3 * inner // count), BF16)
    (mine,) = call(
        functools.partial(temporal_kernel, places, chips, group),
        [shape((rows, width + inner))],
        [near, far, wo_temporal, *weights],
        [held(width)] + [wide] * 4 + [attended, blocks],
        small=True,
    )
    other = flip(mine, "seq", 1)
    back = [shape((per_chip, width + inner))] * chips
    if n_dp == 4 and n_seq == peers:
        size = inner // n_seq
        *back, keep, send_x, send_y = call(
            functools.partial(return_kernel, chips, block, inner, width),
            back
            + [shape((n_dp, size, width), F32)]
            + [shape((2, size, width))] * 2,
            [mine, other, near, far],
            [
                pltpu.VMEM((n_seq, 2 * rows, size), BF16),
                pltpu.VMEM((n_dp, 2 * rows, width // n_dp), BF16),
                pltpu.VMEM((per_chip, width + inner), BF16),
                sems(1),
            ],
            far_out=range(1),
            small=True,
        )
    else:
        *back, both = call(
            functools.partial(whole_return_kernel, chips, block, inner, width),
            back + [shape((2, inner, width))],
            [mine, other, near],
            small=True,
        )
    back = from_chips(back)
    block_out, tokens_grad, qkv_grad = call(
        functools.partial(last_kernel, chips, patches),
        [shape((rows, width)), shape((rows, width)), shape((rows, 3 * inner))],
        [*back, wo_spatial, qkv_rows, spatial_p, wo_temporal, hidden],
        [held(width + inner), held(width), held(3 * inner)] + [wide] * 4 + [sems(3)],
        far_out=range(3),
        small=True,
    )
    if n_dp == 4 and n_seq == peers:
        temporal_grad, spatial_grad = reduced(keep, send_x, send_y, back[1])
    else:
        both = lax.psum_scatter(both, "seq", scatter_dimension=1, tiled=True)
        both = lax.psum_scatter(both, "dp", scatter_dimension=2, tiled=True).astype(F32)
        temporal_grad, spatial_grad = both[0], both[1]
    return (
        block_out.reshape(frames, patches, width),
        tokens_grad.reshape(frames, patches, width),
        qkv_grad.reshape(frames, patches, 3 * inner),
        spatial_grad,
        temporal_grad,
    )


def solution(mesh):
    placed = (
        P(("dp", "seq"), None, None),
        P(("dp", "seq"), None, None),
        P(),
        P(None, "dp"),
        P(),
        P(("dp", "seq"), None, None),
    )
    return jax.shard_map(
        shards,
        mesh=mesh,
        in_specs=placed,
        out_specs=(
            P(("dp", "seq"), None, None),
            P(("dp", "seq"), None, None),
            P(("dp", "seq"), None, None),
            P("seq", "dp"),
            P("seq", "dp"),
        ),
        check_vma=False,
    )
```

```python
import functools
import math

import jax
import jax.numpy as jnp
from jax import lax
from jax.experimental import pallas as pl
from jax.experimental.pallas import tpu as pltpu
from jax.sharding import PartitionSpec as P

DH = 72
FRAMES = 16
LANES = 128
BF16 = jnp.bfloat16
F32 = jnp.float32
VMEM = pl.BlockSpec(memory_space=pltpu.VMEM)
SMEM = pl.BlockSpec(memory_space=pltpu.SMEM)
HBM = pl.BlockSpec(memory_space=pltpu.HBM)
PAD = 2 * LANES
LIMIT = 16 * 1024 * 1024
MOST = 60 * 1024 * 1024


def dot(left, right):
    return jnp.dot(left, right, preferred_element_type=F32)


def dot_bt(left, right):
    return lax.dot_general(left, right, (((1,), (1,)), ((), ())), preferred_element_type=F32)


def dot_at(left, right):
    return lax.dot_general(left, right, (((0,), (0,)), ((), ())), preferred_element_type=F32)


def call(body, outs, args, scratch=(), us=0, far_in=(), far_out=(), small=False):
    moved = sum(math.prod(a.shape) * a.dtype.itemsize for a in (*args, *outs))
    near = [SMEM if a.dtype == jnp.int32 else VMEM for a in args]
    return pl.pallas_call(
        body,
        out_shape=outs,
        in_specs=[HBM if i in far_in else spec for i, spec in enumerate(near)],
        out_specs=[
            HBM if i in far_out else SMEM if out.dtype == jnp.int32 else VMEM
            for i, out in enumerate(outs)
        ],
        scratch_shapes=list(scratch),
        compiler_params=pltpu.CompilerParams(vmem_limit_bytes=LIMIT if small else MOST),
        cost_estimate=pl.CostEstimate(
            flops=us * 1150000000, bytes_accessed=moved if us else 0, transcendentals=0
        ),
    )(*args)


def started(pairs, sems):
    copies = [pltpu.make_async_copy(a, b, sems.at[i]) for i, (a, b) in enumerate(pairs)]
    for copy in copies:
        copy.start()
    return copies


def shape(dims, dtype=BF16):
    return jax.ShapeDtypeStruct(dims, dtype)


TOKEN = shape((1,), jnp.int32)


def window(head):
    low = head * DH // LANES * LANES
    high = -(-(head + 1) * DH // LANES) * LANES
    return low, high


def head_only(block, head):
    low, high = window(head)
    lane = lax.broadcasted_iota(jnp.int32, (1, high - low), 1) + low
    keep = (lane >= head * DH) & (lane < (head + 1) * DH)
    return jnp.where(keep, block, jnp.zeros_like(block))


def add_tiles(tiles, head, value):
    low, high = window(head)
    for at in range(low // LANES, high // LANES):
        part = value[:, at * LANES - low : (at + 1) * LANES - low]
        tiles[at] = part if tiles[at] is None else tiles[at] + part


def joined(tiles):
    return jnp.concatenate([tile.astype(BF16) for tile in tiles], axis=1)


def same_group(rows, kind):
    row = lax.broadcasted_iota(jnp.int32, (rows, rows), 0)
    col = lax.broadcasted_iota(jnp.int32, (rows, rows), 1)
    how, size = kind
    return row // size == col // size if how == "block" else row % size == col % size


def softmax_forward(q_ref, k_ref, v_ref, p_ref, heads, kind):
    rows = q_ref.shape[0]
    mask = same_group(rows, kind)
    tiles = [None] * (q_ref.shape[1] // LANES)
    for head in range(heads):
        low, high = window(head)
        s = dot_bt(q_ref[:, low:high], head_only(k_ref[:, low:high], head)) * (1.0 / math.sqrt(DH))
        s = jnp.where(mask, s, -jnp.inf)
        e = jnp.exp(s - jnp.max(s, axis=1, keepdims=True))
        p = e / jnp.sum(e, axis=1, keepdims=True)
        p_ref[head] = p
        add_tiles(tiles, head, dot(p.astype(BF16), head_only(v_ref[:, low:high], head)))
    return joined(tiles)


def softmax_backward(q_ref, k_ref, v_ref, g_ref, p_ref, heads):
    count = q_ref.shape[1] // LANES
    dq, dk, dv = [None] * count, [None] * count, [None] * count
    for head in range(heads):
        low, high = window(head)
        p = p_ref[head]
        g = head_only(g_ref[:, low:high], head)
        add_tiles(dv, head, dot_at(p.astype(BF16), g))
        dp = dot_bt(g, v_ref[:, low:high])
        ds = p * (dp - jnp.sum(p * dp, axis=1, keepdims=True)) * (1.0 / math.sqrt(DH))
        ds = ds.astype(BF16)
        add_tiles(dq, head, dot(ds, head_only(k_ref[:, low:high], head)))
        add_tiles(dk, head, dot_at(ds, head_only(q_ref[:, low:high], head)))
    return joined(dq), joined(dk), joined(dv)


def put(ref, value):
    width = value.shape[1]
    ref[:, width // LANES * LANES :] = jnp.zeros(
        (ref.shape[0], ref.shape[1] - width // LANES * LANES), ref.dtype
    )
    ref[:, :width] = value


def place(chips):
    seq = lax.axis_index("seq")
    return lax.axis_index("dp"), seq % 2, seq % (2 * chips) // 2, seq


def spatial_kernel(chips, patches, *refs):
    idx = place(chips)
    far, outs, refs = refs[:4], refs[4 : 4 + chips], refs[4 + chips :]
    hid_far, p_far, tok, cot, qkv, wos, held, hid, p_ref, qs, ks, vs, sems = refs
    inner, width = wos.shape
    count, block, _ = held.shape
    loads = started(zip(far, (qkv, tok, wos, cot)), sems)
    loads[0].wait()
    x = qkv[...]
    put(qs, x[:, :inner])
    put(ks, x[:, inner : 2 * inner])
    put(vs, x[:, 2 * inner :])
    o = softmax_forward(qs, ks, vs, p_ref, inner // DH, ("block", patches))[:, :inner]
    stores = started([(p_ref, p_far)], sems.at[pl.ds(4, 1)])
    for at in range(3):
        loads[1 + at].wait()
    hid[...] = (tok[...].astype(F32) + dot(o, wos[...])).astype(BF16)
    for at in range(count):
        rows = slice(at * block, (at + 1) * block)
        held[at, :, :width] = hid[rows]
        held[at, :, width : 2 * width] = cot[rows]
        held[at, :, 2 * width : 2 * width + inner] = o[rows]
    stores += started([(hid, hid_far)], sems.at[pl.ds(5, 1)])
    for q in range(chips):
        for f in range(count // chips):
            rows = slice(f * block, (f + 1) * block)
            outs[q][rows] = held[f * chips + (idx[2] ^ q)]
    for copy in stores:
        copy.wait()


def own_patches(ref, core, block):
    rows, width = ref.shape
    value = ref[...].astype(F32).reshape(rows // block, block, width)
    value = jnp.where(core == 0, value[:, : block // 2], value[:, block // 2 :])
    return value.reshape(rows // 2, width)


def all_patches(mine, other, core, block):
    rows, width = mine.shape
    mine = mine.astype(F32).reshape(2 * rows // block, block // 2, width)
    other = other.astype(F32).reshape(2 * rows // block, block // 2, width)
    first, second = jnp.where(core == 0, mine, other), jnp.where(core == 0, other, mine)
    return jnp.concatenate([first, second], axis=1).reshape(2 * rows, width).astype(BF16)


def half_kernel(chips, got, own, half, kept):
    rows = half.shape[0]
    core = place(chips)[1]
    half[...] = jnp.where(core == 0, got[:rows].astype(F32), got[rows:].astype(F32)).astype(BF16)
    kept[...] = own[...]


def join_rows_kernel(*refs):
    out, low = refs[-1], 0
    for ref in refs[:-1]:
        out[low : low + ref.shape[0], : ref.shape[1]] = ref[...]
        low += ref.shape[0]


def temporal_kernel(shards, chips, group, near, far, wot, *refs):
    idx = place(chips)
    weights, refs = refs[: len(shards)], refs[len(shards) :]
    (mine, *outs), (cot, q, k, v, g, p_ref, blocks) = refs[:chips], refs[chips:]
    inner, width = wot.shape
    heads = inner // DH
    value = [own_patches(ref, idx[1], 2 * group) for ref in (near, far)]
    value = jnp.concatenate(value, axis=0).astype(BF16)
    hidden = value[:, :width]
    cot[...] = value[:, width : 2 * width]
    size = blocks.shape[2]
    for at, w in zip(shards, weights):
        value = dot_bt(hidden, w[...]).astype(BF16)
        for i, block in enumerate(at(idx)):
            blocks[block] = value[:, i * size : (i + 1) * size]
    whole = jnp.concatenate([blocks[i] for i in range(blocks.shape[0])], axis=1)
    put(q, whole[:, :inner])
    put(k, whole[:, inner : 2 * inner])
    put(v, whole[:, 2 * inner :])
    mine[:, width:] = softmax_forward(q, k, v, p_ref, heads, ("cycle", group))[:, :inner]
    put(g, dot_bt(cot[...], wot[...]).astype(BF16))
    dq, dk, dv = softmax_backward(q, k, v, g, p_ref, heads)
    whole = jnp.concatenate([dq[:, :inner], dk[:, :inner], dv[:, :inner]], axis=1)
    for i in range(blocks.shape[0]):
        blocks[i] = whole[:, i * size : (i + 1) * size]
    grad = jnp.zeros(cot.shape, F32)
    for at, w in zip(shards, weights):
        lhs = jnp.concatenate([blocks[block] for block in at(idx)], axis=1)
        grad += dot(lhs, w[...])
    mine[:, :width] = (cot[...].astype(F32) + grad.astype(BF16).astype(F32)).astype(BF16)
    half = mine.shape[0] // 2
    rows = half // chips
    for q, out in enumerate(outs, 1):
        out[:rows] = mine[q * rows : (q + 1) * rows]
        out[rows:] = mine[half + q * rows : half + (q + 1) * rows]


def others_kernel(mine, *refs):
    parts, out = refs[:-1], refs[-1]
    half = mine.shape[0] // 2
    rows = half // (1 + len(parts))
    out[:rows] = mine[half : half + rows]
    for q, part in enumerate(parts, 1):
        out[q * rows : (q + 1) * rows] = part[rows:]


def whole_parts_kernel(chips, block, inner, width, mine, other, *refs):
    idx = place(chips)
    held, part = refs
    cot, so = held[:, width : 2 * width], held[:, 2 * width : 2 * width + inner]
    half = mine.shape[0] // 2
    near = all_patches(mine[:half], other[half:], idx[1], block)
    part[0] = dot_at(near[:, width:], cot).astype(BF16)
    part[1] = dot_at(so, near[:, :width]).astype(BF16)


def parts_kernel(chips, block, inner, width, mine, other, *refs):
    idx = place(chips)
    sent, refs = refs[:2], refs[2:]
    keep, send_x, send_y, heads, cols = refs
    half = mine.shape[0] // 2
    near = all_patches(mine[:half], other[half:], idx[1], block)
    far = all_patches(mine[half:], other[:half], idx[1], block)
    rows = near.shape[0]
    size = heads.shape[2]
    count, _, wide = cols.shape
    for i in range(2):
        if i == 0:
            lefts = [near[:, width:], far[:, width:]]
            rights = [part[:, width : 2 * width] for part in sent]
        else:
            lefts = [part[:, 2 * width : 2 * width + inner] for part in sent]
            rights = [near[:, :width], far[:, :width]]
        for at in range(2):
            held = slice(at * rows, (at + 1) * rows)
            for h in range(heads.shape[0]):
                heads[h, held] = lefts[at][:, h * size : (h + 1) * size]
            for r in range(count):
                cols[r, held] = rights[at][:, r * wide : (r + 1) * wide]
        left = jnp.concatenate([heads[idx[3] ^ (2 * q)] for q in range(chips)], axis=1)
        first = 1 if i == 0 else 2
        for r in range(count):
            full = dot_at(left, cols[idx[0] ^ r])
            value = jnp.concatenate([full[q * size : (q + 1) * size] for q in range(chips)], axis=1)
            if r & first:
                (send_x, send_y)[i][r // 2 if i == 0 else r - 2] = value.astype(BF16)
            else:
                keep[2 * i + (r > 0)] = value


def sum_first_kernel(keep, got_x, got_y, own, send_y, send_x):
    for i, (got, send) in enumerate(((got_x, send_y), (got_y, send_x))):
        own[i] = keep[2 * i] + got[0].astype(F32)
        send[...] = (keep[2 * i + 1] + got[1].astype(F32)).astype(BF16)


def sum_second_kernel(own, got_y, got_x, kept, *outs):
    totals = [own[0] + got_y[...].astype(F32), own[1] + got_x[...].astype(F32)]
    size = totals[0].shape[1] // (1 + len(outs))
    for q, out in enumerate((kept, *outs)):
        cut = [total[:, q * size : (q + 1) * size] for total in totals]
        out[...] = jnp.concatenate(cut, axis=1).astype(out.dtype)


def sum_kernel(own, *refs):
    got, outs = refs[:-2], refs[-2:]
    total = own[...]
    for part in got:
        total += part[...].astype(F32)
    size = outs[0].shape[1]
    for i, out in enumerate(outs):
        out[...] = total[:, i * size : (i + 1) * size]


def last_kernel(chips, patches, *refs):
    idx = place(chips)
    held, got, refs = refs[:chips], refs[chips], refs[chips + 1 :]
    (wos, qkv, p_ref, wot, hid), refs = refs[:5], refs[5:]
    block_far, out_far, grads_far, rows, block_out, grads, qs, ks, vs, gs, sems = refs
    inner, width = wos.shape
    frames = rows.shape[0] // patches
    block = patches // chips
    each = frames * block // 2
    for q in range(chips):
        value = all_patches(held[q][:each], got[q * each : (q + 1) * each], idx[1], block)
        for f in range(frames):
            low = pl.multiple_of(f * patches + (idx[2] ^ q) * block, block)
            rows[pl.ds(low, block)] = value[f * block : (f + 1) * block]
    value = rows[...]
    grad, attended = value[:, :width], value[:, width:]
    stores = started([(rows.at[:, pl.ds(0, width)], out_far)], sems.at[pl.ds(0, 1)])
    block_out[...] = (hid[...].astype(F32) + dot(attended, wot[...])).astype(BF16)
    stores += started([(block_out, block_far)], sems.at[pl.ds(1, 1)])
    put(gs, dot_bt(grad, wos[...]).astype(BF16))
    x = qkv[...]
    put(qs, x[:, :inner])
    put(ks, x[:, inner : 2 * inner])
    put(vs, x[:, 2 * inner :])
    dq, dk, dv = softmax_backward(qs, ks, vs, gs, p_ref, inner // DH)
    grads[...] = jnp.concatenate([dq[:, :inner], dk[:, :inner], dv[:, :inner]], axis=1)
    stores += started([(grads, grads_far)], sems.at[pl.ds(2, 1)])
    for copy in stores:
        copy.wait()


def flip(value, axis, bit):
    return lax.ppermute(value, axis, [(i, i ^ bit) for i in range(lax.axis_size(axis))])


def sems(n):
    return pltpu.SemaphoreType.DMA((n,))


def across(value, bits):
    n = lax.axis_size("seq")
    pairs = [
        (d * n + i, (d ^ bits[i % 2]) * n + i) for d in range(lax.axis_size("dp")) for i in range(n)
    ]
    return lax.ppermute(value, ("dp", "seq"), pairs)


def gather(weight, parts, chips):
    n = lax.axis_size("dp")
    rows, sent = parts[0].shape
    whole = [shape((len(parts) * rows, sent + PAD))]
    if n != 4:
        (near,) = call(join_rows_kernel, whole, from_chips(parts), small=True)
        weights = [lax.all_gather(weight, "dp", axis=0, tiled=True)]
        return near, flip(near, "seq", 1), weights, [lambda idx: [0]], 1
    half, width = weight.shape[0] // 2, weight.shape[1]
    side = across(weight, (1, 2))
    corner, own = call(
        functools.partial(half_kernel, chips),
        [shape((half, width)), shape((rows, sent))],
        [side, parts[0]],
        small=True,
    )
    corner = across(corner, (2, 1))
    (near,) = call(join_rows_kernel, whole, [own, *from_chips(parts)[1:]], small=True)
    weights = [weight, side, flip(side, "seq", 1), corner, flip(corner, "seq", 1)]

    def both(shard):
        return lambda idx: [2 * shard(idx), 2 * shard(idx) + 1]

    shards = [
        both(lambda idx: idx[0]),
        both(lambda idx: idx[0] ^ (1 + idx[1])),
        both(lambda idx: idx[0] ^ (2 - idx[1])),
        lambda idx: [2 * (idx[0] ^ 3) + idx[1]],
        lambda idx: [2 * (idx[0] ^ 3) + 1 - idx[1]],
    ]
    return near, flip(near, "seq", 1), weights, shards, 2 * n


def from_chips(parts):
    return [parts[0]] + [flip(parts[q], "seq", 2 * q) for q in range(1, len(parts))]


def reduced(keep, send_x, send_y):
    _, size, width = keep.shape
    step = shape((size, width))
    own, send_t, send_s = call(
        sum_first_kernel,
        [shape((2, size, width), F32), step, step],
        [keep, flip(send_x, "dp", 1), flip(send_y, "dp", 2)],
        small=True,
    )
    n = lax.axis_size("seq") // 2
    block = (size, 2 * width // n)
    own, *sends = call(
        sum_second_kernel,
        [shape(block, F32)] + [shape(block)] * (n - 1),
        [own, flip(send_t, "dp", 2), flip(send_s, "dp", 1)],
        small=True,
    )
    got = [flip(value, "seq", 2 * (q + 1)) for q, value in enumerate(sends)]
    return call(sum_kernel, [shape((size, width // n), F32)] * 2, [own, *got], small=True)


def shards(tokens, spatial_qkv, wo_spatial, w_temporal, wo_temporal, cotangent):
    frames, patches, width = tokens.shape
    inner = wo_spatial.shape[0]
    heads = inner // DH
    padded = -(-inner // LANES) * LANES
    rows = frames * patches
    peers = FRAMES // frames
    chips = peers // 2
    group = patches // peers
    block = 2 * group
    n_dp, n_seq = lax.axis_size("dp"), lax.axis_size("seq")

    def held(columns, dtype=BF16):
        return pltpu.VMEM((rows, columns), dtype)

    wide = held(padded)
    attended = pltpu.VMEM((heads, rows, rows), F32)
    projection = pltpu.VMEM((inner, width), BF16)
    per_chip = rows // chips
    qkv_rows = spatial_qkv.reshape(rows, 3 * inner)
    sent = -(-(2 * width + inner) // LANES) * LANES
    *near, hidden, spatial_p = call(
        functools.partial(spatial_kernel, chips, patches),
        [shape((per_chip, sent))] * chips
        + [shape((rows, width)), shape((heads, rows, rows), F32)],
        [qkv_rows, tokens.reshape(rows, width), wo_spatial, cotangent.reshape(rows, width)],
        [held(width), held(width), held(3 * inner), projection]
        + [pltpu.VMEM((frames * chips, block, sent), BF16), held(width), attended]
        + [wide] * 3
        + [sems(6)],
        far_in=range(4),
        far_out=(chips, chips + 1),
    )
    near, far, weights, places, count = gather(w_temporal.T, near, chips)
    blocks = pltpu.VMEM((count, rows, 3 * inner // count), BF16)
    mine, *back = call(
        functools.partial(temporal_kernel, places, chips, group),
        [shape((rows, width + inner))] + [shape((per_chip, width + inner))] * (chips - 1),
        [near, far, wo_temporal, *weights],
        [held(width)] + [wide] * 4 + [attended, blocks],
        small=True,
    )
    other = flip(mine, "seq", 1)
    if n_dp == 4 and n_seq == peers:
        size = inner // n_seq
        keep, send_x, send_y = call(
            functools.partial(parts_kernel, chips, block, inner, width),
            [shape((n_dp, size, width), F32)] + [shape((2, size, width))] * 2,
            [mine, other, near, far],
            [
                pltpu.VMEM((n_seq, 2 * rows, size), BF16),
                pltpu.VMEM((n_dp, 2 * rows, width // n_dp), BF16),
            ],
            small=True,
        )
    else:
        (both,) = call(
            functools.partial(whole_parts_kernel, chips, block, inner, width),
            [shape((2, inner, width))],
            [mine, other, near],
            small=True,
        )
    back = from_chips([mine, *back])
    (others,) = call(
        others_kernel, [shape((rows // 2, width + inner))], back, small=True
    )
    block_out, tokens_grad, qkv_grad = call(
        functools.partial(last_kernel, chips, patches),
        [shape((rows, width)), shape((rows, width)), shape((rows, 3 * inner))],
        [*back, flip(others, "seq", 1), wo_spatial, qkv_rows, spatial_p, wo_temporal, hidden],
        [held(width + inner), held(width), held(3 * inner)] + [wide] * 4 + [sems(3)],
        far_out=range(3),
        small=True,
    )
    if n_dp == 4 and n_seq == peers:
        temporal_grad, spatial_grad = reduced(keep, send_x, send_y)
    else:
        both = lax.psum_scatter(both, "seq", scatter_dimension=1, tiled=True)
        both = lax.psum_scatter(both, "dp", scatter_dimension=2, tiled=True).astype(F32)
        temporal_grad, spatial_grad = both[0], both[1]
    return (
        block_out.reshape(frames, patches, width),
        tokens_grad.reshape(frames, patches, width),
        qkv_grad.reshape(frames, patches, 3 * inner),
        spatial_grad,
        temporal_grad,
    )


def solution(mesh):
    placed = (
        P(("dp", "seq"), None, None),
        P(("dp", "seq"), None, None),
        P(),
        P(None, "dp"),
        P(),
        P(("dp", "seq"), None, None),
    )
    return jax.shard_map(
        shards,
        mesh=mesh,
        in_specs=placed,
        out_specs=(
            P(("dp", "seq"), None, None),
            P(("dp", "seq"), None, None),
            P(("dp", "seq"), None, None),
            P("seq", "dp"),
            P("seq", "dp"),
        ),
        check_vma=False,
    )
```

```python
import functools
import math

import jax
import jax.numpy as jnp
from jax import lax
from jax.experimental import pallas as pl
from jax.experimental.pallas import tpu as pltpu
from jax.sharding import PartitionSpec as P

DH = 72
FRAMES = 16
LANES = 128
BF16 = jnp.bfloat16
F32 = jnp.float32
VMEM = pl.BlockSpec(memory_space=pltpu.VMEM)
SMEM = pl.BlockSpec(memory_space=pltpu.SMEM)
HBM = pl.BlockSpec(memory_space=pltpu.HBM)
PAD = 2 * LANES
LIMIT = 16 * 1024 * 1024
MOST = 60 * 1024 * 1024


def dot(left, right):
    return jnp.dot(left, right, preferred_element_type=F32)


def dot_bt(left, right):
    return lax.dot_general(left, right, (((1,), (1,)), ((), ())), preferred_element_type=F32)


def dot_at(left, right):
    return lax.dot_general(left, right, (((0,), (0,)), ((), ())), preferred_element_type=F32)


def call(body, outs, args, scratch=(), us=0, far_in=(), far_out=(), small=False):
    moved = sum(math.prod(a.shape) * a.dtype.itemsize for a in (*args, *outs))
    near = [SMEM if a.dtype == jnp.int32 else VMEM for a in args]
    return pl.pallas_call(
        body,
        out_shape=outs,
        in_specs=[HBM if i in far_in else spec for i, spec in enumerate(near)],
        out_specs=[
            HBM if i in far_out else SMEM if out.dtype == jnp.int32 else VMEM
            for i, out in enumerate(outs)
        ],
        scratch_shapes=list(scratch),
        compiler_params=pltpu.CompilerParams(vmem_limit_bytes=LIMIT if small else MOST),
        cost_estimate=pl.CostEstimate(
            flops=us * 1150000000, bytes_accessed=moved if us else 0, transcendentals=0
        ),
    )(*args)


def started(pairs, sems):
    copies = [pltpu.make_async_copy(a, b, sems.at[i]) for i, (a, b) in enumerate(pairs)]
    for copy in copies:
        copy.start()
    return copies


def shape(dims, dtype=BF16):
    return jax.ShapeDtypeStruct(dims, dtype)


TOKEN = shape((1,), jnp.int32)


def window(head):
    low = head * DH // LANES * LANES
    high = -(-(head + 1) * DH // LANES) * LANES
    return low, high


def head_only(block, head):
    low, high = window(head)
    lane = lax.broadcasted_iota(jnp.int32, (1, high - low), 1) + low
    keep = (lane >= head * DH) & (lane < (head + 1) * DH)
    return jnp.where(keep, block, jnp.zeros_like(block))


def add_tiles(tiles, head, value):
    low, high = window(head)
    for at in range(low // LANES, high // LANES):
        part = value[:, at * LANES - low : (at + 1) * LANES - low]
        tiles[at] = part if tiles[at] is None else tiles[at] + part


def joined(tiles):
    return jnp.concatenate([tile.astype(BF16) for tile in tiles], axis=1)


def same_group(rows, kind):
    row = lax.broadcasted_iota(jnp.int32, (rows, rows), 0)
    col = lax.broadcasted_iota(jnp.int32, (rows, rows), 1)
    how, size = kind
    return row // size == col // size if how == "block" else row % size == col % size


def softmax_forward(q_ref, k_ref, v_ref, p_ref, heads, kind):
    rows = q_ref.shape[0]
    mask = same_group(rows, kind)
    tiles = [None] * (q_ref.shape[1] // LANES)
    for head in range(heads):
        low, high = window(head)
        s = dot_bt(q_ref[:, low:high], head_only(k_ref[:, low:high], head)) * (1.0 / math.sqrt(DH))
        s = jnp.where(mask, s, -jnp.inf)
        e = jnp.exp(s - jnp.max(s, axis=1, keepdims=True))
        p = e / jnp.sum(e, axis=1, keepdims=True)
        p_ref[head] = p
        add_tiles(tiles, head, dot(p.astype(BF16), head_only(v_ref[:, low:high], head)))
    return joined(tiles)


def softmax_backward(q_ref, k_ref, v_ref, g_ref, p_ref, heads):
    count = q_ref.shape[1] // LANES
    dq, dk, dv = [None] * count, [None] * count, [None] * count
    for head in range(heads):
        low, high = window(head)
        p = p_ref[head]
        g = head_only(g_ref[:, low:high], head)
        add_tiles(dv, head, dot_at(p.astype(BF16), g))
        dp = dot_bt(g, v_ref[:, low:high])
        ds = p * (dp - jnp.sum(p * dp, axis=1, keepdims=True)) * (1.0 / math.sqrt(DH))
        ds = ds.astype(BF16)
        add_tiles(dq, head, dot(ds, head_only(k_ref[:, low:high], head)))
        add_tiles(dk, head, dot_at(ds, head_only(q_ref[:, low:high], head)))
    return joined(dq), joined(dk), joined(dv)


def put(ref, value):
    width = value.shape[1]
    ref[:, width // LANES * LANES :] = jnp.zeros(
        (ref.shape[0], ref.shape[1] - width // LANES * LANES), ref.dtype
    )
    ref[:, :width] = value


def place(chips):
    seq = lax.axis_index("seq")
    return lax.axis_index("dp"), seq % 2, seq % (2 * chips) // 2, seq


def spatial_kernel(chips, patches, *refs):
    idx = place(chips)
    far, outs, refs = refs[:4], refs[4 : 4 + chips], refs[4 + chips :]
    hid_far, p_far, tok, cot, qkv, wos, held, hid, p_ref, qs, ks, vs, sems = refs
    inner, width = wos.shape
    count, block, _ = held.shape
    loads = started(zip(far, (qkv, tok, wos, cot)), sems)
    loads[0].wait()
    x = qkv[...]
    put(qs, x[:, :inner])
    put(ks, x[:, inner : 2 * inner])
    put(vs, x[:, 2 * inner :])
    o = softmax_forward(qs, ks, vs, p_ref, inner // DH, ("block", patches))[:, :inner]
    stores = started([(p_ref, p_far)], sems.at[pl.ds(4, 1)])
    for at in range(3):
        loads[1 + at].wait()
    hid[...] = (tok[...].astype(F32) + dot(o, wos[...])).astype(BF16)
    for at in range(count):
        rows = slice(at * block, (at + 1) * block)
        held[at, :, :width] = hid[rows]
        held[at, :, width : 2 * width] = cot[rows]
        held[at, :, 2 * width : 2 * width + inner] = o[rows]
    stores += started([(hid, hid_far)], sems.at[pl.ds(5, 1)])
    for q in range(chips):
        for f in range(count // chips):
            rows = slice(f * block, (f + 1) * block)
            outs[q][rows] = held[f * chips + (idx[2] ^ q)]
    for copy in stores:
        copy.wait()


def own_patches(ref, core, block):
    rows, width = ref.shape
    value = ref[...].astype(F32).reshape(rows // block, block, width)
    value = jnp.where(core == 0, value[:, : block // 2], value[:, block // 2 :])
    return value.reshape(rows // 2, width)


def all_patches(mine, other, core, block):
    rows, width = mine.shape
    mine = mine.astype(F32).reshape(2 * rows // block, block // 2, width)
    other = other.astype(F32).reshape(2 * rows // block, block // 2, width)
    first, second = jnp.where(core == 0, mine, other), jnp.where(core == 0, other, mine)
    return jnp.concatenate([first, second], axis=1).reshape(2 * rows, width).astype(BF16)


def half_kernel(chips, got, own, half, kept):
    rows = half.shape[0]
    core = place(chips)[1]
    half[...] = jnp.where(core == 0, got[:rows].astype(F32), got[rows:].astype(F32)).astype(BF16)
    kept[...] = own[...]


def join_rows_kernel(*refs):
    out, low = refs[-1], 0
    for ref in refs[-2::-1]:
        out[low : low + ref.shape[0], : ref.shape[1]] = ref[...]
        low += ref.shape[0]


def temporal_kernel(shards, chips, group, near, far, wot, *refs):
    idx = place(chips)
    weights, refs = refs[: len(shards)], refs[len(shards) :]
    (mine, *outs), (cot, q, k, v, g, p_ref, blocks) = refs[:chips], refs[chips:]
    inner, width = wot.shape
    heads = inner // DH
    value = [own_patches(ref, idx[1], 2 * group) for ref in (near, far)]
    value = jnp.concatenate(value, axis=0).astype(BF16)
    hidden = value[:, :width]
    cot[...] = value[:, width : 2 * width]
    size = blocks.shape[2]
    for at, w in zip(shards, weights):
        value = dot_bt(hidden, w[...]).astype(BF16)
        for i, block in enumerate(at(idx)):
            blocks[block] = value[:, i * size : (i + 1) * size]
    whole = jnp.concatenate([blocks[i] for i in range(blocks.shape[0])], axis=1)
    put(q, whole[:, :inner])
    put(k, whole[:, inner : 2 * inner])
    put(v, whole[:, 2 * inner :])
    mine[:, width:] = softmax_forward(q, k, v, p_ref, heads, ("cycle", group))[:, :inner]
    put(g, dot_bt(cot[...], wot[...]).astype(BF16))
    dq, dk, dv = softmax_backward(q, k, v, g, p_ref, heads)
    whole = jnp.concatenate([dq[:, :inner], dk[:, :inner], dv[:, :inner]], axis=1)
    for i in range(blocks.shape[0]):
        blocks[i] = whole[:, i * size : (i + 1) * size]
    grad = jnp.zeros(cot.shape, F32)
    for at, w in zip(shards, weights):
        lhs = jnp.concatenate([blocks[block] for block in at(idx)], axis=1)
        grad += dot(lhs, w[...])
    mine[:, :width] = (cot[...].astype(F32) + grad.astype(BF16).astype(F32)).astype(BF16)
    half = mine.shape[0] // 2
    rows = half // chips
    for q, out in enumerate(outs, 1):
        out[:rows] = mine[q * rows : (q + 1) * rows]
        out[rows:] = mine[half + q * rows : half + (q + 1) * rows]


def others_kernel(mine, *refs):
    parts, out = refs[-2::-1], refs[-1]
    half = mine.shape[0] // 2
    rows = half // (1 + len(parts))
    out[:rows] = mine[half : half + rows]
    for q, part in enumerate(parts, 1):
        out[q * rows : (q + 1) * rows] = part[rows:]


def whole_parts_kernel(chips, block, inner, width, mine, other, *refs):
    idx = place(chips)
    held, part = refs
    cot, so = held[:, width : 2 * width], held[:, 2 * width : 2 * width + inner]
    half = mine.shape[0] // 2
    near = all_patches(mine[:half], other[half:], idx[1], block)
    part[0] = dot_at(near[:, width:], cot).astype(BF16)
    part[1] = dot_at(so, near[:, :width]).astype(BF16)


def parts_kernel(chips, block, inner, width, mine, other, *refs):
    idx = place(chips)
    sent, refs = refs[:2], refs[2:]
    keep, send_x, send_y, heads, cols = refs
    half = mine.shape[0] // 2
    near = all_patches(mine[:half], other[half:], idx[1], block)
    far = all_patches(mine[half:], other[:half], idx[1], block)
    rows = near.shape[0]
    size = heads.shape[2]
    count, _, wide = cols.shape
    for i in range(2):
        if i == 0:
            lefts = [near[:, width:], far[:, width:]]
            rights = [part[:, width : 2 * width] for part in sent]
        else:
            lefts = [part[:, 2 * width : 2 * width + inner] for part in sent]
            rights = [near[:, :width], far[:, :width]]
        for at in range(2):
            held = slice(at * rows, (at + 1) * rows)
            for h in range(heads.shape[0]):
                heads[h, held] = lefts[at][:, h * size : (h + 1) * size]
            for r in range(count):
                cols[r, held] = rights[at][:, r * wide : (r + 1) * wide]
        left = jnp.concatenate([heads[idx[3] ^ (2 * q)] for q in range(chips)], axis=1)
        first = 1 if i == 0 else 2
        for r in range(count):
            full = dot_at(left, cols[idx[0] ^ r])
            value = jnp.concatenate([full[q * size : (q + 1) * size] for q in range(chips)], axis=1)
            if r & first:
                (send_x, send_y)[i][r // 2 if i == 0 else r - 2] = value.astype(BF16)
            else:
                keep[2 * i + (r > 0)] = value


def sum_first_kernel(keep, got_x, got_y, own, send_y, send_x):
    for i, (got, send) in enumerate(((got_x, send_y), (got_y, send_x))):
        own[i] = keep[2 * i] + got[0].astype(F32)
        send[...] = (keep[2 * i + 1] + got[1].astype(F32)).astype(BF16)


def sum_second_kernel(own, got_y, got_x, kept, *outs):
    totals = [own[0] + got_y[...].astype(F32), own[1] + got_x[...].astype(F32)]
    size = totals[0].shape[1] // (1 + len(outs))
    for q, out in enumerate((kept, *outs)):
        cut = [total[:, q * size : (q + 1) * size] for total in totals]
        out[...] = jnp.concatenate(cut, axis=1).astype(out.dtype)


def sum_kernel(own, *refs):
    got, outs = refs[:-2], refs[-2:]
    total = own[...]
    for part in got:
        total += part[...].astype(F32)
    size = outs[0].shape[1]
    for i, out in enumerate(outs):
        out[...] = total[:, i * size : (i + 1) * size]


def last_kernel(chips, patches, *refs):
    idx = place(chips)
    held, got, refs = refs[:chips][::-1], refs[chips], refs[chips + 1 :]
    (wos, qkv, p_ref, wot, hid), refs = refs[:5], refs[5:]
    block_far, out_far, grads_far, rows, block_out, grads, qs, ks, vs, gs, sems = refs
    inner, width = wos.shape
    frames = rows.shape[0] // patches
    block = patches // chips
    each = frames * block // 2
    for q in range(chips):
        value = all_patches(held[q][:each], got[q * each : (q + 1) * each], idx[1], block)
        for f in range(frames):
            low = pl.multiple_of(f * patches + (idx[2] ^ q) * block, block)
            rows[pl.ds(low, block)] = value[f * block : (f + 1) * block]
    value = rows[...]
    grad, attended = value[:, :width], value[:, width:]
    stores = started([(rows.at[:, pl.ds(0, width)], out_far)], sems.at[pl.ds(0, 1)])
    block_out[...] = (hid[...].astype(F32) + dot(attended, wot[...])).astype(BF16)
    stores += started([(block_out, block_far)], sems.at[pl.ds(1, 1)])
    put(gs, dot_bt(grad, wos[...]).astype(BF16))
    x = qkv[...]
    put(qs, x[:, :inner])
    put(ks, x[:, inner : 2 * inner])
    put(vs, x[:, 2 * inner :])
    dq, dk, dv = softmax_backward(qs, ks, vs, gs, p_ref, inner // DH)
    grads[...] = jnp.concatenate([dq[:, :inner], dk[:, :inner], dv[:, :inner]], axis=1)
    stores += started([(grads, grads_far)], sems.at[pl.ds(2, 1)])
    for copy in stores:
        copy.wait()


def flip(value, axis, bit):
    return lax.ppermute(value, axis, [(i, i ^ bit) for i in range(lax.axis_size(axis))])


def sems(n):
    return pltpu.SemaphoreType.DMA((n,))


def across(value, bits):
    n = lax.axis_size("seq")
    pairs = [
        (d * n + i, (d ^ bits[i % 2]) * n + i) for d in range(lax.axis_size("dp")) for i in range(n)
    ]
    return lax.ppermute(value, ("dp", "seq"), pairs)


def gather(weight, parts, chips):
    n = lax.axis_size("dp")
    rows, sent = parts[0].shape
    whole = [shape((len(parts) * rows, sent + PAD))]
    if n != 4:
        (near,) = call(join_rows_kernel, whole, from_chips(parts)[::-1], small=True)
        weights = [lax.all_gather(weight, "dp", axis=0, tiled=True)]
        return near, flip(near, "seq", 1), weights, [lambda idx: [0]], 1
    half, width = weight.shape[0] // 2, weight.shape[1]
    side = across(weight, (1, 2))
    corner, own = call(
        functools.partial(half_kernel, chips),
        [shape((half, width)), shape((rows, sent))],
        [side, parts[0]],
        small=True,
    )
    corner = across(corner, (2, 1))
    (near,) = call(join_rows_kernel, whole, [*from_chips(parts)[:0:-1], own], small=True)
    weights = [weight, side, flip(side, "seq", 1), corner, flip(corner, "seq", 1)]

    def both(shard):
        return lambda idx: [2 * shard(idx), 2 * shard(idx) + 1]

    shards = [
        both(lambda idx: idx[0]),
        both(lambda idx: idx[0] ^ (1 + idx[1])),
        both(lambda idx: idx[0] ^ (2 - idx[1])),
        lambda idx: [2 * (idx[0] ^ 3) + idx[1]],
        lambda idx: [2 * (idx[0] ^ 3) + 1 - idx[1]],
    ]
    return near, flip(near, "seq", 1), weights, shards, 2 * n


def from_chips(parts):
    return [parts[0]] + [flip(parts[q], "seq", 2 * q) for q in range(1, len(parts))]


def reduced(keep, send_x, send_y):
    _, size, width = keep.shape
    step = shape((size, width))
    own, send_t, send_s = call(
        sum_first_kernel,
        [shape((2, size, width), F32), step, step],
        [keep, flip(send_x, "dp", 1), flip(send_y, "dp", 2)],
        small=True,
    )
    n = lax.axis_size("seq") // 2
    block = (size, 2 * width // n)
    own, *sends = call(
        sum_second_kernel,
        [shape(block, F32)] + [shape(block)] * (n - 1),
        [own, flip(send_t, "dp", 2), flip(send_s, "dp", 1)],
        small=True,
    )
    got = from_chips([own, *sends])[1:]
    return call(sum_kernel, [shape((size, width // n), F32)] * 2, [own, *got[::-1]], small=True)


def shards(tokens, spatial_qkv, wo_spatial, w_temporal, wo_temporal, cotangent):
    frames, patches, width = tokens.shape
    inner = wo_spatial.shape[0]
    heads = inner // DH
    padded = -(-inner // LANES) * LANES
    rows = frames * patches
    peers = FRAMES // frames
    chips = peers // 2
    group = patches // peers
    block = 2 * group
    n_dp, n_seq = lax.axis_size("dp"), lax.axis_size("seq")

    def held(columns, dtype=BF16):
        return pltpu.VMEM((rows, columns), dtype)

    wide = held(padded)
    attended = pltpu.VMEM((heads, rows, rows), F32)
    projection = pltpu.VMEM((inner, width), BF16)
    per_chip = rows // chips
    qkv_rows = spatial_qkv.reshape(rows, 3 * inner)
    sent = -(-(2 * width + inner) // LANES) * LANES
    *near, hidden, spatial_p = call(
        functools.partial(spatial_kernel, chips, patches),
        [shape((per_chip, sent))] * chips
        + [shape((rows, width)), shape((heads, rows, rows), F32)],
        [qkv_rows, tokens.reshape(rows, width), wo_spatial, cotangent.reshape(rows, width)],
        [held(width), held(width), held(3 * inner), projection]
        + [pltpu.VMEM((frames * chips, block, sent), BF16), held(width), attended]
        + [wide] * 3
        + [sems(6)],
        far_in=range(4),
        far_out=(chips, chips + 1),
    )
    near, far, weights, places, count = gather(w_temporal.T, near, chips)
    blocks = pltpu.VMEM((count, rows, 3 * inner // count), BF16)
    mine, *back = call(
        functools.partial(temporal_kernel, places, chips, group),
        [shape((rows, width + inner))] + [shape((per_chip, width + inner))] * (chips - 1),
        [near, far, wo_temporal, *weights],
        [held(width)] + [wide] * 4 + [attended, blocks],
        small=True,
    )
    other = flip(mine, "seq", 1)
    if n_dp == 4 and n_seq == peers:
        size = inner // n_seq
        keep, send_x, send_y = call(
            functools.partial(parts_kernel, chips, block, inner, width),
            [shape((n_dp, size, width), F32)] + [shape((2, size, width))] * 2,
            [mine, other, near, far],
            [
                pltpu.VMEM((n_seq, 2 * rows, size), BF16),
                pltpu.VMEM((n_dp, 2 * rows, width // n_dp), BF16),
            ],
            small=True,
        )
    else:
        (both,) = call(
            functools.partial(whole_parts_kernel, chips, block, inner, width),
            [shape((2, inner, width))],
            [mine, other, near],
            small=True,
        )
    back = from_chips([mine, *back])
    (others,) = call(
        others_kernel,
        [shape((rows // 2, width + inner))],
        [back[0], *back[:0:-1]],
        small=True,
    )
    block_out, tokens_grad, qkv_grad = call(
        functools.partial(last_kernel, chips, patches),
        [shape((rows, width)), shape((rows, width)), shape((rows, 3 * inner))],
        [*back[::-1], flip(others, "seq", 1), wo_spatial, qkv_rows, spatial_p, wo_temporal, hidden],
        [held(width + inner), held(width), held(3 * inner)] + [wide] * 4 + [sems(3)],
        far_out=range(3),
        small=True,
    )
    if n_dp == 4 and n_seq == peers:
        temporal_grad, spatial_grad = reduced(keep, send_x, send_y)
    else:
        both = lax.psum_scatter(both, "seq", scatter_dimension=1, tiled=True)
        both = lax.psum_scatter(both, "dp", scatter_dimension=2, tiled=True).astype(F32)
        temporal_grad, spatial_grad = both[0], both[1]
    return (
        block_out.reshape(frames, patches, width),
        tokens_grad.reshape(frames, patches, width),
        qkv_grad.reshape(frames, patches, 3 * inner),
        spatial_grad,
        temporal_grad,
    )


def solution(mesh):
    placed = (
        P(("dp", "seq"), None, None),
        P(("dp", "seq"), None, None),
        P(),
        P(None, "dp"),
        P(),
        P(("dp", "seq"), None, None),
    )
    return jax.shard_map(
        shards,
        mesh=mesh,
        in_specs=placed,
        out_specs=(
            P(("dp", "seq"), None, None),
            P(("dp", "seq"), None, None),
            P(("dp", "seq"), None, None),
            P("seq", "dp"),
            P("seq", "dp"),
        ),
        check_vma=False,
    )
```

```python
import functools
import math

import jax
import jax.numpy as jnp
from jax import lax
from jax.experimental import pallas as pl
from jax.experimental.pallas import tpu as pltpu
from jax.sharding import PartitionSpec as P

DH = 72
FRAMES = 16
LANES = 128
BF16 = jnp.bfloat16
F32 = jnp.float32
VMEM = pl.BlockSpec(memory_space=pltpu.VMEM)
SMEM = pl.BlockSpec(memory_space=pltpu.SMEM)
HBM = pl.BlockSpec(memory_space=pltpu.HBM)
PAD = 2 * LANES
LIMIT = 16 * 1024 * 1024
MOST = 60 * 1024 * 1024


def dot(left, right):
    return jnp.dot(left, right, preferred_element_type=F32)


def dot_bt(left, right):
    return lax.dot_general(left, right, (((1,), (1,)), ((), ())), preferred_element_type=F32)


def dot_at(left, right):
    return lax.dot_general(left, right, (((0,), (0,)), ((), ())), preferred_element_type=F32)


def call(body, outs, args, scratch=(), us=0, far_in=(), far_out=(), small=False):
    moved = sum(math.prod(a.shape) * a.dtype.itemsize for a in (*args, *outs))
    near = [SMEM if a.dtype == jnp.int32 else VMEM for a in args]
    return pl.pallas_call(
        body,
        out_shape=outs,
        in_specs=[HBM if i in far_in else spec for i, spec in enumerate(near)],
        out_specs=[
            HBM if i in far_out else SMEM if out.dtype == jnp.int32 else VMEM
            for i, out in enumerate(outs)
        ],
        scratch_shapes=list(scratch),
        compiler_params=pltpu.CompilerParams(vmem_limit_bytes=LIMIT if small else MOST),
        cost_estimate=pl.CostEstimate(
            flops=us * 1150000000, bytes_accessed=moved if us else 0, transcendentals=0
        ),
    )(*args)


def started(pairs, sems):
    copies = [pltpu.make_async_copy(a, b, sems.at[i]) for i, (a, b) in enumerate(pairs)]
    for copy in copies:
        copy.start()
    return copies


def shape(dims, dtype=BF16):
    return jax.ShapeDtypeStruct(dims, dtype)


TOKEN = shape((1,), jnp.int32)


def tile(value, head):
    piece = value[:, head * DH : (head + 1) * DH]
    return jnp.concatenate([piece, jnp.zeros((piece.shape[0], LANES - DH), piece.dtype)], axis=1)


def spread(value, ref):
    for head in range(ref.shape[0]):
        ref[head] = tile(value, head)


def joined(tiles):
    return jnp.concatenate([part[:, :DH].astype(BF16) for part in tiles], axis=1)


def same_group(rows, kind):
    row = lax.broadcasted_iota(jnp.int32, (rows, rows), 0)
    col = lax.broadcasted_iota(jnp.int32, (rows, rows), 1)
    how, size = kind
    return row // size == col // size if how == "block" else row % size == col % size


def softmax_forward(qkv, p_ref, kind):
    heads = qkv.shape[0] // 3
    mask = same_group(qkv.shape[1], kind)
    outs = []
    for head in range(heads):
        s = dot_bt(qkv[head], qkv[heads + head]) * (1.0 / math.sqrt(DH))
        s = jnp.where(mask, s, -jnp.inf)
        e = jnp.exp(s - jnp.max(s, axis=1, keepdims=True))
        p = e / jnp.sum(e, axis=1, keepdims=True)
        p_ref[head] = p
        outs.append(dot(p.astype(BF16), qkv[2 * heads + head]))
    return joined(outs)


def softmax_backward(qkv, g_ref, p_ref, grads):
    heads = qkv.shape[0] // 3
    for head in range(heads):
        p, g = p_ref[head], g_ref[head]
        grads[2 * heads + head] = dot_at(p.astype(BF16), g).astype(BF16)
        dp = dot_bt(g, qkv[2 * heads + head])
        ds = p * (dp - jnp.sum(p * dp, axis=1, keepdims=True)) * (1.0 / math.sqrt(DH))
        ds = ds.astype(BF16)
        grads[head] = dot(ds, qkv[heads + head]).astype(BF16)
        grads[heads + head] = dot_at(ds, qkv[head]).astype(BF16)


def place(chips):
    seq = lax.axis_index("seq")
    return lax.axis_index("dp"), seq % 2, seq % (2 * chips) // 2, seq


def spatial_kernel(chips, patches, *refs):
    idx = place(chips)
    far, outs, refs = refs[:4], refs[4 : 4 + chips], refs[4 + chips :]
    hid_far, p_far, tok, cot, qkv, wos, held, hid, p_ref, tiles, sems = refs
    inner, width = wos.shape
    count, block, _ = held.shape
    loads = started(zip(far, (qkv, tok, wos, cot)), sems)
    loads[0].wait()
    spread(qkv[...], tiles)
    o = softmax_forward(tiles, p_ref, ("block", patches))
    stores = started([(p_ref, p_far)], sems.at[pl.ds(4, 1)])
    for at in range(3):
        loads[1 + at].wait()
    hid[...] = (tok[...].astype(F32) + dot(o, wos[...])).astype(BF16)
    for at in range(count):
        rows = slice(at * block, (at + 1) * block)
        held[at, :, :width] = hid[rows]
        held[at, :, width : 2 * width] = cot[rows]
        held[at, :, 2 * width : 2 * width + inner] = o[rows]
    stores += started([(hid, hid_far)], sems.at[pl.ds(5, 1)])
    for q in range(chips):
        for f in range(count // chips):
            rows = slice(f * block, (f + 1) * block)
            outs[q][rows] = held[f * chips + (idx[2] ^ q)]
    for copy in stores:
        copy.wait()


def own_patches(ref, core, block):
    rows, width = ref.shape
    value = ref[...].astype(F32).reshape(rows // block, block, width)
    value = jnp.where(core == 0, value[:, : block // 2], value[:, block // 2 :])
    return value.reshape(rows // 2, width)


def all_patches(mine, other, core, block):
    rows, width = mine.shape
    mine = mine.astype(F32).reshape(2 * rows // block, block // 2, width)
    other = other.astype(F32).reshape(2 * rows // block, block // 2, width)
    first, second = jnp.where(core == 0, mine, other), jnp.where(core == 0, other, mine)
    return jnp.concatenate([first, second], axis=1).reshape(2 * rows, width).astype(BF16)


def half_kernel(chips, got, own, half, kept):
    rows = half.shape[0]
    core = place(chips)[1]
    half[...] = jnp.where(core == 0, got[:rows].astype(F32), got[rows:].astype(F32)).astype(BF16)
    kept[...] = own[...]


def join_rows_kernel(*refs):
    out, low = refs[-1], 0
    for ref in refs[:-1]:
        out[low : low + ref.shape[0], : ref.shape[1]] = ref[...]
        low += ref.shape[0]


def temporal_kernel(shards, blocks, chips, group, near, far, wot, *refs):
    idx = place(chips)
    weights, refs = refs[: len(shards)], refs[len(shards) :]
    (mine, *outs), (cot, qkv, g, p_ref, grads) = refs[:chips], refs[chips:]
    width = wot.shape[1]
    value = [own_patches(ref, idx[1], 2 * group) for ref in (near, far)]
    value = jnp.concatenate(value, axis=0).astype(BF16)
    hidden = value[:, :width]
    cot[...] = value[:, width : 2 * width]
    count = qkv.shape[0] // blocks
    for at, w in zip(shards, weights):
        value = dot_bt(hidden, w[...]).astype(BF16)
        for i, block in enumerate(at(idx)):
            for t in range(count):
                qkv[block * count + t] = tile(value, i * count + t)
    mine[:, width:] = softmax_forward(qkv, p_ref, ("cycle", group))
    spread(dot_bt(cot[...], wot[...]).astype(BF16), g)
    softmax_backward(qkv, g, p_ref, grads)
    grad = jnp.zeros(cot.shape, F32)
    for at, w in zip(shards, weights):
        lhs = joined([grads[block * count + t] for block in at(idx) for t in range(count)])
        grad += dot(lhs, w[...])
    mine[:, :width] = (cot[...].astype(F32) + grad.astype(BF16).astype(F32)).astype(BF16)
    half = mine.shape[0] // 2
    rows = half // chips
    for q, out in enumerate(outs, 1):
        out[:rows] = mine[q * rows : (q + 1) * rows]
        out[rows:] = mine[half + q * rows : half + (q + 1) * rows]


def others_kernel(mine, *refs):
    parts, out = refs[-2::-1], refs[-1]
    half = mine.shape[0] // 2
    rows = half // (1 + len(parts))
    out[:rows] = mine[half : half + rows]
    for q, part in enumerate(parts, 1):
        out[q * rows : (q + 1) * rows] = part[rows:]


def whole_parts_kernel(chips, block, inner, width, mine, other, *refs):
    idx = place(chips)
    held, part = refs
    cot, so = held[:, width : 2 * width], held[:, 2 * width : 2 * width + inner]
    half = mine.shape[0] // 2
    near = all_patches(mine[:half], other[half:], idx[1], block)
    part[0] = dot_at(near[:, width:], cot).astype(BF16)
    part[1] = dot_at(so, near[:, :width]).astype(BF16)


def parts_kernel(chips, block, inner, width, mine, other, *refs):
    idx = place(chips)
    sent, refs = refs[:2], refs[2:]
    keep, send_x, send_y, heads, cols = refs
    half = mine.shape[0] // 2
    near = all_patches(mine[:half], other[half:], idx[1], block)
    far = all_patches(mine[half:], other[:half], idx[1], block)
    rows = near.shape[0]
    size = heads.shape[2]
    count, _, wide = cols.shape
    for i in range(2):
        if i == 0:
            lefts = [near[:, width:], far[:, width:]]
            rights = [part[:, width : 2 * width] for part in sent]
        else:
            lefts = [part[:, 2 * width : 2 * width + inner] for part in sent]
            rights = [near[:, :width], far[:, :width]]
        for at in range(2):
            held = slice(at * rows, (at + 1) * rows)
            for h in range(heads.shape[0]):
                heads[h, held] = lefts[at][:, h * size : (h + 1) * size]
            for r in range(count):
                cols[r, held] = rights[at][:, r * wide : (r + 1) * wide]
        left = jnp.concatenate([heads[idx[3] ^ (2 * q)] for q in range(chips)], axis=1)
        first = 1 if i == 0 else 2
        for r in range(count):
            full = dot_at(left, cols[idx[0] ^ r])
            value = jnp.concatenate([full[q * size : (q + 1) * size] for q in range(chips)], axis=1)
            if r & first:
                (send_x, send_y)[i][r // 2 if i == 0 else r - 2] = value.astype(BF16)
            else:
                keep[2 * i + (r > 0)] = value


def sum_first_kernel(keep, got_x, got_y, own, send_y, send_x):
    for i, (got, send) in enumerate(((got_x, send_y), (got_y, send_x))):
        own[i] = keep[2 * i] + got[0].astype(F32)
        send[...] = (keep[2 * i + 1] + got[1].astype(F32)).astype(BF16)


def sum_second_kernel(own, got_y, got_x, kept, *outs):
    totals = [own[0] + got_y[...].astype(F32), own[1] + got_x[...].astype(F32)]
    size = totals[0].shape[1] // (1 + len(outs))
    for q, out in enumerate((kept, *outs)):
        cut = [total[:, q * size : (q + 1) * size] for total in totals]
        out[...] = jnp.concatenate(cut, axis=1).astype(out.dtype)


def sum_kernel(own, *refs):
    got, outs = refs[:-2], refs[-2:]
    total = own[...]
    for part in got:
        total += part[...].astype(F32)
    size = outs[0].shape[1]
    for i, out in enumerate(outs):
        out[...] = total[:, i * size : (i + 1) * size]


def last_kernel(chips, patches, *refs):
    idx = place(chips)
    held, got, refs = refs[:chips][::-1], refs[chips], refs[chips + 1 :]
    (wos, qkv, p_ref, wot, hid), refs = refs[:5], refs[5:]
    block_far, out_far, grads_far, rows, block_out, grads, tiles, gs, parts, sems = refs
    inner, width = wos.shape
    frames = rows.shape[0] // patches
    block = patches // chips
    each = frames * block // 2
    for q in range(chips):
        value = all_patches(held[q][:each], got[q * each : (q + 1) * each], idx[1], block)
        for f in range(frames):
            low = pl.multiple_of(f * patches + (idx[2] ^ q) * block, block)
            rows[pl.ds(low, block)] = value[f * block : (f + 1) * block]
    value = rows[...]
    grad, attended = value[:, :width], value[:, width:]
    stores = started([(rows.at[:, pl.ds(0, width)], out_far)], sems.at[pl.ds(0, 1)])
    block_out[...] = (hid[...].astype(F32) + dot(attended, wot[...])).astype(BF16)
    stores += started([(block_out, block_far)], sems.at[pl.ds(1, 1)])
    spread(dot_bt(grad, wos[...]).astype(BF16), gs)
    spread(qkv[...], tiles)
    softmax_backward(tiles, gs, p_ref, parts)
    grads[...] = joined([parts[i] for i in range(parts.shape[0])])
    stores += started([(grads, grads_far)], sems.at[pl.ds(2, 1)])
    for copy in stores:
        copy.wait()


def flip(value, axis, bit):
    return lax.ppermute(value, axis, [(i, i ^ bit) for i in range(lax.axis_size(axis))])


def sems(n):
    return pltpu.SemaphoreType.DMA((n,))


def across(value, bits):
    n = lax.axis_size("seq")
    pairs = [
        (d * n + i, (d ^ bits[i % 2]) * n + i) for d in range(lax.axis_size("dp")) for i in range(n)
    ]
    return lax.ppermute(value, ("dp", "seq"), pairs)


def gather(weight, parts, chips):
    n = lax.axis_size("dp")
    rows, sent = parts[0].shape
    whole = [shape((len(parts) * rows, sent + PAD))]
    if n != 4:
        (near,) = call(join_rows_kernel, whole, from_chips(parts), small=True)
        weights = [lax.all_gather(weight, "dp", axis=0, tiled=True)]
        return near, flip(near, "seq", 1), weights, [lambda idx: [0]], 1
    half, width = weight.shape[0] // 2, weight.shape[1]
    side = across(weight, (1, 2))
    corner, own = call(
        functools.partial(half_kernel, chips),
        [shape((half, width)), shape((rows, sent))],
        [side, parts[0]],
        small=True,
    )
    corner = across(corner, (2, 1))
    (near,) = call(join_rows_kernel, whole, [own, *from_chips(parts)[1:]], small=True)
    weights = [weight, side, flip(side, "seq", 1), corner, flip(corner, "seq", 1)]

    def both(shard):
        return lambda idx: [2 * shard(idx), 2 * shard(idx) + 1]

    shards = [
        both(lambda idx: idx[0]),
        both(lambda idx: idx[0] ^ (1 + idx[1])),
        both(lambda idx: idx[0] ^ (2 - idx[1])),
        lambda idx: [2 * (idx[0] ^ 3) + idx[1]],
        lambda idx: [2 * (idx[0] ^ 3) + 1 - idx[1]],
    ]
    return near, flip(near, "seq", 1), weights, shards, 2 * n


def from_chips(parts):
    return [parts[0]] + [flip(parts[q], "seq", 2 * q) for q in range(1, len(parts))]


def reduced(keep, send_x, send_y):
    _, size, width = keep.shape
    step = shape((size, width))
    own, send_t, send_s = call(
        sum_first_kernel,
        [shape((2, size, width), F32), step, step],
        [keep, flip(send_x, "dp", 1), flip(send_y, "dp", 2)],
        small=True,
    )
    n = lax.axis_size("seq") // 2
    block = (size, 2 * width // n)
    own, *sends = call(
        sum_second_kernel,
        [shape(block, F32)] + [shape(block)] * (n - 1),
        [own, flip(send_t, "dp", 2), flip(send_s, "dp", 1)],
        small=True,
    )
    got = from_chips([own, *sends])[1:]
    return call(sum_kernel, [shape((size, width // n), F32)] * 2, [own, *got[::-1]], small=True)


def shards(tokens, spatial_qkv, wo_spatial, w_temporal, wo_temporal, cotangent):
    frames, patches, width = tokens.shape
    inner = wo_spatial.shape[0]
    heads = inner // DH
    rows = frames * patches
    peers = FRAMES // frames
    chips = peers // 2
    group = patches // peers
    block = 2 * group
    n_dp, n_seq = lax.axis_size("dp"), lax.axis_size("seq")

    def held(columns):
        return pltpu.VMEM((rows, columns), BF16)

    def tiles(parts):
        return pltpu.VMEM((parts * heads, rows, LANES), BF16)

    attended = pltpu.VMEM((heads, rows, rows), F32)
    projection = pltpu.VMEM((inner, width), BF16)
    per_chip = rows // chips
    qkv_rows = spatial_qkv.reshape(rows, 3 * inner)
    sent = -(-(2 * width + inner) // LANES) * LANES
    *near, hidden, spatial_p = call(
        functools.partial(spatial_kernel, chips, patches),
        [shape((per_chip, sent))] * chips
        + [shape((rows, width)), shape((heads, rows, rows), F32)],
        [qkv_rows, tokens.reshape(rows, width), wo_spatial, cotangent.reshape(rows, width)],
        [held(width), held(width), held(3 * inner), projection]
        + [pltpu.VMEM((frames * chips, block, sent), BF16), held(width), attended]
        + [tiles(3), sems(6)],
        far_in=range(4),
        far_out=(chips, chips + 1),
    )
    near, far, weights, places, count = gather(w_temporal.T, near, chips)
    mine, *back = call(
        functools.partial(temporal_kernel, places, count, chips, group),
        [shape((rows, width + inner))] + [shape((per_chip, width + inner))] * (chips - 1),
        [near, far, wo_temporal, *weights],
        [held(width), tiles(3), tiles(1), attended, tiles(3)],
        small=True,
    )
    other = flip(mine, "seq", 1)
    if n_dp == 4 and n_seq == peers:
        size = inner // n_seq
        keep, send_x, send_y = call(
            functools.partial(parts_kernel, chips, block, inner, width),
            [shape((n_dp, size, width), F32)] + [shape((2, size, width))] * 2,
            [mine, other, near, far],
            [
                pltpu.VMEM((n_seq, 2 * rows, size), BF16),
                pltpu.VMEM((n_dp, 2 * rows, width // n_dp), BF16),
            ],
            small=True,
        )
    else:
        (both,) = call(
            functools.partial(whole_parts_kernel, chips, block, inner, width),
            [shape((2, inner, width))],
            [mine, other, near],
            small=True,
        )
    back = from_chips([mine, *back])
    (others,) = call(
        others_kernel,
        [shape((rows // 2, width + inner))],
        [back[0], *back[:0:-1]],
        small=True,
    )
    block_out, tokens_grad, qkv_grad = call(
        functools.partial(last_kernel, chips, patches),
        [shape((rows, width)), shape((rows, width)), shape((rows, 3 * inner))],
        [*back[::-1], flip(others, "seq", 1), wo_spatial, qkv_rows, spatial_p, wo_temporal, hidden],
        [held(width + inner), held(width), held(3 * inner)]
        + [tiles(3), tiles(1), tiles(3), sems(3)],
        far_out=range(3),
        small=True,
    )
    if n_dp == 4 and n_seq == peers:
        temporal_grad, spatial_grad = reduced(keep, send_x, send_y)
    else:
        both = lax.psum_scatter(both, "seq", scatter_dimension=1, tiled=True)
        both = lax.psum_scatter(both, "dp", scatter_dimension=2, tiled=True).astype(F32)
        temporal_grad, spatial_grad = both[0], both[1]
    return (
        block_out.reshape(frames, patches, width),
        tokens_grad.reshape(frames, patches, width),
        qkv_grad.reshape(frames, patches, 3 * inner),
        spatial_grad,
        temporal_grad,
    )


def solution(mesh):
    placed = (
        P(("dp", "seq"), None, None),
        P(("dp", "seq"), None, None),
        P(),
        P(None, "dp"),
        P(),
        P(("dp", "seq"), None, None),
    )
    return jax.shard_map(
        shards,
        mesh=mesh,
        in_specs=placed,
        out_specs=(
            P(("dp", "seq"), None, None),
            P(("dp", "seq"), None, None),
            P(("dp", "seq"), None, None),
            P("seq", "dp"),
            P("seq", "dp"),
        ),
        check_vma=False,
    )
```

```python
import functools
import math

import jax
import jax.numpy as jnp
from jax import lax
from jax.experimental import pallas as pl
from jax.experimental.pallas import tpu as pltpu
from jax.sharding import PartitionSpec as P

DH = 72
FRAMES = 16
LANES = 128
BF16 = jnp.bfloat16
F32 = jnp.float32
VMEM = pl.BlockSpec(memory_space=pltpu.VMEM)
SMEM = pl.BlockSpec(memory_space=pltpu.SMEM)
HBM = pl.BlockSpec(memory_space=pltpu.HBM)
PAD = 2 * LANES
LIMIT = 16 * 1024 * 1024
MOST = 53 * 1024 * 1024


def dot(left, right):
    return jnp.dot(left, right, preferred_element_type=F32)


def dot_bt(left, right):
    return lax.dot_general(left, right, (((1,), (1,)), ((), ())), preferred_element_type=F32)


def dot_at(left, right):
    return lax.dot_general(left, right, (((0,), (0,)), ((), ())), preferred_element_type=F32)


def call(body, outs, args, scratch=(), us=0, far_in=(), far_out=(), small=False):
    moved = sum(math.prod(a.shape) * a.dtype.itemsize for a in (*args, *outs))
    near = [SMEM if a.dtype == jnp.int32 else VMEM for a in args]
    return pl.pallas_call(
        body,
        out_shape=outs,
        in_specs=[HBM if i in far_in else spec for i, spec in enumerate(near)],
        out_specs=[
            HBM if i in far_out else SMEM if out.dtype == jnp.int32 else VMEM
            for i, out in enumerate(outs)
        ],
        scratch_shapes=list(scratch),
        compiler_params=pltpu.CompilerParams(vmem_limit_bytes=LIMIT if small else MOST),
        cost_estimate=pl.CostEstimate(
            flops=us * 1150000000, bytes_accessed=moved if us else 0, transcendentals=0
        ),
    )(*args)


def started(pairs, sems):
    copies = [pltpu.make_async_copy(a, b, sems.at[i]) for i, (a, b) in enumerate(pairs)]
    for copy in copies:
        copy.start()
    return copies


def shape(dims, dtype=BF16):
    return jax.ShapeDtypeStruct(dims, dtype)


TOKEN = shape((1,), jnp.int32)


def window(head):
    low = head * DH // LANES * LANES
    high = -(-(head + 1) * DH // LANES) * LANES
    return low, high


def head_only(block, head):
    low, high = window(head)
    lane = lax.broadcasted_iota(jnp.int32, (1, high - low), 1) + low
    keep = (lane >= head * DH) & (lane < (head + 1) * DH)
    return jnp.where(keep, block, jnp.zeros_like(block))


def add_tiles(tiles, head, value):
    low, high = window(head)
    for at in range(low // LANES, high // LANES):
        part = value[:, at * LANES - low : (at + 1) * LANES - low]
        tiles[at] = part if tiles[at] is None else tiles[at] + part


def joined(tiles):
    return jnp.concatenate([tile.astype(BF16) for tile in tiles], axis=1)


def same_group(rows, kind):
    row = lax.broadcasted_iota(jnp.int32, (rows, rows), 0)
    col = lax.broadcasted_iota(jnp.int32, (rows, rows), 1)
    how, size = kind
    return row // size == col // size if how == "block" else row % size == col % size


def softmax_forward(q_ref, k_ref, v_ref, p_ref, heads, kind):
    rows = q_ref.shape[0]
    mask = same_group(rows, kind)
    tiles = [None] * (q_ref.shape[1] // LANES)
    for head in range(heads):
        low, high = window(head)
        s = dot_bt(q_ref[:, low:high], head_only(k_ref[:, low:high], head)) * (1.0 / math.sqrt(DH))
        s = jnp.where(mask, s, -jnp.inf)
        e = jnp.exp(s - jnp.max(s, axis=1, keepdims=True))
        p = e / jnp.sum(e, axis=1, keepdims=True)
        p_ref[head] = p
        add_tiles(tiles, head, dot(p.astype(BF16), head_only(v_ref[:, low:high], head)))
    return joined(tiles)


def softmax_backward(q_ref, k_ref, v_ref, g_ref, p_ref, heads):
    count = q_ref.shape[1] // LANES
    dq, dk, dv = [None] * count, [None] * count, [None] * count
    for head in range(heads):
        low, high = window(head)
        p = p_ref[head]
        g = head_only(g_ref[:, low:high], head)
        add_tiles(dv, head, dot_at(p.astype(BF16), g))
        dp = dot_bt(g, v_ref[:, low:high])
        ds = p * (dp - jnp.sum(p * dp, axis=1, keepdims=True)) * (1.0 / math.sqrt(DH))
        ds = ds.astype(BF16)
        add_tiles(dq, head, dot(ds, head_only(k_ref[:, low:high], head)))
        add_tiles(dk, head, dot_at(ds, head_only(q_ref[:, low:high], head)))
    return joined(dq), joined(dk), joined(dv)


def put(ref, value):
    width = value.shape[1]
    ref[:, width // LANES * LANES :] = jnp.zeros(
        (ref.shape[0], ref.shape[1] - width // LANES * LANES), ref.dtype
    )
    ref[:, :width] = value


def place(chips):
    seq = lax.axis_index("seq")
    return lax.axis_index("dp"), seq % 2, seq % (2 * chips) // 2, seq


def spatial_kernel(chips, patches, *refs):
    idx = place(chips)
    far, outs, refs = refs[:4], refs[4 : 4 + chips], refs[4 + chips :]
    hid_far, p_far, tok, cot, qkv, wos, held, hid, p_ref, qs, ks, vs, sems = refs
    inner, width = wos.shape
    count, block, _ = held.shape
    loads = started(zip(far, (qkv, tok, wos, cot)), sems)
    loads[0].wait()
    x = qkv[...]
    put(qs, x[:, :inner])
    put(ks, x[:, inner : 2 * inner])
    put(vs, x[:, 2 * inner :])
    o = softmax_forward(qs, ks, vs, p_ref, inner // DH, ("block", patches))[:, :inner]
    stores = started([(p_ref, p_far)], sems.at[pl.ds(4, 1)])
    for at in range(3):
        loads[1 + at].wait()
    hid[...] = (tok[...].astype(F32) + dot(o, wos[...])).astype(BF16)
    for at in range(count):
        rows = slice(at * block, (at + 1) * block)
        held[at, :, :width] = hid[rows]
        held[at, :, width : 2 * width] = cot[rows]
        held[at, :, 2 * width : 2 * width + inner] = o[rows]
    stores += started([(hid, hid_far)], sems.at[pl.ds(5, 1)])
    for q in range(chips):
        for f in range(count // chips):
            rows = slice(f * block, (f + 1) * block)
            outs[q][rows] = held[f * chips + (idx[2] ^ q)]
    for copy in stores:
        copy.wait()


def own_patches(ref, core, block):
    rows, width = ref.shape
    value = ref[...].astype(F32).reshape(rows // block, block, width)
    value = jnp.where(core == 0, value[:, : block // 2], value[:, block // 2 :])
    return value.reshape(rows // 2, width)


def all_patches(mine, other, core, block):
    rows, width = mine.shape
    mine = mine.astype(F32).reshape(2 * rows // block, block // 2, width)
    other = other.astype(F32).reshape(2 * rows // block, block // 2, width)
    first, second = jnp.where(core == 0, mine, other), jnp.where(core == 0, other, mine)
    return jnp.concatenate([first, second], axis=1).reshape(2 * rows, width).astype(BF16)


def half_kernel(chips, got, own, half, kept):
    rows = half.shape[0]
    core = place(chips)[1]
    half[...] = jnp.where(core == 0, got[:rows].astype(F32), got[rows:].astype(F32)).astype(BF16)
    kept[...] = own[...]


def join_rows_kernel(*refs):
    out, low = refs[-1], 0
    for ref in refs[:-1]:
        out[low : low + ref.shape[0], : ref.shape[1]] = ref[...]
        low += ref.shape[0]


def temporal_kernel(shards, chips, group, near, far, wot, *refs):
    idx = place(chips)
    weights, refs = refs[: len(shards)], refs[len(shards) :]
    (mine, *outs), (cot, q, k, v, g, p_ref, blocks) = refs[:chips], refs[chips:]
    inner, width = wot.shape
    heads = inner // DH
    value = [own_patches(ref, idx[1], 2 * group) for ref in (near, far)]
    value = jnp.concatenate(value, axis=0).astype(BF16)
    hidden = value[:, :width]
    cot[...] = value[:, width : 2 * width]
    size = blocks.shape[2]
    for at, w in zip(shards, weights):
        value = dot_bt(hidden, w[...]).astype(BF16)
        for i, block in enumerate(at(idx)):
            blocks[block] = value[:, i * size : (i + 1) * size]
    whole = jnp.concatenate([blocks[i] for i in range(blocks.shape[0])], axis=1)
    put(q, whole[:, :inner])
    put(k, whole[:, inner : 2 * inner])
    put(v, whole[:, 2 * inner :])
    mine[:, width:] = softmax_forward(q, k, v, p_ref, heads, ("cycle", group))[:, :inner]
    put(g, dot_bt(cot[...], wot[...]).astype(BF16))
    dq, dk, dv = softmax_backward(q, k, v, g, p_ref, heads)
    whole = jnp.concatenate([dq[:, :inner], dk[:, :inner], dv[:, :inner]], axis=1)
    for i in range(blocks.shape[0]):
        blocks[i] = whole[:, i * size : (i + 1) * size]
    grad = jnp.zeros(cot.shape, F32)
    for at, w in zip(shards, weights):
        lhs = jnp.concatenate([blocks[block] for block in at(idx)], axis=1)
        grad += dot(lhs, w[...])
    mine[:, :width] = (cot[...].astype(F32) + grad.astype(BF16).astype(F32)).astype(BF16)
    half = mine.shape[0] // 2
    rows = half // chips
    for q, out in enumerate(outs, 1):
        out[:rows] = mine[q * rows : (q + 1) * rows]
        out[rows:] = mine[half + q * rows : half + (q + 1) * rows]


def others_kernel(mine, *refs):
    parts, out = refs[-2::-1], refs[-1]
    half = mine.shape[0] // 2
    rows = half // (1 + len(parts))
    out[:rows] = mine[half : half + rows]
    for q, part in enumerate(parts, 1):
        out[q * rows : (q + 1) * rows] = part[rows:]


def whole_parts_kernel(chips, block, inner, width, mine, other, *refs):
    idx = place(chips)
    held, part = refs
    cot, so = held[:, width : 2 * width], held[:, 2 * width : 2 * width + inner]
    half = mine.shape[0] // 2
    near = all_patches(mine[:half], other[half:], idx[1], block)
    part[0] = dot_at(near[:, width:], cot).astype(BF16)
    part[1] = dot_at(so, near[:, :width]).astype(BF16)


def parts_kernel(chips, block, inner, width, mine, other, *refs):
    idx = place(chips)
    sent, refs = refs[:2], refs[2:]
    keep, send_x, send_y, heads, cols = refs
    half = mine.shape[0] // 2
    near = all_patches(mine[:half], other[half:], idx[1], block)
    far = all_patches(mine[half:], other[:half], idx[1], block)
    rows = near.shape[0]
    size = heads.shape[2]
    count, _, wide = cols.shape
    for i in range(2):
        if i == 0:
            lefts = [near[:, width:], far[:, width:]]
            rights = [part[:, width : 2 * width] for part in sent]
        else:
            lefts = [part[:, 2 * width : 2 * width + inner] for part in sent]
            rights = [near[:, :width], far[:, :width]]
        for at in range(2):
            held = slice(at * rows, (at + 1) * rows)
            for h in range(heads.shape[0]):
                heads[h, held] = lefts[at][:, h * size : (h + 1) * size]
            for r in range(count):
                cols[r, held] = rights[at][:, r * wide : (r + 1) * wide]
        left = jnp.concatenate([heads[idx[3] ^ (2 * q)] for q in range(chips)], axis=1)
        first = 1 if i == 0 else 2
        for r in range(count):
            full = dot_at(left, cols[idx[0] ^ r])
            value = jnp.concatenate([full[q * size : (q + 1) * size] for q in range(chips)], axis=1)
            if r & first:
                (send_x, send_y)[i][r // 2 if i == 0 else r - 2] = value.astype(BF16)
            else:
                keep[2 * i + (r > 0)] = value


def sum_first_kernel(keep, got_x, got_y, own, send_y, send_x):
    for i, (got, send) in enumerate(((got_x, send_y), (got_y, send_x))):
        own[i] = keep[2 * i] + got[0].astype(F32)
        send[...] = (keep[2 * i + 1] + got[1].astype(F32)).astype(BF16)


def sum_second_kernel(own, got_y, got_x, kept, *outs):
    totals = [own[0] + got_y[...].astype(F32), own[1] + got_x[...].astype(F32)]
    size = totals[0].shape[1] // (1 + len(outs))
    for q, out in enumerate((kept, *outs)):
        cut = [total[:, q * size : (q + 1) * size] for total in totals]
        out[...] = jnp.concatenate(cut, axis=1).astype(out.dtype)


def sum_kernel(own, *refs):
    got, outs = refs[:-2], refs[-2:]
    total = own[...]
    for part in got:
        total += part[...].astype(F32)
    size = outs[0].shape[1]
    for i, out in enumerate(outs):
        out[...] = total[:, i * size : (i + 1) * size]


def last_kernel(chips, patches, *refs):
    idx = place(chips)
    held, got, refs = refs[:chips][::-1], refs[chips], refs[chips + 1 :]
    (wos, qkv, p_ref, wot, hid), refs = refs[:5], refs[5:]
    block_far, out_far, grads_far, rows, block_out, grads, qs, ks, vs, gs, sems = refs
    inner, width = wos.shape
    frames = rows.shape[0] // patches
    block = patches // chips
    each = frames * block // 2
    for q in range(chips):
        value = all_patches(held[q][:each], got[q * each : (q + 1) * each], idx[1], block)
        for f in range(frames):
            low = pl.multiple_of(f * patches + (idx[2] ^ q) * block, block)
            rows[pl.ds(low, block)] = value[f * block : (f + 1) * block]
    value = rows[...]
    grad, attended = value[:, :width], value[:, width:]
    stores = started([(rows.at[:, pl.ds(0, width)], out_far)], sems.at[pl.ds(0, 1)])
    block_out[...] = (hid[...].astype(F32) + dot(attended, wot[...])).astype(BF16)
    stores += started([(block_out, block_far)], sems.at[pl.ds(1, 1)])
    put(gs, dot_bt(grad, wos[...]).astype(BF16))
    x = qkv[...]
    put(qs, x[:, :inner])
    put(ks, x[:, inner : 2 * inner])
    put(vs, x[:, 2 * inner :])
    dq, dk, dv = softmax_backward(qs, ks, vs, gs, p_ref, inner // DH)
    grads[...] = jnp.concatenate([dq[:, :inner], dk[:, :inner], dv[:, :inner]], axis=1)
    stores += started([(grads, grads_far)], sems.at[pl.ds(2, 1)])
    for copy in stores:
        copy.wait()


def flip(value, axis, bit):
    return lax.ppermute(value, axis, [(i, i ^ bit) for i in range(lax.axis_size(axis))])


def sems(n):
    return pltpu.SemaphoreType.DMA((n,))


def across(value, bits):
    n = lax.axis_size("seq")
    pairs = [
        (d * n + i, (d ^ bits[i % 2]) * n + i) for d in range(lax.axis_size("dp")) for i in range(n)
    ]
    return lax.ppermute(value, ("dp", "seq"), pairs)


def gather(weight, parts, chips):
    n = lax.axis_size("dp")
    rows, sent = parts[0].shape
    whole = [shape((len(parts) * rows, sent + PAD))]
    if n != 4:
        (near,) = call(join_rows_kernel, whole, from_chips(parts), small=True)
        weights = [lax.all_gather(weight, "dp", axis=0, tiled=True)]
        return near, flip(near, "seq", 1), weights, [lambda idx: [0]], 1
    half, width = weight.shape[0] // 2, weight.shape[1]
    side = across(weight, (1, 2))
    corner, own = call(
        functools.partial(half_kernel, chips),
        [shape((half, width)), shape((rows, sent))],
        [side, parts[0]],
        small=True,
    )
    corner = across(corner, (2, 1))
    (near,) = call(join_rows_kernel, whole, [own, *from_chips(parts)[1:]], small=True)
    weights = [weight, side, flip(side, "seq", 1), corner, flip(corner, "seq", 1)]

    def both(shard):
        return lambda idx: [2 * shard(idx), 2 * shard(idx) + 1]

    shards = [
        both(lambda idx: idx[0]),
        both(lambda idx: idx[0] ^ (1 + idx[1])),
        both(lambda idx: idx[0] ^ (2 - idx[1])),
        lambda idx: [2 * (idx[0] ^ 3) + idx[1]],
        lambda idx: [2 * (idx[0] ^ 3) + 1 - idx[1]],
    ]
    return near, flip(near, "seq", 1), weights, shards, 2 * n


def from_chips(parts):
    return [parts[0]] + [flip(parts[q], "seq", 2 * q) for q in range(1, len(parts))]


def reduced(keep, send_x, send_y):
    _, size, width = keep.shape
    step = shape((size, width))
    own, send_t, send_s = call(
        sum_first_kernel,
        [shape((2, size, width), F32), step, step],
        [keep, flip(send_x, "dp", 1), flip(send_y, "dp", 2)],
        small=True,
    )
    n = lax.axis_size("seq") // 2
    block = (size, 2 * width // n)
    own, *sends = call(
        sum_second_kernel,
        [shape(block, F32)] + [shape(block)] * (n - 1),
        [own, flip(send_t, "dp", 2), flip(send_s, "dp", 1)],
        small=True,
    )
    got = from_chips([own, *sends])[1:]
    return call(sum_kernel, [shape((size, width // n), F32)] * 2, [own, *got[::-1]], small=True)


def shards(tokens, spatial_qkv, wo_spatial, w_temporal, wo_temporal, cotangent):
    frames, patches, width = tokens.shape
    inner = wo_spatial.shape[0]
    heads = inner // DH
    padded = -(-inner // LANES) * LANES
    rows = frames * patches
    peers = FRAMES // frames
    chips = peers // 2
    group = patches // peers
    block = 2 * group
    n_dp, n_seq = lax.axis_size("dp"), lax.axis_size("seq")

    def held(columns, dtype=BF16):
        return pltpu.VMEM((rows, columns), dtype)

    wide = held(padded)
    attended = pltpu.VMEM((heads, rows, rows), F32)
    projection = pltpu.VMEM((inner, width), BF16)
    per_chip = rows // chips
    qkv_rows = spatial_qkv.reshape(rows, 3 * inner)
    sent = -(-(2 * width + inner) // LANES) * LANES
    *near, hidden, spatial_p = call(
        functools.partial(spatial_kernel, chips, patches),
        [shape((per_chip, sent))] * chips
        + [shape((rows, width)), shape((heads, rows, rows), F32)],
        [qkv_rows, tokens.reshape(rows, width), wo_spatial, cotangent.reshape(rows, width)],
        [held(width), held(width), held(3 * inner), projection]
        + [pltpu.VMEM((frames * chips, block, sent), BF16), held(width), attended]
        + [wide] * 3
        + [sems(6)],
        far_in=range(4),
        far_out=(chips, chips + 1),
    )
    near, far, weights, places, count = gather(w_temporal.T, near, chips)
    blocks = pltpu.VMEM((count, rows, 3 * inner // count), BF16)
    mine, *back = call(
        functools.partial(temporal_kernel, places, chips, group),
        [shape((rows, width + inner))] + [shape((per_chip, width + inner))] * (chips - 1),
        [near, far, wo_temporal, *weights],
        [held(width)] + [wide] * 4 + [attended, blocks],
        small=True,
    )
    other = flip(mine, "seq", 1)
    if n_dp == 4 and n_seq == peers:
        size = inner // n_seq
        keep, send_x, send_y = call(
            functools.partial(parts_kernel, chips, block, inner, width),
            [shape((n_dp, size, width), F32)] + [shape((2, size, width))] * 2,
            [mine, other, near, far],
            [
                pltpu.VMEM((n_seq, 2 * rows, size), BF16),
                pltpu.VMEM((n_dp, 2 * rows, width // n_dp), BF16),
            ],
            small=True,
        )
    else:
        (both,) = call(
            functools.partial(whole_parts_kernel, chips, block, inner, width),
            [shape((2, inner, width))],
            [mine, other, near],
            small=True,
        )
    back = from_chips([mine, *back])
    (others,) = call(
        others_kernel,
        [shape((rows // 2, width + inner))],
        [back[0], *back[:0:-1]],
        small=True,
    )
    block_out, tokens_grad, qkv_grad = call(
        functools.partial(last_kernel, chips, patches),
        [shape((rows, width)), shape((rows, width)), shape((rows, 3 * inner))],
        [*back[::-1], flip(others, "seq", 1), wo_spatial, qkv_rows, spatial_p, wo_temporal, hidden],
        [held(width + inner), held(width), held(3 * inner)] + [wide] * 4 + [sems(3)],
        far_out=range(3),
        small=True,
    )
    if n_dp == 4 and n_seq == peers:
        temporal_grad, spatial_grad = reduced(keep, send_x, send_y)
    else:
        both = lax.psum_scatter(both, "seq", scatter_dimension=1, tiled=True)
        both = lax.psum_scatter(both, "dp", scatter_dimension=2, tiled=True).astype(F32)
        temporal_grad, spatial_grad = both[0], both[1]
    return (
        block_out.reshape(frames, patches, width),
        tokens_grad.reshape(frames, patches, width),
        qkv_grad.reshape(frames, patches, 3 * inner),
        spatial_grad,
        temporal_grad,
    )


def solution(mesh):
    placed = (
        P(("dp", "seq"), None, None),
        P(("dp", "seq"), None, None),
        P(),
        P(None, "dp"),
        P(),
        P(("dp", "seq"), None, None),
    )
    return jax.shard_map(
        shards,
        mesh=mesh,
        in_specs=placed,
        out_specs=(
            P(("dp", "seq"), None, None),
            P(("dp", "seq"), None, None),
            P(("dp", "seq"), None, None),
            P("seq", "dp"),
            P("seq", "dp"),
        ),
        check_vma=False,
    )
```

```python
import functools
import math

import jax
import jax.numpy as jnp
from jax import lax
from jax.experimental import pallas as pl
from jax.experimental.pallas import tpu as pltpu
from jax.sharding import PartitionSpec as P

DH = 72
FRAMES = 16
LANES = 128
BF16 = jnp.bfloat16
F32 = jnp.float32
VMEM = pl.BlockSpec(memory_space=pltpu.VMEM)
SMEM = pl.BlockSpec(memory_space=pltpu.SMEM)
HBM = pl.BlockSpec(memory_space=pltpu.HBM)
PAD = 2 * LANES
LIMIT = 16 * 1024 * 1024
MOST = 53 * 1024 * 1024


def dot(left, right):
    return jnp.dot(left, right, preferred_element_type=F32)


def dot_bt(left, right):
    return lax.dot_general(left, right, (((1,), (1,)), ((), ())), preferred_element_type=F32)


def dot_weight(rows, weight):
    return dot_bt(weight, rows).T


def dot_at(left, right):
    return lax.dot_general(left, right, (((0,), (0,)), ((), ())), preferred_element_type=F32)


def call(body, outs, args, scratch=(), us=0, far_in=(), far_out=(), small=False):
    moved = sum(math.prod(a.shape) * a.dtype.itemsize for a in (*args, *outs))
    near = [SMEM if a.dtype == jnp.int32 else VMEM for a in args]
    return pl.pallas_call(
        body,
        out_shape=outs,
        in_specs=[HBM if i in far_in else spec for i, spec in enumerate(near)],
        out_specs=[
            HBM if i in far_out else SMEM if out.dtype == jnp.int32 else VMEM
            for i, out in enumerate(outs)
        ],
        scratch_shapes=list(scratch),
        compiler_params=pltpu.CompilerParams(vmem_limit_bytes=LIMIT if small else MOST),
        cost_estimate=pl.CostEstimate(
            flops=us * 1150000000, bytes_accessed=moved if us else 0, transcendentals=0
        ),
    )(*args)


def started(pairs, sems):
    copies = [pltpu.make_async_copy(a, b, sems.at[i]) for i, (a, b) in enumerate(pairs)]
    for copy in copies:
        copy.start()
    return copies


def shape(dims, dtype=BF16):
    return jax.ShapeDtypeStruct(dims, dtype)


TOKEN = shape((1,), jnp.int32)


def window(head):
    low = head * DH // LANES * LANES
    high = -(-(head + 1) * DH // LANES) * LANES
    return low, high


def head_only(block, head):
    low, high = window(head)
    lane = lax.broadcasted_iota(jnp.int32, (1, high - low), 1) + low
    keep = (lane >= head * DH) & (lane < (head + 1) * DH)
    return jnp.where(keep, block, jnp.zeros_like(block))


def add_tiles(tiles, head, value):
    low, high = window(head)
    for at in range(low // LANES, high // LANES):
        part = value[:, at * LANES - low : (at + 1) * LANES - low]
        tiles[at] = part if tiles[at] is None else tiles[at] + part


def joined(tiles):
    return jnp.concatenate([tile.astype(BF16) for tile in tiles], axis=1)


def same_group(rows, kind):
    row = lax.broadcasted_iota(jnp.int32, (rows, rows), 0)
    col = lax.broadcasted_iota(jnp.int32, (rows, rows), 1)
    how, size = kind
    return row // size == col // size if how == "block" else row % size == col % size


def softmax_forward(q_ref, k_ref, v_ref, p_ref, heads, kind):
    rows = q_ref.shape[0]
    mask = same_group(rows, kind)
    tiles = [None] * (q_ref.shape[1] // LANES)
    for head in range(heads):
        low, high = window(head)
        s = dot_bt(q_ref[:, low:high], head_only(k_ref[:, low:high], head)) * (1.0 / math.sqrt(DH))
        s = jnp.where(mask, s, -jnp.inf)
        e = jnp.exp(s - jnp.max(s, axis=1, keepdims=True))
        p = e / jnp.sum(e, axis=1, keepdims=True)
        p_ref[head] = p
        add_tiles(tiles, head, dot(p.astype(BF16), head_only(v_ref[:, low:high], head)))
    return joined(tiles)


def softmax_backward(q_ref, k_ref, v_ref, g_ref, p_ref, heads):
    count = q_ref.shape[1] // LANES
    dq, dk, dv = [None] * count, [None] * count, [None] * count
    for head in range(heads):
        low, high = window(head)
        p = p_ref[head]
        g = head_only(g_ref[:, low:high], head)
        add_tiles(dv, head, dot_at(p.astype(BF16), g))
        dp = dot_bt(g, v_ref[:, low:high])
        ds = p * (dp - jnp.sum(p * dp, axis=1, keepdims=True)) * (1.0 / math.sqrt(DH))
        ds = ds.astype(BF16)
        add_tiles(dq, head, dot(ds, head_only(k_ref[:, low:high], head)))
        add_tiles(dk, head, dot_at(ds, head_only(q_ref[:, low:high], head)))
    return joined(dq), joined(dk), joined(dv)


def put(ref, value):
    width = value.shape[1]
    ref[:, width // LANES * LANES :] = jnp.zeros(
        (ref.shape[0], ref.shape[1] - width // LANES * LANES), ref.dtype
    )
    ref[:, :width] = value


def place(chips):
    seq = lax.axis_index("seq")
    return lax.axis_index("dp"), seq % 2, seq % (2 * chips) // 2, seq


def spatial_kernel(chips, patches, *refs):
    idx = place(chips)
    far, outs, refs = refs[:4], refs[4 : 4 + chips], refs[4 + chips :]
    hid_far, p_far, tok, cot, qkv, wos, held, hid, p_ref, qs, ks, vs, sems = refs
    inner, width = wos.shape
    count, block, _ = held.shape
    loads = started(zip(far, (qkv, tok, wos, cot)), sems)
    loads[0].wait()
    x = qkv[...]
    put(qs, x[:, :inner])
    put(ks, x[:, inner : 2 * inner])
    put(vs, x[:, 2 * inner :])
    o = softmax_forward(qs, ks, vs, p_ref, inner // DH, ("block", patches))[:, :inner]
    stores = started([(p_ref, p_far)], sems.at[pl.ds(4, 1)])
    for at in range(3):
        loads[1 + at].wait()
    hid[...] = (tok[...].astype(F32) + dot(o, wos[...])).astype(BF16)
    for at in range(count):
        rows = slice(at * block, (at + 1) * block)
        held[at, :, :width] = hid[rows]
        held[at, :, width : 2 * width] = cot[rows]
        held[at, :, 2 * width : 2 * width + inner] = o[rows]
    stores += started([(hid, hid_far)], sems.at[pl.ds(5, 1)])
    for q in range(chips):
        for f in range(count // chips):
            rows = slice(f * block, (f + 1) * block)
            outs[q][rows] = held[f * chips + (idx[2] ^ q)]
    for copy in stores:
        copy.wait()


def own_patches(ref, core, block):
    rows, width = ref.shape
    value = ref[...].astype(F32).reshape(rows // block, block, width)
    value = jnp.where(core == 0, value[:, : block // 2], value[:, block // 2 :])
    return value.reshape(rows // 2, width)


def all_patches(mine, other, core, block):
    rows, width = mine.shape
    mine = mine.astype(F32).reshape(2 * rows // block, block // 2, width)
    other = other.astype(F32).reshape(2 * rows // block, block // 2, width)
    first, second = jnp.where(core == 0, mine, other), jnp.where(core == 0, other, mine)
    return jnp.concatenate([first, second], axis=1).reshape(2 * rows, width).astype(BF16)


def half_kernel(chips, got, own, half, kept):
    rows = half.shape[0]
    core = place(chips)[1]
    half[...] = jnp.where(core == 0, got[:rows].astype(F32), got[rows:].astype(F32)).astype(BF16)
    kept[...] = own[...]


def join_rows_kernel(*refs):
    out, low = refs[-1], 0
    for ref in refs[:-1]:
        out[low : low + ref.shape[0], : ref.shape[1]] = ref[...]
        low += ref.shape[0]


def temporal_kernel(shards, chips, group, near, far, wot, *refs):
    idx = place(chips)
    weights, refs = refs[: len(shards)], refs[len(shards) :]
    (mine, *outs), (cot, q, k, v, g, p_ref, blocks) = refs[:chips], refs[chips:]
    inner, width = wot.shape
    heads = inner // DH
    value = [own_patches(ref, idx[1], 2 * group) for ref in (near, far)]
    value = jnp.concatenate(value, axis=0).astype(BF16)
    hidden = value[:, :width]
    cot[...] = value[:, width : 2 * width]
    size = blocks.shape[2]
    for at, w in zip(shards, weights):
        value = dot_weight(hidden, w[...]).astype(BF16)
        for i, block in enumerate(at(idx)):
            blocks[block] = value[:, i * size : (i + 1) * size]
    whole = jnp.concatenate([blocks[i] for i in range(blocks.shape[0])], axis=1)
    put(q, whole[:, :inner])
    put(k, whole[:, inner : 2 * inner])
    put(v, whole[:, 2 * inner :])
    mine[:, width:] = softmax_forward(q, k, v, p_ref, heads, ("cycle", group))[:, :inner]
    put(g, dot_weight(cot[...], wot[...]).astype(BF16))
    dq, dk, dv = softmax_backward(q, k, v, g, p_ref, heads)
    whole = jnp.concatenate([dq[:, :inner], dk[:, :inner], dv[:, :inner]], axis=1)
    for i in range(blocks.shape[0]):
        blocks[i] = whole[:, i * size : (i + 1) * size]
    grad = jnp.zeros(cot.shape, F32)
    for at, w in zip(shards, weights):
        lhs = jnp.concatenate([blocks[block] for block in at(idx)], axis=1)
        grad += dot(lhs, w[...])
    mine[:, :width] = (cot[...].astype(F32) + grad.astype(BF16).astype(F32)).astype(BF16)
    half = mine.shape[0] // 2
    rows = half // chips
    for q, out in enumerate(outs, 1):
        out[:rows] = mine[q * rows : (q + 1) * rows]
        out[rows:] = mine[half + q * rows : half + (q + 1) * rows]


def others_kernel(mine, *refs):
    parts, out = refs[-2::-1], refs[-1]
    half = mine.shape[0] // 2
    rows = half // (1 + len(parts))
    out[:rows] = mine[half : half + rows]
    for q, part in enumerate(parts, 1):
        out[q * rows : (q + 1) * rows] = part[rows:]


def whole_parts_kernel(chips, block, inner, width, mine, other, *refs):
    idx = place(chips)
    held, part = refs
    cot, so = held[:, width : 2 * width], held[:, 2 * width : 2 * width + inner]
    half = mine.shape[0] // 2
    near = all_patches(mine[:half], other[half:], idx[1], block)
    part[0] = dot_at(near[:, width:], cot).astype(BF16)
    part[1] = dot_at(so, near[:, :width]).astype(BF16)


def parts_kernel(chips, block, inner, width, mine, other, *refs):
    idx = place(chips)
    sent, refs = refs[:2], refs[2:]
    keep, send_x, send_y, heads, cols = refs
    half = mine.shape[0] // 2
    near = all_patches(mine[:half], other[half:], idx[1], block)
    far = all_patches(mine[half:], other[:half], idx[1], block)
    rows = near.shape[0]
    size = heads.shape[2]
    count, _, wide = cols.shape
    for i in range(2):
        if i == 0:
            lefts = [near[:, width:], far[:, width:]]
            rights = [part[:, width : 2 * width] for part in sent]
        else:
            lefts = [part[:, 2 * width : 2 * width + inner] for part in sent]
            rights = [near[:, :width], far[:, :width]]
        for at in range(2):
            held = slice(at * rows, (at + 1) * rows)
            for h in range(heads.shape[0]):
                heads[h, held] = lefts[at][:, h * size : (h + 1) * size]
            for r in range(count):
                cols[r, held] = rights[at][:, r * wide : (r + 1) * wide]
        left = jnp.concatenate([heads[idx[3] ^ (2 * q)] for q in range(chips)], axis=1)
        first = 1 if i == 0 else 2
        for r in range(count):
            full = dot_at(left, cols[idx[0] ^ r])
            value = jnp.concatenate([full[q * size : (q + 1) * size] for q in range(chips)], axis=1)
            if r & first:
                (send_x, send_y)[i][r // 2 if i == 0 else r - 2] = value.astype(BF16)
            else:
                keep[2 * i + (r > 0)] = value


def sum_first_kernel(keep, got_x, got_y, own, send_y, send_x):
    for i, (got, send) in enumerate(((got_x, send_y), (got_y, send_x))):
        own[i] = keep[2 * i] + got[0].astype(F32)
        send[...] = (keep[2 * i + 1] + got[1].astype(F32)).astype(BF16)


def sum_second_kernel(own, got_y, got_x, kept, *outs):
    totals = [own[0] + got_y[...].astype(F32), own[1] + got_x[...].astype(F32)]
    size = totals[0].shape[1] // (1 + len(outs))
    for q, out in enumerate((kept, *outs)):
        cut = [total[:, q * size : (q + 1) * size] for total in totals]
        out[...] = jnp.concatenate(cut, axis=1).astype(out.dtype)


def sum_kernel(own, *refs):
    got, outs = refs[:-2], refs[-2:]
    total = own[...]
    for part in got:
        total += part[...].astype(F32)
    size = outs[0].shape[1]
    for i, out in enumerate(outs):
        out[...] = total[:, i * size : (i + 1) * size]


def last_kernel(chips, patches, *refs):
    idx = place(chips)
    held, got, refs = refs[:chips][::-1], refs[chips], refs[chips + 1 :]
    (wos, qkv, p_ref, wot, hid), refs = refs[:5], refs[5:]
    block_far, out_far, grads_far, rows, block_out, grads, qs, ks, vs, gs, sems = refs
    inner, width = wos.shape
    frames = rows.shape[0] // patches
    block = patches // chips
    each = frames * block // 2
    for q in range(chips):
        value = all_patches(held[q][:each], got[q * each : (q + 1) * each], idx[1], block)
        for f in range(frames):
            low = pl.multiple_of(f * patches + (idx[2] ^ q) * block, block)
            rows[pl.ds(low, block)] = value[f * block : (f + 1) * block]
    value = rows[...]
    grad, attended = value[:, :width], value[:, width:]
    stores = started([(rows.at[:, pl.ds(0, width)], out_far)], sems.at[pl.ds(0, 1)])
    block_out[...] = (hid[...].astype(F32) + dot(attended, wot[...])).astype(BF16)
    stores += started([(block_out, block_far)], sems.at[pl.ds(1, 1)])
    put(gs, dot_weight(grad, wos[...]).astype(BF16))
    x = qkv[...]
    put(qs, x[:, :inner])
    put(ks, x[:, inner : 2 * inner])
    put(vs, x[:, 2 * inner :])
    dq, dk, dv = softmax_backward(qs, ks, vs, gs, p_ref, inner // DH)
    grads[...] = jnp.concatenate([dq[:, :inner], dk[:, :inner], dv[:, :inner]], axis=1)
    stores += started([(grads, grads_far)], sems.at[pl.ds(2, 1)])
    for copy in stores:
        copy.wait()


def flip(value, axis, bit):
    return lax.ppermute(value, axis, [(i, i ^ bit) for i in range(lax.axis_size(axis))])


def sems(n):
    return pltpu.SemaphoreType.DMA((n,))


def across(value, bits):
    n = lax.axis_size("seq")
    pairs = [
        (d * n + i, (d ^ bits[i % 2]) * n + i) for d in range(lax.axis_size("dp")) for i in range(n)
    ]
    return lax.ppermute(value, ("dp", "seq"), pairs)


def gather(weight, parts, chips):
    n = lax.axis_size("dp")
    rows, sent = parts[0].shape
    whole = [shape((len(parts) * rows, sent + PAD))]
    if n != 4:
        (near,) = call(join_rows_kernel, whole, from_chips(parts), small=True)
        weights = [lax.all_gather(weight, "dp", axis=0, tiled=True)]
        return near, flip(near, "seq", 1), weights, [lambda idx: [0]], 1
    half, width = weight.shape[0] // 2, weight.shape[1]
    side = across(weight, (1, 2))
    corner, own = call(
        functools.partial(half_kernel, chips),
        [shape((half, width)), shape((rows, sent))],
        [side, parts[0]],
        small=True,
    )
    corner = across(corner, (2, 1))
    (near,) = call(join_rows_kernel, whole, [own, *from_chips(parts)[1:]], small=True)
    weights = [weight, side, flip(side, "seq", 1), corner, flip(corner, "seq", 1)]

    def both(shard):
        return lambda idx: [2 * shard(idx), 2 * shard(idx) + 1]

    shards = [
        both(lambda idx: idx[0]),
        both(lambda idx: idx[0] ^ (1 + idx[1])),
        both(lambda idx: idx[0] ^ (2 - idx[1])),
        lambda idx: [2 * (idx[0] ^ 3) + idx[1]],
        lambda idx: [2 * (idx[0] ^ 3) + 1 - idx[1]],
    ]
    return near, flip(near, "seq", 1), weights, shards, 2 * n


def from_chips(parts):
    return [parts[0]] + [flip(parts[q], "seq", 2 * q) for q in range(1, len(parts))]


def reduced(keep, send_x, send_y):
    _, size, width = keep.shape
    step = shape((size, width))
    own, send_t, send_s = call(
        sum_first_kernel,
        [shape((2, size, width), F32), step, step],
        [keep, flip(send_x, "dp", 1), flip(send_y, "dp", 2)],
        small=True,
    )
    n = lax.axis_size("seq") // 2
    block = (size, 2 * width // n)
    own, *sends = call(
        sum_second_kernel,
        [shape(block, F32)] + [shape(block)] * (n - 1),
        [own, flip(send_t, "dp", 2), flip(send_s, "dp", 1)],
        small=True,
    )
    got = from_chips([own, *sends])[1:]
    return call(sum_kernel, [shape((size, width // n), F32)] * 2, [own, *got[::-1]], small=True)


def shards(tokens, spatial_qkv, wo_spatial, w_temporal, wo_temporal, cotangent):
    frames, patches, width = tokens.shape
    inner = wo_spatial.shape[0]
    heads = inner // DH
    padded = -(-inner // LANES) * LANES
    rows = frames * patches
    peers = FRAMES // frames
    chips = peers // 2
    group = patches // peers
    block = 2 * group
    n_dp, n_seq = lax.axis_size("dp"), lax.axis_size("seq")

    def held(columns, dtype=BF16):
        return pltpu.VMEM((rows, columns), dtype)

    wide = held(padded)
    attended = pltpu.VMEM((heads, rows, rows), F32)
    projection = pltpu.VMEM((inner, width), BF16)
    per_chip = rows // chips
    qkv_rows = spatial_qkv.reshape(rows, 3 * inner)
    sent = -(-(2 * width + inner) // LANES) * LANES
    *near, hidden, spatial_p = call(
        functools.partial(spatial_kernel, chips, patches),
        [shape((per_chip, sent))] * chips
        + [shape((rows, width)), shape((heads, rows, rows), F32)],
        [qkv_rows, tokens.reshape(rows, width), wo_spatial, cotangent.reshape(rows, width)],
        [held(width), held(width), held(3 * inner), projection]
        + [pltpu.VMEM((frames * chips, block, sent), BF16), held(width), attended]
        + [wide] * 3
        + [sems(6)],
        far_in=range(4),
        far_out=(chips, chips + 1),
    )
    near, far, weights, places, count = gather(w_temporal.T, near, chips)
    blocks = pltpu.VMEM((count, rows, 3 * inner // count), BF16)
    mine, *back = call(
        functools.partial(temporal_kernel, places, chips, group),
        [shape((rows, width + inner))] + [shape((per_chip, width + inner))] * (chips - 1),
        [near, far, wo_temporal, *weights],
        [held(width)] + [wide] * 4 + [attended, blocks],
        small=True,
    )
    other = flip(mine, "seq", 1)
    if n_dp == 4 and n_seq == peers:
        size = inner // n_seq
        keep, send_x, send_y = call(
            functools.partial(parts_kernel, chips, block, inner, width),
            [shape((n_dp, size, width), F32)] + [shape((2, size, width))] * 2,
            [mine, other, near, far],
            [
                pltpu.VMEM((n_seq, 2 * rows, size), BF16),
                pltpu.VMEM((n_dp, 2 * rows, width // n_dp), BF16),
            ],
            small=True,
        )
    else:
        (both,) = call(
            functools.partial(whole_parts_kernel, chips, block, inner, width),
            [shape((2, inner, width))],
            [mine, other, near],
            small=True,
        )
    back = from_chips([mine, *back])
    (others,) = call(
        others_kernel,
        [shape((rows // 2, width + inner))],
        [back[0], *back[:0:-1]],
        small=True,
    )
    block_out, tokens_grad, qkv_grad = call(
        functools.partial(last_kernel, chips, patches),
        [shape((rows, width)), shape((rows, width)), shape((rows, 3 * inner))],
        [*back[::-1], flip(others, "seq", 1), wo_spatial, qkv_rows, spatial_p, wo_temporal, hidden],
        [held(width + inner), held(width), held(3 * inner)] + [wide] * 4 + [sems(3)],
        far_out=range(3),
        small=True,
    )
    if n_dp == 4 and n_seq == peers:
        temporal_grad, spatial_grad = reduced(keep, send_x, send_y)
    else:
        both = lax.psum_scatter(both, "seq", scatter_dimension=1, tiled=True)
        both = lax.psum_scatter(both, "dp", scatter_dimension=2, tiled=True).astype(F32)
        temporal_grad, spatial_grad = both[0], both[1]
    return (
        block_out.reshape(frames, patches, width),
        tokens_grad.reshape(frames, patches, width),
        qkv_grad.reshape(frames, patches, 3 * inner),
        spatial_grad,
        temporal_grad,
    )


def solution(mesh):
    placed = (
        P(("dp", "seq"), None, None),
        P(("dp", "seq"), None, None),
        P(),
        P(None, "dp"),
        P(),
        P(("dp", "seq"), None, None),
    )
    return jax.shard_map(
        shards,
        mesh=mesh,
        in_specs=placed,
        out_specs=(
            P(("dp", "seq"), None, None),
            P(("dp", "seq"), None, None),
            P(("dp", "seq"), None, None),
            P("seq", "dp"),
            P("seq", "dp"),
        ),
        check_vma=False,
    )
```

```python
import functools
import math

import jax
import jax.numpy as jnp
from jax import lax
from jax.experimental import pallas as pl
from jax.experimental.pallas import tpu as pltpu
from jax.sharding import PartitionSpec as P

DH = 72
FRAMES = 16
LANES = 128
BF16 = jnp.bfloat16
F32 = jnp.float32
VMEM = pl.BlockSpec(memory_space=pltpu.VMEM)
SMEM = pl.BlockSpec(memory_space=pltpu.SMEM)
HBM = pl.BlockSpec(memory_space=pltpu.HBM)
PAD = 2 * LANES
WIDER = 1088
LIMIT = 16 * 1024 * 1024
MOST = 53 * 1024 * 1024


def dot(left, right):
    return jnp.dot(left, right, preferred_element_type=F32)


def dot_bt(left, right):
    return lax.dot_general(left, right, (((1,), (1,)), ((), ())), preferred_element_type=F32)


def dot_weight(rows, weight):
    return dot_bt(weight, rows).T


def dot_at(left, right):
    return lax.dot_general(left, right, (((0,), (0,)), ((), ())), preferred_element_type=F32)


def call(body, outs, args, scratch=(), us=0, far_in=(), far_out=(), small=False):
    moved = sum(math.prod(a.shape) * a.dtype.itemsize for a in (*args, *outs))
    near = [SMEM if a.dtype == jnp.int32 else VMEM for a in args]
    return pl.pallas_call(
        body,
        out_shape=outs,
        in_specs=[HBM if i in far_in else spec for i, spec in enumerate(near)],
        out_specs=[
            HBM if i in far_out else SMEM if out.dtype == jnp.int32 else VMEM
            for i, out in enumerate(outs)
        ],
        scratch_shapes=list(scratch),
        compiler_params=pltpu.CompilerParams(vmem_limit_bytes=LIMIT if small else MOST),
        cost_estimate=pl.CostEstimate(
            flops=us * 1150000000, bytes_accessed=moved if us else 0, transcendentals=0
        ),
    )(*args)


def started(pairs, sems):
    copies = [pltpu.make_async_copy(a, b, sems.at[i]) for i, (a, b) in enumerate(pairs)]
    for copy in copies:
        copy.start()
    return copies


def shape(dims, dtype=BF16):
    return jax.ShapeDtypeStruct(dims, dtype)


TOKEN = shape((1,), jnp.int32)


def window(head):
    low = head * DH // LANES * LANES
    high = -(-(head + 1) * DH // LANES) * LANES
    return low, high


def head_only(block, head):
    low, high = window(head)
    lane = lax.broadcasted_iota(jnp.int32, (1, high - low), 1) + low
    keep = (lane >= head * DH) & (lane < (head + 1) * DH)
    return jnp.where(keep, block, jnp.zeros_like(block))


def add_tiles(tiles, head, value):
    low, high = window(head)
    for at in range(low // LANES, high // LANES):
        part = value[:, at * LANES - low : (at + 1) * LANES - low]
        tiles[at] = part if tiles[at] is None else tiles[at] + part


def joined(tiles):
    return jnp.concatenate([tile.astype(BF16) for tile in tiles], axis=1)


def same_group(rows, kind):
    row = lax.broadcasted_iota(jnp.int32, (rows, rows), 0)
    col = lax.broadcasted_iota(jnp.int32, (rows, rows), 1)
    how, size = kind
    return row // size == col // size if how == "block" else row % size == col % size


def softmax_forward(q_ref, k_ref, v_ref, p_ref, heads, kind):
    rows = q_ref.shape[0]
    mask = same_group(rows, kind)
    tiles = [None] * (q_ref.shape[1] // LANES)
    for head in range(heads):
        low, high = window(head)
        s = dot_bt(q_ref[:, low:high], head_only(k_ref[:, low:high], head)) * (1.0 / math.sqrt(DH))
        s = jnp.where(mask, s, -jnp.inf)
        e = jnp.exp(s - jnp.max(s, axis=1, keepdims=True))
        p = e / jnp.sum(e, axis=1, keepdims=True)
        p_ref[head] = p
        add_tiles(tiles, head, dot(p.astype(BF16), head_only(v_ref[:, low:high], head)))
    return joined(tiles)


def softmax_backward(q_ref, k_ref, v_ref, g_ref, p_ref, heads):
    count = q_ref.shape[1] // LANES
    dq, dk, dv = [None] * count, [None] * count, [None] * count
    for head in range(heads):
        low, high = window(head)
        p = p_ref[head]
        g = head_only(g_ref[:, low:high], head)
        add_tiles(dv, head, dot_at(p.astype(BF16), g))
        dp = dot_bt(g, v_ref[:, low:high])
        ds = p * (dp - jnp.sum(p * dp, axis=1, keepdims=True)) * (1.0 / math.sqrt(DH))
        ds = ds.astype(BF16)
        add_tiles(dq, head, dot(ds, head_only(k_ref[:, low:high], head)))
        add_tiles(dk, head, dot_at(ds, head_only(q_ref[:, low:high], head)))
    return joined(dq), joined(dk), joined(dv)


def put(ref, value):
    width = value.shape[1]
    ref[:, width // LANES * LANES :] = jnp.zeros(
        (ref.shape[0], ref.shape[1] - width // LANES * LANES), ref.dtype
    )
    ref[:, :width] = value


def place(chips):
    seq = lax.axis_index("seq")
    return lax.axis_index("dp"), seq % 2, seq % (2 * chips) // 2, seq


def spatial_kernel(chips, patches, *refs):
    idx = place(chips)
    far, outs, refs = refs[:4], refs[4 : 4 + chips], refs[4 + chips :]
    hid_far, p_far, tok, cot, qkv, wos, held, hid, p_ref, qs, ks, vs, sems = refs
    inner, width = wos.shape
    count, block, _ = held.shape
    loads = started(zip(far, (qkv, tok, wos, cot)), sems)
    loads[0].wait()
    x = qkv[...]
    put(qs, x[:, :inner])
    put(ks, x[:, inner : 2 * inner])
    put(vs, x[:, 2 * inner :])
    o = softmax_forward(qs, ks, vs, p_ref, inner // DH, ("block", patches))[:, :inner]
    stores = started([(p_ref, p_far)], sems.at[pl.ds(4, 1)])
    for at in range(3):
        loads[1 + at].wait()
    hid[...] = (tok[...].astype(F32) + dot(o, wos[...])).astype(BF16)
    for at in range(count):
        rows = slice(at * block, (at + 1) * block)
        held[at, :, :width] = hid[rows]
        held[at, :, width : 2 * width] = cot[rows]
        held[at, :, 2 * width : 2 * width + inner] = o[rows]
    stores += started([(hid, hid_far)], sems.at[pl.ds(5, 1)])
    for q in range(chips):
        for f in range(count // chips):
            rows = slice(f * block, (f + 1) * block)
            outs[q][rows] = held[f * chips + (idx[2] ^ q)]
    for copy in stores:
        copy.wait()


def own_patches(ref, core, block):
    rows, width = ref.shape
    value = ref[...].astype(F32).reshape(rows // block, block, width)
    value = jnp.where(core == 0, value[:, : block // 2], value[:, block // 2 :])
    return value.reshape(rows // 2, width)


def all_patches(mine, other, core, block):
    rows, width = mine.shape
    mine = mine.astype(F32).reshape(2 * rows // block, block // 2, width)
    other = other.astype(F32).reshape(2 * rows // block, block // 2, width)
    first, second = jnp.where(core == 0, mine, other), jnp.where(core == 0, other, mine)
    return jnp.concatenate([first, second], axis=1).reshape(2 * rows, width).astype(BF16)


def half_kernel(chips, got, own, half, kept):
    rows = half.shape[0]
    core = place(chips)[1]
    half[...] = jnp.where(core == 0, got[:rows].astype(F32), got[rows:].astype(F32)).astype(BF16)
    kept[...] = own[...]


def join_rows_kernel(*refs):
    out, low = refs[-1], 0
    for ref in refs[:-1]:
        out[low : low + ref.shape[0], : ref.shape[1]] = ref[...]
        low += ref.shape[0]


def temporal_kernel(shards, chips, group, near, far, wot, *refs):
    idx = place(chips)
    weights, refs = refs[: len(shards)], refs[len(shards) :]
    (mine, *outs), (cot, q, k, v, g, p_ref, blocks) = refs[:chips], refs[chips:]
    inner, width = wot.shape
    heads = inner // DH
    value = [own_patches(ref, idx[1], 2 * group) for ref in (near, far)]
    value = jnp.concatenate(value, axis=0).astype(BF16)
    hidden = value[:, :width]
    cot[...] = value[:, width : 2 * width]
    size = blocks.shape[2]
    for at, w in zip(shards, weights):
        value = dot_weight(hidden, w[...]).astype(BF16)
        for i, block in enumerate(at(idx)):
            blocks[block] = value[:, i * size : (i + 1) * size]
    whole = jnp.concatenate([blocks[i] for i in range(blocks.shape[0])], axis=1)
    put(q, whole[:, :inner])
    put(k, whole[:, inner : 2 * inner])
    put(v, whole[:, 2 * inner :])
    mine[:, width:] = softmax_forward(q, k, v, p_ref, heads, ("cycle", group))[:, :inner]
    put(g, dot_weight(cot[...], wot[...]).astype(BF16))
    dq, dk, dv = softmax_backward(q, k, v, g, p_ref, heads)
    whole = jnp.concatenate([dq[:, :inner], dk[:, :inner], dv[:, :inner]], axis=1)
    for i in range(blocks.shape[0]):
        blocks[i] = whole[:, i * size : (i + 1) * size]
    grad = jnp.zeros(cot.shape, F32)
    for at, w in zip(shards, weights):
        lhs = jnp.concatenate([blocks[block] for block in at(idx)], axis=1)
        grad += dot(lhs, w[...])
    mine[:, :width] = (cot[...].astype(F32) + grad.astype(BF16).astype(F32)).astype(BF16)
    half = mine.shape[0] // 2
    rows = half // chips
    for q, out in enumerate(outs, 1):
        out[:rows] = mine[q * rows : (q + 1) * rows]
        out[rows:] = mine[half + q * rows : half + (q + 1) * rows]


def others_kernel(mine, *refs):
    parts, out = refs[-2::-1], refs[-1]
    half = mine.shape[0] // 2
    rows = half // (1 + len(parts))
    width = mine.shape[1]
    out[:rows, :width] = mine[half : half + rows]
    for q, part in enumerate(parts, 1):
        out[q * rows : (q + 1) * rows, :width] = part[rows:]


def whole_parts_kernel(chips, block, inner, width, mine, other, *refs):
    idx = place(chips)
    held, part = refs
    cot, so = held[:, width : 2 * width], held[:, 2 * width : 2 * width + inner]
    half = mine.shape[0] // 2
    near = all_patches(mine[:half], other[half:], idx[1], block)
    part[0] = dot_at(near[:, width:], cot).astype(BF16)
    part[1] = dot_at(so, near[:, :width]).astype(BF16)


def parts_kernel(chips, block, inner, width, mine, other, *refs):
    idx = place(chips)
    sent, refs = refs[:2], refs[2:]
    keep, send, heads, cols = refs
    half = mine.shape[0] // 2
    near = all_patches(mine[:half], other[half:], idx[1], block)
    far = all_patches(mine[half:], other[:half], idx[1], block)
    rows = near.shape[0]
    size = heads.shape[2]
    count, _, wide = cols.shape
    for i in range(2):
        if i == 0:
            lefts = [near[:, width:], far[:, width:]]
            rights = [part[:, width : 2 * width] for part in sent]
        else:
            lefts = [part[:, 2 * width : 2 * width + inner] for part in sent]
            rights = [near[:, :width], far[:, :width]]
        for at in range(2):
            held = slice(at * rows, (at + 1) * rows)
            for h in range(heads.shape[0]):
                heads[h, held] = lefts[at][:, h * size : (h + 1) * size]
            for r in range(count):
                cols[r, held] = rights[at][:, r * wide : (r + 1) * wide]
        left = jnp.concatenate([heads[idx[3] ^ (2 * q)] for q in range(chips)], axis=1)
        for at, r in enumerate((0, 2 - idx[1], 1 + idx[1], 3)):
            full = dot_at(left, cols[idx[0] ^ r])
            value = jnp.concatenate([full[q * size : (q + 1) * size] for q in range(chips)], axis=1)
            if at < 2:
                keep[2 * i + at] = value
            else:
                send[2 * i + at - 2] = value.astype(BF16)


def sum_first_kernel(keep, got, own, send):
    for i in range(2):
        own[i] = keep[2 * i] + got[2 * i].astype(F32)
        send[i] = (keep[2 * i + 1] + got[2 * i + 1].astype(F32)).astype(BF16)


def sum_second_kernel(own, got, kept, *outs):
    totals = [own[i] + got[i].astype(F32) for i in range(2)]
    size = totals[0].shape[1] // (1 + len(outs))
    for q, out in enumerate((kept, *outs)):
        cut = [total[:, q * size : (q + 1) * size] for total in totals]
        out[...] = jnp.concatenate(cut, axis=1).astype(out.dtype)


def sum_kernel(own, *refs):
    got, outs = refs[:-2], refs[-2:]
    total = own[...]
    for part in got:
        total += part[...].astype(F32)
    size = outs[0].shape[1]
    for i, out in enumerate(outs):
        out[...] = total[:, i * size : (i + 1) * size]


def last_kernel(chips, patches, *refs):
    idx = place(chips)
    held, got, refs = refs[:chips][::-1], refs[chips], refs[chips + 1 :]
    (wos, qkv, p_ref, wot, hid), refs = refs[:5], refs[5:]
    block_far, out_far, grads_far, rows, block_out, grads, qs, ks, vs, gs, sems = refs
    inner, width = wos.shape
    frames = rows.shape[0] // patches
    block = patches // chips
    each = frames * block // 2
    for q in range(chips):
        other = got[q * each : (q + 1) * each, : rows.shape[1]]
        value = all_patches(held[q][:each], other, idx[1], block)
        for f in range(frames):
            low = pl.multiple_of(f * patches + (idx[2] ^ q) * block, block)
            rows[pl.ds(low, block)] = value[f * block : (f + 1) * block]
    value = rows[...]
    grad, attended = value[:, :width], value[:, width:]
    stores = started([(rows.at[:, pl.ds(0, width)], out_far)], sems.at[pl.ds(0, 1)])
    block_out[...] = (hid[...].astype(F32) + dot(attended, wot[...])).astype(BF16)
    stores += started([(block_out, block_far)], sems.at[pl.ds(1, 1)])
    put(gs, dot_bt(grad, wos[...]).astype(BF16))
    x = qkv[...]
    put(qs, x[:, :inner])
    put(ks, x[:, inner : 2 * inner])
    put(vs, x[:, 2 * inner :])
    dq, dk, dv = softmax_backward(qs, ks, vs, gs, p_ref, inner // DH)
    grads[...] = jnp.concatenate([dq[:, :inner], dk[:, :inner], dv[:, :inner]], axis=1)
    stores += started([(grads, grads_far)], sems.at[pl.ds(2, 1)])
    for copy in stores:
        copy.wait()


def flip(value, axis, bit):
    return lax.ppermute(value, axis, [(i, i ^ bit) for i in range(lax.axis_size(axis))])


def sems(n):
    return pltpu.SemaphoreType.DMA((n,))


def across(value, bits):
    n = lax.axis_size("seq")
    pairs = [
        (d * n + i, (d ^ bits[i % 2]) * n + i) for d in range(lax.axis_size("dp")) for i in range(n)
    ]
    return lax.ppermute(value, ("dp", "seq"), pairs)


def gather(weight, parts, chips):
    n = lax.axis_size("dp")
    rows, sent = parts[0].shape
    whole = [shape((len(parts) * rows, sent + PAD))]
    if n != 4:
        (near,) = call(join_rows_kernel, whole, from_chips(parts), small=True)
        weights = [lax.all_gather(weight, "dp", axis=0, tiled=True)]
        return near, flip(near, "seq", 1), weights, [lambda idx: [0]], 1
    half, width = weight.shape[0] // 2, weight.shape[1]
    side = across(weight, (1, 2))
    corner, own = call(
        functools.partial(half_kernel, chips),
        [shape((half, width)), shape((rows, sent))],
        [side, parts[0]],
        small=True,
    )
    corner = across(corner, (2, 1))
    (near,) = call(join_rows_kernel, whole, [own, *from_chips(parts)[1:]], small=True)
    weights = [weight, side, flip(side, "seq", 1), corner, flip(corner, "seq", 1)]

    def both(shard):
        return lambda idx: [2 * shard(idx), 2 * shard(idx) + 1]

    shards = [
        both(lambda idx: idx[0]),
        both(lambda idx: idx[0] ^ (1 + idx[1])),
        both(lambda idx: idx[0] ^ (2 - idx[1])),
        lambda idx: [2 * (idx[0] ^ 3) + idx[1]],
        lambda idx: [2 * (idx[0] ^ 3) + 1 - idx[1]],
    ]
    return near, flip(near, "seq", 1), weights, shards, 2 * n


def from_chips(parts):
    return [parts[0]] + [flip(parts[q], "seq", 2 * q) for q in range(1, len(parts))]


def reduced(keep, send):
    _, size, width = keep.shape
    step = (2, size, width)
    own, send = call(
        sum_first_kernel,
        [shape(step, F32), shape(step)],
        [keep, across(send, (1, 2))],
        small=True,
    )
    n = lax.axis_size("seq") // 2
    block = (size, 2 * width // n)
    own, *sends = call(
        sum_second_kernel,
        [shape(block, F32)] + [shape(block)] * (n - 1),
        [own, across(send, (2, 1))],
        small=True,
    )
    got = from_chips([own, *sends])[1:]
    return call(sum_kernel, [shape((size, width // n), F32)] * 2, [own, *got[::-1]], small=True)


def shards(tokens, spatial_qkv, wo_spatial, w_temporal, wo_temporal, cotangent):
    frames, patches, width = tokens.shape
    inner = wo_spatial.shape[0]
    heads = inner // DH
    padded = -(-inner // LANES) * LANES
    rows = frames * patches
    peers = FRAMES // frames
    chips = peers // 2
    group = patches // peers
    block = 2 * group
    n_dp, n_seq = lax.axis_size("dp"), lax.axis_size("seq")

    def held(columns, dtype=BF16):
        return pltpu.VMEM((rows, columns), dtype)

    wide = held(padded)
    attended = pltpu.VMEM((heads, rows, rows), F32)
    projection = pltpu.VMEM((inner, width), BF16)
    per_chip = rows // chips
    qkv_rows = spatial_qkv.reshape(rows, 3 * inner)
    sent = -(-(2 * width + inner) // LANES) * LANES
    *near, hidden, spatial_p = call(
        functools.partial(spatial_kernel, chips, patches),
        [shape((per_chip, sent))] * chips
        + [shape((rows, width)), shape((heads, rows, rows), F32)],
        [qkv_rows, tokens.reshape(rows, width), wo_spatial, cotangent.reshape(rows, width)],
        [held(width), held(width), held(3 * inner), projection]
        + [pltpu.VMEM((frames * chips, block, sent), BF16), held(width), attended]
        + [wide] * 3
        + [sems(6)],
        far_in=range(4),
        far_out=(chips, chips + 1),
    )
    near, far, weights, places, count = gather(w_temporal.T, near, chips)
    blocks = pltpu.VMEM((count, rows, 3 * inner // count), BF16)
    mine, *back = call(
        functools.partial(temporal_kernel, places, chips, group),
        [shape((rows, width + inner))] + [shape((per_chip, width + inner))] * (chips - 1),
        [near, far, wo_temporal, *weights],
        [held(width)] + [wide] * 4 + [attended, blocks],
        small=True,
    )
    other = flip(mine, "seq", 1)
    if n_dp == 4 and n_seq == peers:
        size = inner // n_seq
        keep, send = call(
            functools.partial(parts_kernel, chips, block, inner, width),
            [shape((4, size, width), F32), shape((4, size, width))],
            [mine, other, near, far],
            [
                pltpu.VMEM((n_seq, 2 * rows, size), BF16),
                pltpu.VMEM((n_dp, 2 * rows, width // n_dp), BF16),
            ],
            small=True,
        )
    else:
        (both,) = call(
            functools.partial(whole_parts_kernel, chips, block, inner, width),
            [shape((2, inner, width))],
            [mine, other, near],
            small=True,
        )
    back = from_chips([mine, *back])
    (others,) = call(
        others_kernel,
        [shape((rows // 2, width + inner + WIDER))],
        [back[0], *back[:0:-1]],
        small=True,
    )
    block_out, tokens_grad, qkv_grad = call(
        functools.partial(last_kernel, chips, patches),
        [shape((rows, width)), shape((rows, width)), shape((rows, 3 * inner))],
        [*back[::-1], flip(others, "seq", 1), wo_spatial, qkv_rows, spatial_p, wo_temporal, hidden],
        [held(width + inner), held(width), held(3 * inner)] + [wide] * 4 + [sems(3)],
        far_out=range(3),
        small=True,
    )
    if n_dp == 4 and n_seq == peers:
        temporal_grad, spatial_grad = reduced(keep, send)
    else:
        both = lax.psum_scatter(both, "seq", scatter_dimension=1, tiled=True)
        both = lax.psum_scatter(both, "dp", scatter_dimension=2, tiled=True).astype(F32)
        temporal_grad, spatial_grad = both[0], both[1]
    return (
        block_out.reshape(frames, patches, width),
        tokens_grad.reshape(frames, patches, width),
        qkv_grad.reshape(frames, patches, 3 * inner),
        spatial_grad,
        temporal_grad,
    )


def solution(mesh):
    placed = (
        P(("dp", "seq"), None, None),
        P(("dp", "seq"), None, None),
        P(),
        P(None, "dp"),
        P(),
        P(("dp", "seq"), None, None),
    )
    return jax.shard_map(
        shards,
        mesh=mesh,
        in_specs=placed,
        out_specs=(
            P(("dp", "seq"), None, None),
            P(("dp", "seq"), None, None),
            P(("dp", "seq"), None, None),
            P("seq", "dp"),
            P("seq", "dp"),
        ),
        check_vma=False,
    )
```

```python
import functools
import math

import jax
import jax.numpy as jnp
from jax import lax
from jax.experimental import pallas as pl
from jax.experimental.pallas import tpu as pltpu
from jax.sharding import PartitionSpec as P

DH = 72
FRAMES = 16
LANES = 128
BF16 = jnp.bfloat16
F32 = jnp.float32
VMEM = pl.BlockSpec(memory_space=pltpu.VMEM)
SMEM = pl.BlockSpec(memory_space=pltpu.SMEM)
HBM = pl.BlockSpec(memory_space=pltpu.HBM)
PAD = 2 * LANES
LIMIT = 16 * 1024 * 1024
MOST = 53 * 1024 * 1024


def dot(left, right):
    return jnp.dot(left, right, preferred_element_type=F32)


def dot_bt(left, right):
    return lax.dot_general(left, right, (((1,), (1,)), ((), ())), preferred_element_type=F32)


def dot_weight(rows, weight):
    return dot_bt(weight, rows).T


def dot_at(left, right):
    return lax.dot_general(left, right, (((0,), (0,)), ((), ())), preferred_element_type=F32)


def call(body, outs, args, scratch=(), us=0, far_in=(), far_out=(), small=False):
    moved = sum(math.prod(a.shape) * a.dtype.itemsize for a in (*args, *outs))
    near = [SMEM if a.dtype == jnp.int32 else VMEM for a in args]
    return pl.pallas_call(
        body,
        out_shape=outs,
        in_specs=[HBM if i in far_in else spec for i, spec in enumerate(near)],
        out_specs=[
            HBM if i in far_out else SMEM if out.dtype == jnp.int32 else VMEM
            for i, out in enumerate(outs)
        ],
        scratch_shapes=list(scratch),
        compiler_params=pltpu.CompilerParams(vmem_limit_bytes=LIMIT if small else MOST),
        cost_estimate=pl.CostEstimate(
            flops=us * 1150000000, bytes_accessed=moved if us else 0, transcendentals=0
        ),
    )(*args)


def started(pairs, sems):
    copies = [pltpu.make_async_copy(a, b, sems.at[i]) for i, (a, b) in enumerate(pairs)]
    for copy in copies:
        copy.start()
    return copies


def shape(dims, dtype=BF16):
    return jax.ShapeDtypeStruct(dims, dtype)


TOKEN = shape((1,), jnp.int32)


def window(head):
    low = head * DH // LANES * LANES
    high = -(-(head + 1) * DH // LANES) * LANES
    return low, high


def head_only(block, head):
    low, high = window(head)
    lane = lax.broadcasted_iota(jnp.int32, (1, high - low), 1) + low
    keep = (lane >= head * DH) & (lane < (head + 1) * DH)
    return jnp.where(keep, block, jnp.zeros_like(block))


def add_tiles(tiles, head, value):
    low, high = window(head)
    for at in range(low // LANES, high // LANES):
        part = value[:, at * LANES - low : (at + 1) * LANES - low]
        tiles[at] = part if tiles[at] is None else tiles[at] + part


def joined(tiles):
    return jnp.concatenate([tile.astype(BF16) for tile in tiles], axis=1)


def same_group(rows, kind):
    row = lax.broadcasted_iota(jnp.int32, (rows, rows), 0)
    col = lax.broadcasted_iota(jnp.int32, (rows, rows), 1)
    how, size = kind
    return row // size == col // size if how == "block" else row % size == col % size


def softmax_forward(q_ref, k_ref, v_ref, p_ref, heads, kind):
    rows = q_ref.shape[0]
    mask = same_group(rows, kind)
    tiles = [None] * (q_ref.shape[1] // LANES)
    for head in range(heads):
        low, high = window(head)
        s = dot_bt(q_ref[:, low:high], head_only(k_ref[:, low:high], head)) * (1.0 / math.sqrt(DH))
        s = jnp.where(mask, s, -jnp.inf)
        e = jnp.exp(s - jnp.max(s, axis=1, keepdims=True))
        p = e / jnp.sum(e, axis=1, keepdims=True)
        p_ref[head] = p
        add_tiles(tiles, head, dot(p.astype(BF16), head_only(v_ref[:, low:high], head)))
    return joined(tiles)


def softmax_backward(q_ref, k_ref, v_ref, g_ref, p_ref, heads):
    count = q_ref.shape[1] // LANES
    dq, dk, dv = [None] * count, [None] * count, [None] * count
    for head in range(heads):
        low, high = window(head)
        p = p_ref[head]
        g = head_only(g_ref[:, low:high], head)
        add_tiles(dv, head, dot_at(p.astype(BF16), g))
        dp = dot_bt(g, v_ref[:, low:high])
        ds = p * (dp - jnp.sum(p * dp, axis=1, keepdims=True)) * (1.0 / math.sqrt(DH))
        ds = ds.astype(BF16)
        add_tiles(dq, head, dot(ds, head_only(k_ref[:, low:high], head)))
        add_tiles(dk, head, dot_at(ds, head_only(q_ref[:, low:high], head)))
    return joined(dq), joined(dk), joined(dv)


def put(ref, value):
    width = value.shape[1]
    ref[:, width // LANES * LANES :] = jnp.zeros(
        (ref.shape[0], ref.shape[1] - width // LANES * LANES), ref.dtype
    )
    ref[:, :width] = value


def place(chips):
    seq = lax.axis_index("seq")
    return lax.axis_index("dp"), seq % 2, seq % (2 * chips) // 2, seq


def spatial_kernel(chips, patches, *refs):
    idx = place(chips)
    far, outs, refs = refs[:4], refs[4 : 4 + chips], refs[4 + chips :]
    hid_far, p_far, tok, cot, qkv, wos, held, hid, p_ref, qs, ks, vs, sems = refs
    inner, width = wos.shape
    count, block, _ = held.shape
    loads = started(zip(far, (qkv, tok, wos, cot)), sems)
    loads[0].wait()
    x = qkv[...]
    put(qs, x[:, :inner])
    put(ks, x[:, inner : 2 * inner])
    put(vs, x[:, 2 * inner :])
    o = softmax_forward(qs, ks, vs, p_ref, inner // DH, ("block", patches))[:, :inner]
    stores = started([(p_ref, p_far)], sems.at[pl.ds(4, 1)])
    for at in range(3):
        loads[1 + at].wait()
    hid[...] = (tok[...].astype(F32) + dot(o, wos[...])).astype(BF16)
    for at in range(count):
        rows = slice(at * block, (at + 1) * block)
        held[at, :, :width] = hid[rows]
        held[at, :, width : 2 * width] = cot[rows]
        held[at, :, 2 * width : 2 * width + inner] = o[rows]
    stores += started([(hid, hid_far)], sems.at[pl.ds(5, 1)])
    for q in range(chips):
        for f in range(count // chips):
            rows = slice(f * block, (f + 1) * block)
            outs[q][rows] = held[f * chips + (idx[2] ^ q)]
    for copy in stores:
        copy.wait()


def own_patches(ref, core, block):
    rows, width = ref.shape
    value = ref[...].astype(F32).reshape(rows // block, block, width)
    value = jnp.where(core == 0, value[:, : block // 2], value[:, block // 2 :])
    return value.reshape(rows // 2, width)


def all_patches(mine, other, core, block):
    rows, width = mine.shape
    mine = mine.astype(F32).reshape(2 * rows // block, block // 2, width)
    other = other.astype(F32).reshape(2 * rows // block, block // 2, width)
    first, second = jnp.where(core == 0, mine, other), jnp.where(core == 0, other, mine)
    return jnp.concatenate([first, second], axis=1).reshape(2 * rows, width).astype(BF16)


def half_kernel(chips, got, own, half, kept):
    rows = half.shape[0]
    core = place(chips)[1]
    half[...] = jnp.where(core == 0, got[:rows].astype(F32), got[rows:].astype(F32)).astype(BF16)
    kept[...] = own[...]


def join_rows_kernel(*refs):
    out, low = refs[-1], 0
    for ref in refs[:-1]:
        out[low : low + ref.shape[0], : ref.shape[1]] = ref[...]
        low += ref.shape[0]


def temporal_kernel(shards, chips, group, near, far, wot, *refs):
    idx = place(chips)
    weights, refs = refs[: len(shards)], refs[len(shards) :]
    (mine, *outs), (cot, q, k, v, g, p_ref, blocks) = refs[:chips], refs[chips:]
    inner, width = wot.shape
    heads = inner // DH
    value = [own_patches(ref, idx[1], 2 * group) for ref in (near, far)]
    value = jnp.concatenate(value, axis=0).astype(BF16)
    hidden = value[:, :width]
    cot[...] = value[:, width : 2 * width]
    size = blocks.shape[2]
    for at, w in zip(shards, weights):
        value = dot_weight(hidden, w[...]).astype(BF16)
        for i, block in enumerate(at(idx)):
            blocks[block] = value[:, i * size : (i + 1) * size]
    whole = jnp.concatenate([blocks[i] for i in range(blocks.shape[0])], axis=1)
    put(q, whole[:, :inner])
    put(k, whole[:, inner : 2 * inner])
    put(v, whole[:, 2 * inner :])
    mine[:, width:] = softmax_forward(q, k, v, p_ref, heads, ("cycle", group))[:, :inner]
    put(g, dot_weight(cot[...], wot[...]).astype(BF16))
    dq, dk, dv = softmax_backward(q, k, v, g, p_ref, heads)
    whole = jnp.concatenate([dq[:, :inner], dk[:, :inner], dv[:, :inner]], axis=1)
    for i in range(blocks.shape[0]):
        blocks[i] = whole[:, i * size : (i + 1) * size]
    grad = jnp.zeros(cot.shape, F32)
    for at, w in zip(shards, weights):
        lhs = jnp.concatenate([blocks[block] for block in at(idx)], axis=1)
        grad += dot(lhs, w[...])
    mine[:, :width] = (cot[...].astype(F32) + grad.astype(BF16).astype(F32)).astype(BF16)
    half = mine.shape[0] // 2
    rows = half // chips
    for q, out in enumerate(outs, 1):
        out[:rows] = mine[q * rows : (q + 1) * rows]
        out[rows:] = mine[half + q * rows : half + (q + 1) * rows]


def others_kernel(mine, *refs):
    parts, out = refs[-2::-1], refs[-1]
    half = mine.shape[0] // 2
    rows = half // (1 + len(parts))
    out[:rows] = mine[half : half + rows]
    for q, part in enumerate(parts, 1):
        out[q * rows : (q + 1) * rows] = part[rows:]


def whole_parts_kernel(chips, block, inner, width, mine, other, *refs):
    idx = place(chips)
    held, part = refs
    cot, so = held[:, width : 2 * width], held[:, 2 * width : 2 * width + inner]
    half = mine.shape[0] // 2
    near = all_patches(mine[:half], other[half:], idx[1], block)
    part[0] = dot_at(near[:, width:], cot).astype(BF16)
    part[1] = dot_at(so, near[:, :width]).astype(BF16)


def products(idx, core, chips, block, inner, width, rows, first, second, heads, cols):
    held = [own_patches(ref, core, block)[:, width:] for ref in (first, second)]
    held = jnp.concatenate(held, axis=0).astype(BF16)
    size = heads.shape[2]
    count, _, wide = cols.shape
    for i in range(2):
        left = rows[:, width:] if i == 0 else held[:, width : width + inner]
        right = held[:, :width] if i == 0 else rows[:, :width]
        for h in range(heads.shape[0]):
            heads[h] = left[:, h * size : (h + 1) * size]
        for r in range(count):
            cols[r] = right[:, r * wide : (r + 1) * wide]
        left = jnp.concatenate([heads[idx[3] ^ (2 * q)] for q in range(chips)], axis=1)
        for r in range(count):
            full = dot_at(left, cols[idx[0] ^ r])
            value = [full[q * size : (q + 1) * size] for q in range(chips)]
            yield i, r, jnp.concatenate(value, axis=1)


def own_parts_kernel(chips, block, inner, width, mine, near, far, part, heads, cols):
    idx = place(chips)
    sizes = (chips, block, inner, width)
    for i, r, value in products(idx, idx[1], *sizes, mine, near, far, heads, cols):
        part[4 * i + r] = value


def parts_kernel(chips, block, inner, width, other, near, far, part, *refs):
    keep, send_x, send_y, heads, cols = refs
    idx = place(chips)
    sizes = (chips, block, inner, width)
    for i, r, value in products(idx, 1 - idx[1], *sizes, other, far, near, heads, cols):
        value += part[4 * i + r]
        if r & (1 if i == 0 else 2):
            (send_x, send_y)[i][r // 2 if i == 0 else r - 2] = value.astype(BF16)
        else:
            keep[2 * i + (r > 0)] = value


def sum_first_kernel(keep, got_x, got_y, own, send_y, send_x):
    for i, (got, send) in enumerate(((got_x, send_y), (got_y, send_x))):
        own[i] = keep[2 * i] + got[0].astype(F32)
        send[...] = (keep[2 * i + 1] + got[1].astype(F32)).astype(BF16)


def sum_second_kernel(own, got_y, got_x, kept, *outs):
    totals = [own[0] + got_y[...].astype(F32), own[1] + got_x[...].astype(F32)]
    size = totals[0].shape[1] // (1 + len(outs))
    for q, out in enumerate((kept, *outs)):
        cut = [total[:, q * size : (q + 1) * size] for total in totals]
        out[...] = jnp.concatenate(cut, axis=1).astype(out.dtype)


def sum_kernel(own, *refs):
    got, outs = refs[:-2], refs[-2:]
    total = own[...]
    for part in got:
        total += part[...].astype(F32)
    size = outs[0].shape[1]
    for i, out in enumerate(outs):
        out[...] = total[:, i * size : (i + 1) * size]


def last_kernel(chips, patches, *refs):
    idx = place(chips)
    held, got, refs = refs[:chips][::-1], refs[chips], refs[chips + 1 :]
    (wos, qkv, p_ref, wot, hid), refs = refs[:5], refs[5:]
    block_far, out_far, grads_far, rows, block_out, grads, qs, ks, vs, gs, sems = refs
    inner, width = wos.shape
    frames = rows.shape[0] // patches
    block = patches // chips
    each = frames * block // 2
    for q in range(chips):
        value = all_patches(held[q][:each], got[q * each : (q + 1) * each], idx[1], block)
        for f in range(frames):
            low = pl.multiple_of(f * patches + (idx[2] ^ q) * block, block)
            rows[pl.ds(low, block)] = value[f * block : (f + 1) * block]
    value = rows[...]
    grad, attended = value[:, :width], value[:, width:]
    stores = started([(rows.at[:, pl.ds(0, width)], out_far)], sems.at[pl.ds(0, 1)])
    block_out[...] = (hid[...].astype(F32) + dot(attended, wot[...])).astype(BF16)
    stores += started([(block_out, block_far)], sems.at[pl.ds(1, 1)])
    put(gs, dot_bt(grad, wos[...]).astype(BF16))
    x = qkv[...]
    put(qs, x[:, :inner])
    put(ks, x[:, inner : 2 * inner])
    put(vs, x[:, 2 * inner :])
    dq, dk, dv = softmax_backward(qs, ks, vs, gs, p_ref, inner // DH)
    grads[...] = jnp.concatenate([dq[:, :inner], dk[:, :inner], dv[:, :inner]], axis=1)
    stores += started([(grads, grads_far)], sems.at[pl.ds(2, 1)])
    for copy in stores:
        copy.wait()


def flip(value, axis, bit):
    return lax.ppermute(value, axis, [(i, i ^ bit) for i in range(lax.axis_size(axis))])


def sems(n):
    return pltpu.SemaphoreType.DMA((n,))


def across(value, bits):
    n = lax.axis_size("seq")
    pairs = [
        (d * n + i, (d ^ bits[i % 2]) * n + i) for d in range(lax.axis_size("dp")) for i in range(n)
    ]
    return lax.ppermute(value, ("dp", "seq"), pairs)


def gather(weight, parts, chips):
    n = lax.axis_size("dp")
    rows, sent = parts[0].shape
    whole = [shape((len(parts) * rows, sent + PAD))]
    if n != 4:
        (near,) = call(join_rows_kernel, whole, from_chips(parts), small=True)
        weights = [lax.all_gather(weight, "dp", axis=0, tiled=True)]
        return near, flip(near, "seq", 1), weights, [lambda idx: [0]], 1
    half, width = weight.shape[0] // 2, weight.shape[1]
    side = across(weight, (1, 2))
    corner, own = call(
        functools.partial(half_kernel, chips),
        [shape((half, width)), shape((rows, sent))],
        [side, parts[0]],
        small=True,
    )
    corner = across(corner, (2, 1))
    (near,) = call(join_rows_kernel, whole, [own, *from_chips(parts)[1:]], small=True)
    weights = [weight, side, flip(side, "seq", 1), corner, flip(corner, "seq", 1)]

    def both(shard):
        return lambda idx: [2 * shard(idx), 2 * shard(idx) + 1]

    shards = [
        both(lambda idx: idx[0]),
        both(lambda idx: idx[0] ^ (1 + idx[1])),
        both(lambda idx: idx[0] ^ (2 - idx[1])),
        lambda idx: [2 * (idx[0] ^ 3) + idx[1]],
        lambda idx: [2 * (idx[0] ^ 3) + 1 - idx[1]],
    ]
    return near, flip(near, "seq", 1), weights, shards, 2 * n


def from_chips(parts):
    return [parts[0]] + [flip(parts[q], "seq", 2 * q) for q in range(1, len(parts))]


def reduced(keep, send_x, send_y):
    _, size, width = keep.shape
    step = shape((size, width))
    own, send_t, send_s = call(
        sum_first_kernel,
        [shape((2, size, width), F32), step, step],
        [keep, flip(send_x, "dp", 1), flip(send_y, "dp", 2)],
        small=True,
    )
    n = lax.axis_size("seq") // 2
    block = (size, 2 * width // n)
    own, *sends = call(
        sum_second_kernel,
        [shape(block, F32)] + [shape(block)] * (n - 1),
        [own, flip(send_t, "dp", 2), flip(send_s, "dp", 1)],
        small=True,
    )
    got = from_chips([own, *sends])[1:]
    return call(sum_kernel, [shape((size, width // n), F32)] * 2, [own, *got[::-1]], small=True)


def shards(tokens, spatial_qkv, wo_spatial, w_temporal, wo_temporal, cotangent):
    frames, patches, width = tokens.shape
    inner = wo_spatial.shape[0]
    heads = inner // DH
    padded = -(-inner // LANES) * LANES
    rows = frames * patches
    peers = FRAMES // frames
    chips = peers // 2
    group = patches // peers
    block = 2 * group
    n_dp, n_seq = lax.axis_size("dp"), lax.axis_size("seq")

    def held(columns, dtype=BF16):
        return pltpu.VMEM((rows, columns), dtype)

    wide = held(padded)
    attended = pltpu.VMEM((heads, rows, rows), F32)
    projection = pltpu.VMEM((inner, width), BF16)
    per_chip = rows // chips
    qkv_rows = spatial_qkv.reshape(rows, 3 * inner)
    sent = -(-(2 * width + inner) // LANES) * LANES
    *near, hidden, spatial_p = call(
        functools.partial(spatial_kernel, chips, patches),
        [shape((per_chip, sent))] * chips
        + [shape((rows, width)), shape((heads, rows, rows), F32)],
        [qkv_rows, tokens.reshape(rows, width), wo_spatial, cotangent.reshape(rows, width)],
        [held(width), held(width), held(3 * inner), projection]
        + [pltpu.VMEM((frames * chips, block, sent), BF16), held(width), attended]
        + [wide] * 3
        + [sems(6)],
        far_in=range(4),
        far_out=(chips, chips + 1),
    )
    near, far, weights, places, count = gather(w_temporal.T, near, chips)
    blocks = pltpu.VMEM((count, rows, 3 * inner // count), BF16)
    mine, *back = call(
        functools.partial(temporal_kernel, places, chips, group),
        [shape((rows, width + inner))] + [shape((per_chip, width + inner))] * (chips - 1),
        [near, far, wo_temporal, *weights],
        [held(width)] + [wide] * 4 + [attended, blocks],
        small=True,
    )
    other = flip(mine, "seq", 1)
    if n_dp == 4 and n_seq == peers:
        size = inner // n_seq
        work = [
            pltpu.VMEM((n_seq, rows, size), BF16),
            pltpu.VMEM((n_dp, rows, width // n_dp), BF16),
        ]
        (part,) = call(
            functools.partial(own_parts_kernel, chips, block, inner, width),
            [shape((2 * n_dp, size, width), F32)],
            [mine, near, far],
            work,
            small=True,
        )
        keep, send_x, send_y = call(
            functools.partial(parts_kernel, chips, block, inner, width),
            [shape((n_dp, size, width), F32)] + [shape((2, size, width))] * 2,
            [other, near, far, part],
            work,
            small=True,
        )
    else:
        (both,) = call(
            functools.partial(whole_parts_kernel, chips, block, inner, width),
            [shape((2, inner, width))],
            [mine, other, near],
            small=True,
        )
    back = from_chips([mine, *back])
    (others,) = call(
        others_kernel,
        [shape((rows // 2, width + inner))],
        [back[0], *back[:0:-1]],
        small=True,
    )
    block_out, tokens_grad, qkv_grad = call(
        functools.partial(last_kernel, chips, patches),
        [shape((rows, width)), shape((rows, width)), shape((rows, 3 * inner))],
        [*back[::-1], flip(others, "seq", 1), wo_spatial, qkv_rows, spatial_p, wo_temporal, hidden],
        [held(width + inner), held(width), held(3 * inner)] + [wide] * 4 + [sems(3)],
        far_out=range(3),
        small=True,
    )
    if n_dp == 4 and n_seq == peers:
        temporal_grad, spatial_grad = reduced(keep, send_x, send_y)
    else:
        both = lax.psum_scatter(both, "seq", scatter_dimension=1, tiled=True)
        both = lax.psum_scatter(both, "dp", scatter_dimension=2, tiled=True).astype(F32)
        temporal_grad, spatial_grad = both[0], both[1]
    return (
        block_out.reshape(frames, patches, width),
        tokens_grad.reshape(frames, patches, width),
        qkv_grad.reshape(frames, patches, 3 * inner),
        spatial_grad,
        temporal_grad,
    )


def solution(mesh):
    placed = (
        P(("dp", "seq"), None, None),
        P(("dp", "seq"), None, None),
        P(),
        P(None, "dp"),
        P(),
        P(("dp", "seq"), None, None),
    )
    return jax.shard_map(
        shards,
        mesh=mesh,
        in_specs=placed,
        out_specs=(
            P(("dp", "seq"), None, None),
            P(("dp", "seq"), None, None),
            P(("dp", "seq"), None, None),
            P("seq", "dp"),
            P("seq", "dp"),
        ),
        check_vma=False,
    )
```

```python
import functools
import math

import jax
import jax.numpy as jnp
from jax import lax
from jax.experimental import pallas as pl
from jax.experimental.pallas import tpu as pltpu
from jax.sharding import PartitionSpec as P

DH = 72
FRAMES = 16
LANES = 128
BF16 = jnp.bfloat16
F32 = jnp.float32
VMEM = pl.BlockSpec(memory_space=pltpu.VMEM)
SMEM = pl.BlockSpec(memory_space=pltpu.SMEM)
HBM = pl.BlockSpec(memory_space=pltpu.HBM)
PAD = 2 * LANES
LIMIT = 16 * 1024 * 1024
MOST = 53 * 1024 * 1024


def dot(left, right):
    return jnp.dot(left, right, preferred_element_type=F32)


def dot_bt(left, right):
    return lax.dot_general(left, right, (((1,), (1,)), ((), ())), preferred_element_type=F32)


def dot_weight(rows, weight):
    return dot_bt(weight, rows).T


def dot_at(left, right):
    return lax.dot_general(left, right, (((0,), (0,)), ((), ())), preferred_element_type=F32)


def call(body, outs, args, scratch=(), us=0, far_in=(), far_out=(), small=False):
    moved = sum(math.prod(a.shape) * a.dtype.itemsize for a in (*args, *outs))
    near = [SMEM if a.dtype == jnp.int32 else VMEM for a in args]
    return pl.pallas_call(
        body,
        out_shape=outs,
        in_specs=[HBM if i in far_in else spec for i, spec in enumerate(near)],
        out_specs=[
            HBM if i in far_out else SMEM if out.dtype == jnp.int32 else VMEM
            for i, out in enumerate(outs)
        ],
        scratch_shapes=list(scratch),
        compiler_params=pltpu.CompilerParams(vmem_limit_bytes=LIMIT if small else MOST),
        cost_estimate=pl.CostEstimate(
            flops=us * 1150000000, bytes_accessed=moved if us else 0, transcendentals=0
        ),
    )(*args)


def started(pairs, sems):
    copies = [pltpu.make_async_copy(a, b, sems.at[i]) for i, (a, b) in enumerate(pairs)]
    for copy in copies:
        copy.start()
    return copies


def shape(dims, dtype=BF16):
    return jax.ShapeDtypeStruct(dims, dtype)


TOKEN = shape((1,), jnp.int32)


def window(head):
    low = head * DH // LANES * LANES
    high = -(-(head + 1) * DH // LANES) * LANES
    return low, high


def head_only(block, head):
    low, high = window(head)
    lane = lax.broadcasted_iota(jnp.int32, (1, high - low), 1) + low
    keep = (lane >= head * DH) & (lane < (head + 1) * DH)
    return jnp.where(keep, block, jnp.zeros_like(block))


def add_tiles(tiles, head, value):
    low, high = window(head)
    for at in range(low // LANES, high // LANES):
        part = value[:, at * LANES - low : (at + 1) * LANES - low]
        tiles[at] = part if tiles[at] is None else tiles[at] + part


def joined(tiles):
    return jnp.concatenate([tile.astype(BF16) for tile in tiles], axis=1)


def same_group(rows, kind):
    row = lax.broadcasted_iota(jnp.int32, (rows, rows), 0)
    col = lax.broadcasted_iota(jnp.int32, (rows, rows), 1)
    how, size = kind
    return row // size == col // size if how == "block" else row % size == col % size


def softmax_forward(q_ref, k_ref, v_ref, p_ref, heads, kind):
    rows = q_ref.shape[0]
    mask = same_group(rows, kind)
    tiles = [None] * (q_ref.shape[1] // LANES)
    for head in range(heads):
        low, high = window(head)
        s = dot_bt(q_ref[:, low:high], head_only(k_ref[:, low:high], head)) * (1.0 / math.sqrt(DH))
        s = jnp.where(mask, s, -jnp.inf)
        e = jnp.exp(s - jnp.max(s, axis=1, keepdims=True))
        p = e / jnp.sum(e, axis=1, keepdims=True)
        p_ref[head] = p
        add_tiles(tiles, head, dot(p.astype(BF16), head_only(v_ref[:, low:high], head)))
    return joined(tiles)


def softmax_backward(q_ref, k_ref, v_ref, g_ref, p_ref, heads):
    count = q_ref.shape[1] // LANES
    dq, dk, dv = [None] * count, [None] * count, [None] * count
    for head in range(heads):
        low, high = window(head)
        p = p_ref[head]
        g = head_only(g_ref[:, low:high], head)
        add_tiles(dv, head, dot_at(p.astype(BF16), g))
        dp = dot_bt(g, v_ref[:, low:high])
        ds = p * (dp - jnp.sum(p * dp, axis=1, keepdims=True)) * (1.0 / math.sqrt(DH))
        ds = ds.astype(BF16)
        add_tiles(dq, head, dot(ds, head_only(k_ref[:, low:high], head)))
        add_tiles(dk, head, dot_at(ds, head_only(q_ref[:, low:high], head)))
    return joined(dq), joined(dk), joined(dv)


def put(ref, value):
    width = value.shape[1]
    ref[:, width // LANES * LANES :] = jnp.zeros(
        (ref.shape[0], ref.shape[1] - width // LANES * LANES), ref.dtype
    )
    ref[:, :width] = value


def place(chips):
    seq = lax.axis_index("seq")
    return lax.axis_index("dp"), seq % 2, seq % (2 * chips) // 2, seq


def spatial_kernel(chips, patches, *refs):
    idx = place(chips)
    far, outs, refs = refs[:4], refs[4 : 4 + chips], refs[4 + chips :]
    hid_far, p_far, tok, cot, qkv, wos, held, hid, p_ref, qs, ks, vs, sems = refs
    inner, width = wos.shape
    count, block, _ = held.shape
    loads = started(zip(far, (qkv, tok, wos, cot)), sems)
    loads[0].wait()
    x = qkv[...]
    put(qs, x[:, :inner])
    put(ks, x[:, inner : 2 * inner])
    put(vs, x[:, 2 * inner :])
    o = softmax_forward(qs, ks, vs, p_ref, inner // DH, ("block", patches))[:, :inner]
    stores = started([(p_ref, p_far)], sems.at[pl.ds(4, 1)])
    for at in range(3):
        loads[1 + at].wait()
    hid[...] = (tok[...].astype(F32) + dot(o, wos[...])).astype(BF16)
    for at in range(count):
        rows = slice(at * block, (at + 1) * block)
        held[at, :, :width] = hid[rows]
        held[at, :, width : 2 * width] = cot[rows]
        held[at, :, 2 * width : 2 * width + inner] = o[rows]
    stores += started([(hid, hid_far)], sems.at[pl.ds(5, 1)])
    for q in range(chips):
        for f in range(count // chips):
            rows = slice(f * block, (f + 1) * block)
            outs[q][rows] = held[f * chips + (idx[2] ^ q)]
    for copy in stores:
        copy.wait()


def own_patches(ref, core, block):
    rows, width = ref.shape
    value = ref[...].astype(F32).reshape(rows // block, block, width)
    value = jnp.where(core == 0, value[:, : block // 2], value[:, block // 2 :])
    return value.reshape(rows // 2, width)


def all_patches(mine, other, core, block):
    rows, width = mine.shape
    mine = mine.astype(F32).reshape(2 * rows // block, block // 2, width)
    other = other.astype(F32).reshape(2 * rows // block, block // 2, width)
    first, second = jnp.where(core == 0, mine, other), jnp.where(core == 0, other, mine)
    return jnp.concatenate([first, second], axis=1).reshape(2 * rows, width).astype(BF16)


def half_kernel(chips, got, own, half, kept):
    rows = half.shape[0]
    core = place(chips)[1]
    half[...] = jnp.where(core == 0, got[:rows].astype(F32), got[rows:].astype(F32)).astype(BF16)
    kept[...] = own[...]


def join_rows_kernel(*refs):
    out, low = refs[-1], 0
    for ref in refs[:-1]:
        out[low : low + ref.shape[0], : ref.shape[1]] = ref[...]
        low += ref.shape[0]


def temporal_kernel(shards, chips, group, near, far, wot, *refs):
    idx = place(chips)
    weights, refs = refs[: len(shards)], refs[len(shards) :]
    (mine, *outs), (cot, q, k, v, g, p_ref, blocks) = refs[:chips], refs[chips:]
    inner, width = wot.shape
    heads = inner // DH
    value = [own_patches(ref, idx[1], 2 * group) for ref in (near, far)]
    value = jnp.concatenate(value, axis=0).astype(BF16)
    hidden = value[:, :width]
    cot[...] = value[:, width : 2 * width]
    size = blocks.shape[2]
    for at, w in zip(shards, weights):
        value = dot_weight(hidden, w[...]).astype(BF16)
        for i, block in enumerate(at(idx)):
            blocks[block] = value[:, i * size : (i + 1) * size]
    whole = jnp.concatenate([blocks[i] for i in range(blocks.shape[0])], axis=1)
    put(q, whole[:, :inner])
    put(k, whole[:, inner : 2 * inner])
    put(v, whole[:, 2 * inner :])
    mine[:, width:] = softmax_forward(q, k, v, p_ref, heads, ("cycle", group))[:, :inner]
    put(g, dot_weight(cot[...], wot[...]).astype(BF16))
    dq, dk, dv = softmax_backward(q, k, v, g, p_ref, heads)
    whole = jnp.concatenate([dq[:, :inner], dk[:, :inner], dv[:, :inner]], axis=1)
    for i in range(blocks.shape[0]):
        blocks[i] = whole[:, i * size : (i + 1) * size]
    grad = jnp.zeros(cot.shape, F32)
    for at, w in zip(shards, weights):
        lhs = jnp.concatenate([blocks[block] for block in at(idx)], axis=1)
        grad += dot(lhs, w[...])
    mine[:, :width] = (cot[...].astype(F32) + grad.astype(BF16).astype(F32)).astype(BF16)
    half = mine.shape[0] // 2
    rows = half // chips
    for q, out in enumerate(outs, 1):
        out[:rows] = mine[q * rows : (q + 1) * rows]
        out[rows:] = mine[half + q * rows : half + (q + 1) * rows]


def others_kernel(mine, *refs):
    parts, out = refs[-2::-1], refs[-1]
    half = mine.shape[0] // 2
    rows = half // (1 + len(parts))
    out[:rows] = mine[half : half + rows]
    for q, part in enumerate(parts, 1):
        out[q * rows : (q + 1) * rows] = part[rows:]


def whole_parts_kernel(chips, block, inner, width, mine, other, *refs):
    idx = place(chips)
    held, part = refs
    cot, so = held[:, width : 2 * width], held[:, 2 * width : 2 * width + inner]
    half = mine.shape[0] // 2
    near = all_patches(mine[:half], other[half:], idx[1], block)
    part[0] = dot_at(near[:, width:], cot).astype(BF16)
    part[1] = dot_at(so, near[:, :width]).astype(BF16)


def products(idx, core, chips, block, inner, width, rows, first, second, heads, cols):
    held = [own_patches(ref, core, block)[:, width:] for ref in (first, second)]
    held = jnp.concatenate(held, axis=0).astype(BF16)
    size = heads.shape[2]
    count, _, wide = cols.shape
    for i in range(2):
        left = rows[:, width:] if i == 0 else held[:, width : width + inner]
        right = held[:, :width] if i == 0 else rows[:, :width]
        for h in range(heads.shape[0]):
            heads[h] = left[:, h * size : (h + 1) * size]
        for r in range(count):
            cols[r] = right[:, r * wide : (r + 1) * wide]
        left = jnp.concatenate([heads[idx[3] ^ (2 * q)] for q in range(chips)], axis=1)
        for r in range(count):
            full = dot_at(left, cols[idx[0] ^ r])
            value = [full[q * size : (q + 1) * size] for q in range(chips)]
            yield i, r, jnp.concatenate(value, axis=1)


def own_parts_kernel(chips, block, inner, width, mine, near, far, part, heads, cols):
    idx = place(chips)
    sizes = (chips, block, inner, width)
    for i, r, value in products(idx, idx[1], *sizes, mine, near, far, heads, cols):
        part[4 * i + r] = value


def parts_kernel(chips, block, inner, width, other, near, far, part, *refs):
    keep, send_x, send_y, heads, cols = refs
    idx = place(chips)
    sizes = (chips, block, inner, width)
    for i, r, value in products(idx, 1 - idx[1], *sizes, other, far, near, heads, cols):
        value += part[4 * i + r]
        if r & (1 if i == 0 else 2):
            (send_x, send_y)[i][r // 2 if i == 0 else r - 2] = value.astype(BF16)
        else:
            keep[2 * i + (r > 0)] = value


def sum_first_kernel(keep, got_x, got_y, own, send_y, send_x):
    for i, (got, send) in enumerate(((got_x, send_y), (got_y, send_x))):
        own[i] = keep[2 * i] + got[0].astype(F32)
        send[...] = (keep[2 * i + 1] + got[1].astype(F32)).astype(BF16)


def sum_second_kernel(own, got_y, got_x, kept, *outs):
    totals = [own[0] + got_y[...].astype(F32), own[1] + got_x[...].astype(F32)]
    size = totals[0].shape[1] // (1 + len(outs))
    rows = kept.shape[0]
    for q, out in enumerate((kept, *outs)):
        cut = jnp.concatenate([total[:, q * size : (q + 1) * size] for total in totals], axis=0)
        cut = [cut[i * rows : (i + 1) * rows] for i in range(3)]
        out[...] = jnp.concatenate(cut, axis=1).astype(out.dtype)


def sum_kernel(own, *refs):
    got, outs = refs[:-2], refs[-2:]
    total = own[...]
    for part in got:
        total += part[...].astype(F32)
    rows, size = outs[0].shape
    total = jnp.concatenate([total[:, i * size : (i + 1) * size] for i in range(3)], axis=0)
    for i, out in enumerate(outs):
        out[...] = total[i * rows : (i + 1) * rows]


def last_kernel(chips, patches, *refs):
    idx = place(chips)
    held, got, refs = refs[:chips][::-1], refs[chips], refs[chips + 1 :]
    (wos, qkv, p_ref, wot, hid), refs = refs[:5], refs[5:]
    block_far, out_far, grads_far, rows, block_out, grads, qs, ks, vs, gs, sems = refs
    inner, width = wos.shape
    frames = rows.shape[0] // patches
    block = patches // chips
    each = frames * block // 2
    for q in range(chips):
        value = all_patches(held[q][:each], got[q * each : (q + 1) * each], idx[1], block)
        for f in range(frames):
            low = pl.multiple_of(f * patches + (idx[2] ^ q) * block, block)
            rows[pl.ds(low, block)] = value[f * block : (f + 1) * block]
    value = rows[...]
    grad, attended = value[:, :width], value[:, width:]
    stores = started([(rows.at[:, pl.ds(0, width)], out_far)], sems.at[pl.ds(0, 1)])
    block_out[...] = (hid[...].astype(F32) + dot(attended, wot[...])).astype(BF16)
    stores += started([(block_out, block_far)], sems.at[pl.ds(1, 1)])
    put(gs, dot_bt(grad, wos[...]).astype(BF16))
    x = qkv[...]
    put(qs, x[:, :inner])
    put(ks, x[:, inner : 2 * inner])
    put(vs, x[:, 2 * inner :])
    dq, dk, dv = softmax_backward(qs, ks, vs, gs, p_ref, inner // DH)
    grads[...] = jnp.concatenate([dq[:, :inner], dk[:, :inner], dv[:, :inner]], axis=1)
    stores += started([(grads, grads_far)], sems.at[pl.ds(2, 1)])
    for copy in stores:
        copy.wait()


def flip(value, axis, bit):
    return lax.ppermute(value, axis, [(i, i ^ bit) for i in range(lax.axis_size(axis))])


def sems(n):
    return pltpu.SemaphoreType.DMA((n,))


def across(value, bits):
    n = lax.axis_size("seq")
    pairs = [
        (d * n + i, (d ^ bits[i % 2]) * n + i) for d in range(lax.axis_size("dp")) for i in range(n)
    ]
    return lax.ppermute(value, ("dp", "seq"), pairs)


def gather(weight, parts, chips):
    n = lax.axis_size("dp")
    rows, sent = parts[0].shape
    whole = [shape((len(parts) * rows, sent + PAD))]
    if n != 4:
        (near,) = call(join_rows_kernel, whole, from_chips(parts), small=True)
        weights = [lax.all_gather(weight, "dp", axis=0, tiled=True)]
        return near, flip(near, "seq", 1), weights, [lambda idx: [0]], 1
    half, width = weight.shape[0] // 2, weight.shape[1]
    side = across(weight, (1, 2))
    corner, own = call(
        functools.partial(half_kernel, chips),
        [shape((half, width)), shape((rows, sent))],
        [side, parts[0]],
        small=True,
    )
    corner = across(corner, (2, 1))
    (near,) = call(join_rows_kernel, whole, [own, *from_chips(parts)[1:]], small=True)
    weights = [weight, side, flip(side, "seq", 1), corner, flip(corner, "seq", 1)]

    def both(shard):
        return lambda idx: [2 * shard(idx), 2 * shard(idx) + 1]

    shards = [
        both(lambda idx: idx[0]),
        both(lambda idx: idx[0] ^ (1 + idx[1])),
        both(lambda idx: idx[0] ^ (2 - idx[1])),
        lambda idx: [2 * (idx[0] ^ 3) + idx[1]],
        lambda idx: [2 * (idx[0] ^ 3) + 1 - idx[1]],
    ]
    return near, flip(near, "seq", 1), weights, shards, 2 * n


def from_chips(parts):
    return [parts[0]] + [flip(parts[q], "seq", 2 * q) for q in range(1, len(parts))]


def reduced(keep, send_x, send_y):
    _, size, width = keep.shape
    step = shape((size, width))
    own, send_t, send_s = call(
        sum_first_kernel,
        [shape((2, size, width), F32), step, step],
        [keep, flip(send_x, "dp", 1), flip(send_y, "dp", 2)],
        small=True,
    )
    n = lax.axis_size("seq") // 2
    block = (2 * size // 3, 3 * width // n)
    own, *sends = call(
        sum_second_kernel,
        [shape(block, F32)] + [shape(block)] * (n - 1),
        [own, flip(send_t, "dp", 2), flip(send_s, "dp", 1)],
        small=True,
    )
    got = from_chips([own, *sends])[1:]
    return call(sum_kernel, [shape((size, width // n), F32)] * 2, [own, *got[::-1]], small=True)


def shards(tokens, spatial_qkv, wo_spatial, w_temporal, wo_temporal, cotangent):
    frames, patches, width = tokens.shape
    inner = wo_spatial.shape[0]
    heads = inner // DH
    padded = -(-inner // LANES) * LANES
    rows = frames * patches
    peers = FRAMES // frames
    chips = peers // 2
    group = patches // peers
    block = 2 * group
    n_dp, n_seq = lax.axis_size("dp"), lax.axis_size("seq")

    def held(columns, dtype=BF16):
        return pltpu.VMEM((rows, columns), dtype)

    wide = held(padded)
    attended = pltpu.VMEM((heads, rows, rows), F32)
    projection = pltpu.VMEM((inner, width), BF16)
    per_chip = rows // chips
    qkv_rows = spatial_qkv.reshape(rows, 3 * inner)
    sent = -(-(2 * width + inner) // LANES) * LANES
    *near, hidden, spatial_p = call(
        functools.partial(spatial_kernel, chips, patches),
        [shape((per_chip, sent))] * chips
        + [shape((rows, width)), shape((heads, rows, rows), F32)],
        [qkv_rows, tokens.reshape(rows, width), wo_spatial, cotangent.reshape(rows, width)],
        [held(width), held(width), held(3 * inner), projection]
        + [pltpu.VMEM((frames * chips, block, sent), BF16), held(width), attended]
        + [wide] * 3
        + [sems(6)],
        far_in=range(4),
        far_out=(chips, chips + 1),
    )
    near, far, weights, places, count = gather(w_temporal.T, near, chips)
    blocks = pltpu.VMEM((count, rows, 3 * inner // count), BF16)
    mine, *back = call(
        functools.partial(temporal_kernel, places, chips, group),
        [shape((rows, width + inner))] + [shape((per_chip, width + inner))] * (chips - 1),
        [near, far, wo_temporal, *weights],
        [held(width)] + [wide] * 4 + [attended, blocks],
        small=True,
    )
    other = flip(mine, "seq", 1)
    if n_dp == 4 and n_seq == peers:
        size = inner // n_seq
        work = [
            pltpu.VMEM((n_seq, rows, size), BF16),
            pltpu.VMEM((n_dp, rows, width // n_dp), BF16),
        ]
        (part,) = call(
            functools.partial(own_parts_kernel, chips, block, inner, width),
            [shape((2 * n_dp, size, width), F32)],
            [mine, near, far],
            work,
            small=True,
        )
        keep, send_x, send_y = call(
            functools.partial(parts_kernel, chips, block, inner, width),
            [shape((n_dp, size, width), F32)] + [shape((2, size, width))] * 2,
            [other, near, far, part],
            work,
            small=True,
        )
    else:
        (both,) = call(
            functools.partial(whole_parts_kernel, chips, block, inner, width),
            [shape((2, inner, width))],
            [mine, other, near],
            small=True,
        )
    back = from_chips([mine, *back])
    (others,) = call(
        others_kernel,
        [shape((rows // 2, width + inner))],
        [back[0], *back[:0:-1]],
        small=True,
    )
    block_out, tokens_grad, qkv_grad = call(
        functools.partial(last_kernel, chips, patches),
        [shape((rows, width)), shape((rows, width)), shape((rows, 3 * inner))],
        [*back[::-1], flip(others, "seq", 1), wo_spatial, qkv_rows, spatial_p, wo_temporal, hidden],
        [held(width + inner), held(width), held(3 * inner)] + [wide] * 4 + [sems(3)],
        far_out=range(3),
        small=True,
    )
    if n_dp == 4 and n_seq == peers:
        temporal_grad, spatial_grad = reduced(keep, send_x, send_y)
    else:
        both = lax.psum_scatter(both, "seq", scatter_dimension=1, tiled=True)
        both = lax.psum_scatter(both, "dp", scatter_dimension=2, tiled=True).astype(F32)
        temporal_grad, spatial_grad = both[0], both[1]
    return (
        block_out.reshape(frames, patches, width),
        tokens_grad.reshape(frames, patches, width),
        qkv_grad.reshape(frames, patches, 3 * inner),
        spatial_grad,
        temporal_grad,
    )


def solution(mesh):
    placed = (
        P(("dp", "seq"), None, None),
        P(("dp", "seq"), None, None),
        P(),
        P(None, "dp"),
        P(),
        P(("dp", "seq"), None, None),
    )
    return jax.shard_map(
        shards,
        mesh=mesh,
        in_specs=placed,
        out_specs=(
            P(("dp", "seq"), None, None),
            P(("dp", "seq"), None, None),
            P(("dp", "seq"), None, None),
            P("seq", "dp"),
            P("seq", "dp"),
        ),
        check_vma=False,
    )
```
